32 devices in a mesh: pts: 16 (over z, x, core), rep: 2 (over y).
Axes of the slice: x: 2, y: 2, z: 4, core: 2. Of those that a mesh axis runs over, the one named last changes fastest.
Arguments:
- points: bfloat16 [65536, 512], P(('rep', 'pts')), parts along dimension 0, may hold values from -6 to 6
- point_row_index: int32 [65536], P(('rep', 'pts')), parts along dimension 0, may hold values from 0 to 32767, as said below
- neighbour_ball_list: int32 [256, 4], P(('rep', 'pts')), parts along dimension 0, may hold values from 0 to 127, as said below
- attention_norm_gain: float32 [512], replicated, may hold values from 0.1 to 1.9
- query_weight: bfloat16 [512, 512], replicated, may hold values from -0.25 to 0.25
- key_weight: bfloat16 [512, 512], replicated, may hold values from -0.25 to 0.25
- value_weight: bfloat16 [512, 512], replicated, may hold values from -0.25 to 0.25
- pooled_key_weight: bfloat16 [512, 512], replicated, may hold values from -0.75 to 0.75
- pooled_value_weight: bfloat16 [512, 512], replicated, may hold values from -0.75 to 0.75
- head_score_scale: float32 [16], replicated, may hold values from 4 to 16
- output_weight: bfloat16 [512, 512], replicated, may hold values from -0.25 to 0.25
- feedforward_norm_gain: float32 [512], replicated, may hold values from 0.1 to 1.9
- gate_weight: bfloat16 [512, 1024], replicated, may hold values from -0.25 to 0.25
- up_weight: bfloat16 [512, 1024], replicated, may hold values from -0.25 to 0.25
- down_weight: bfloat16 [1024, 512], replicated, may hold values from -0.1875 to 0.1875
Outputs:
- layer_out: bfloat16 [65536, 512], P(('rep', 'pts')), parts along dimension 0
The draws below stay inside these ranges and needn't reach their ends.
There are 2 independent parts, one for each index of `rep`. The reference program is written for one: setup_inputs(seed, part) draws one part's arguments, and reference() takes and returns one part's arrays. A program takes and returns all parts, laid end to end along the dimension named above; an argument that names none is the same for every part. Nothing has to cross between parts.
Inputs may be any that keep to these rules, and one draw needn't show every extreme that they name: point_row_index holds every number of 0 to 32767 once; of the 2048 points of one device (rows d * 2048 to (d + 1) * 2048 - 1 of points) exactly 128 go to the rows of each device. `neighbour_ball_list`: row b starts with b itself; its other three entries are balls on three different devices among those 1 to 4 places away from ball b's device around the loop of devices, ball c lying on device c // 8.
All inputs are finite; a program needn't handle non-finite values.
Results may differ from the reference program's by a relative error of at most 0.012.
Values may be sent and summed in bfloat16 or wider, within the bound.
No kernel may reach another device: no remote copies, remote signals or barrier semaphores. Data moves between devices by JAX's collectives and lax.ppermute only.
A program may use at most 128 MiB of HBM per device.

```python
import math
import jax
import jax.numpy as jnp
from jax import lax

D = 512
HEAD_TOTAL = 16
HD = 32
FF = 1024
BALL = 256
POOL = 8
OWNERS = 4
REACH = 4
P_DEV = 2048
POINTS = 32768
NBALLS = 128
CK = 32
SEND = 128


def draw_point_row_index(key, part):
    devices = POINTS // P_DEV
    base_key = jax.random.fold_in(key, 11)
    shuffle_key = jax.random.fold_in(key, 13)

    def dest_inverse(dest_index):
        shuffled = jax.random.permutation(jax.random.fold_in(base_key, dest_index), P_DEV)
        return jnp.argsort(shuffled).astype(jnp.int32)
    inverse = jax.vmap(dest_inverse)(jnp.arange(devices, dtype=jnp.int32))
    table = inverse.reshape(devices, devices, SEND) + (jnp.arange(devices, dtype=jnp.int32) * P_DEV)[:, None, None]
    table = jnp.transpose(table, (1, 0, 2)).reshape(devices, P_DEV)

    def source_order(source_index):
        return jax.random.permutation(jax.random.fold_in(shuffle_key, source_index), P_DEV).astype(jnp.int32)
    orders = jax.vmap(source_order)(jnp.arange(devices, dtype=jnp.int32))
    placed = jnp.take_along_axis(table, orders, axis=1)
    return placed.reshape(POINTS).astype(jnp.int32)


def draw_neighbour_ball_list(key, part):
    devices = POINTS // P_DEV
    per_device = P_DEV // BALL
    base_key = jax.random.fold_in(key, 23)
    steps_up = jnp.arange(1, REACH + 1, dtype=jnp.int32)
    choices_table = jnp.concatenate([-steps_up, steps_up]).astype(jnp.int32)

    def one_ball(ball_index):
        ball_key = jax.random.fold_in(base_key, ball_index)
        shifted = jax.random.permutation(jax.random.fold_in(ball_key, 1), choices_table)[:3]
        blocks = jax.random.randint(jax.random.fold_in(ball_key, 2), (3,), 0, per_device, dtype=jnp.int32)
        home = ball_index // per_device
        others = jnp.mod(home + shifted, devices) * per_device + blocks
        return jnp.concatenate([ball_index[None], others]).astype(jnp.int32)
    return jax.vmap(one_ball)(jnp.arange(NBALLS, dtype=jnp.int32))


def block_levels(key, dims, cuts, least, largest):
    loudness = 1.0
    for axis_at, shards_of in cuts:
        heights = jax.random.uniform(jax.random.fold_in(jax.random.fold_in(key, 6), axis_at), (shards_of,), jnp.float32, least / len(cuts), largest / len(cuts))
        loudness = loudness * jnp.repeat(jnp.exp(heights), dims[axis_at] // shards_of).reshape((-1,) + (1,) * (len(dims) - 1 - axis_at))
    return loudness


def scatter_about(stream_key, dims, scale, bound, cuts=(), held_as=jnp.bfloat16):
    result = jax.random.normal(stream_key, dims, jnp.float32) * scale
    if len(cuts) > 0:
        result = block_levels(stream_key, dims, cuts, -0.22, 0.18) * result
    return jnp.clip(result, min=-bound, max=bound).astype(held_as)


def setup_inputs(seed: int = 0, part: int = 0) -> dict:
    streams_of = jax.random.split(jax.random.key(seed), 16)
    own_keys = jax.random.split(jax.random.fold_in(streams_of[15], part), 16)
    return {
        "points": scatter_about(own_keys[0], (POINTS, D), 1.0, 6.0, ((0, 16),)),
        "point_row_index": draw_point_row_index(jax.random.fold_in(jax.random.fold_in(streams_of[15], part), 71), part),
        "neighbour_ball_list": draw_neighbour_ball_list(jax.random.fold_in(jax.random.fold_in(streams_of[15], part), 71), part),
        "attention_norm_gain": jnp.clip(1.0 + 0.18 * jax.random.normal(streams_of[3], (D,), jnp.float32), 0.1, 1.9),
        "query_weight": scatter_about(streams_of[4], (D, D), D ** -0.5, 0.25),
        "key_weight": scatter_about(streams_of[5], (D, D), D ** -0.5, 0.25),
        "value_weight": scatter_about(streams_of[6], (D, D), D ** -0.5, 0.25),
        "pooled_key_weight": scatter_about(streams_of[7], (D, D), (D // POOL) ** -0.5, 0.75),
        "pooled_value_weight": scatter_about(streams_of[8], (D, D), (D // POOL) ** -0.5, 0.75),
        "head_score_scale": jnp.clip(jnp.exp(jax.random.uniform(streams_of[9], (HEAD_TOTAL,), jnp.float32, math.log(4.0), math.log(16.0))), 4.0, 16.0),
        "output_weight": scatter_about(streams_of[10], (D, D), D ** -0.5, 0.25),
        "feedforward_norm_gain": jnp.clip(1.0 + 0.18 * jax.random.normal(streams_of[11], (D,), jnp.float32), 0.1, 1.9),
        "gate_weight": scatter_about(streams_of[12], (D, FF), D ** -0.5, 0.25),
        "up_weight": scatter_about(streams_of[13], (D, FF), D ** -0.5, 0.25),
        "down_weight": scatter_about(streams_of[14], (FF, D), FF ** -0.5, 0.1875),
    }


def row_norm(values, scale_gain):
    mean_square = lax.optimization_barrier(jnp.mean(values * values, axis=-1, keepdims=True))
    return values * lax.rsqrt(mean_square + 1e-05) * scale_gain

def head_norm(values, head_total):
    shaped = values.reshape(values.shape[0], head_total, -1)
    mean_square = lax.optimization_barrier(jnp.mean(shaped * shaped, axis=-1, keepdims=True))
    return shaped * lax.rsqrt(mean_square + 1e-06)

def ball_attention_layer(query_rows, local_key_rows, local_value_rows, coarse_key_rows, coarse_value_rows, head_score_scale):
    keys_all = jnp.concatenate([local_key_rows, coarse_key_rows], axis=0).astype(jnp.float32)
    values_all = jnp.concatenate([local_value_rows, coarse_value_rows], axis=0).astype(jnp.float32)
    score_matrix = jnp.einsum('qhd,khd->hqk', query_rows.astype(jnp.float32), keys_all)
    score_matrix = score_matrix * (head_score_scale / query_rows.shape[-1])[:, None, None]
    exponent = jnp.exp(score_matrix)
    denominator = lax.optimization_barrier(jnp.sum(exponent, axis=-1, keepdims=True))
    probabilities = (exponent / denominator).astype(jnp.bfloat16)
    attended_rows = jnp.einsum('hqk,khd->qhd', probabilities.astype(jnp.float32), values_all)
    return attended_rows.reshape(query_rows.shape[0], -1).astype(jnp.bfloat16)

def reference(points, point_row_index, neighbour_ball_list, attention_norm_gain, query_weight, key_weight, value_weight, pooled_key_weight, pooled_value_weight, head_score_scale, output_weight, feedforward_norm_gain, gate_weight, up_weight, down_weight):
    head_total = head_score_scale.shape[0]
    grouped = jnp.zeros_like(points).at[point_row_index].set(points)
    normed = row_norm(grouped.astype(jnp.float32), attention_norm_gain).astype(jnp.bfloat16)
    query_rows = head_norm(jnp.dot(normed, query_weight, preferred_element_type=jnp.float32), head_total).astype(jnp.bfloat16)
    local_key_rows = head_norm(jnp.dot(normed, key_weight, preferred_element_type=jnp.float32), head_total).astype(jnp.bfloat16)
    local_value_rows = jnp.dot(normed, value_weight, preferred_element_type=jnp.float32).astype(jnp.bfloat16).reshape(POINTS, head_total, HD)
    pooled = lax.optimization_barrier(jnp.mean(normed.astype(jnp.float32).reshape(POINTS // POOL, POOL, D), axis=1)).astype(jnp.bfloat16)
    comp_key = head_norm(jnp.dot(pooled, pooled_key_weight, preferred_element_type=jnp.float32), head_total).astype(jnp.bfloat16)
    comp_key = comp_key.reshape(NBALLS, CK, head_total, HD)
    comp_value = jnp.dot(pooled, pooled_value_weight, preferred_element_type=jnp.float32).astype(jnp.bfloat16)
    comp_value = comp_value.reshape(NBALLS, CK, head_total, HD)

    def one_ball(ball_index):
        start = (ball_index * BALL).astype(jnp.int32)
        ball_query_rows = lax.dynamic_slice_in_dim(query_rows, start, BALL, 0)
        ball_key_rows = lax.dynamic_slice_in_dim(local_key_rows, start, BALL, 0)
        ball_value_rows = lax.dynamic_slice_in_dim(local_value_rows, start, BALL, 0)
        chosen = neighbour_ball_list[ball_index].astype(jnp.int32)
        coarse_key_rows = jnp.take(comp_key, chosen, axis=0).reshape(OWNERS * CK, head_total, HD)
        coarse_value_rows = jnp.take(comp_value, chosen, axis=0).reshape(OWNERS * CK, head_total, HD)
        return ball_attention_layer(ball_query_rows, ball_key_rows, ball_value_rows, coarse_key_rows, coarse_value_rows, head_score_scale)
    attended_rows = lax.map(one_ball, jnp.arange(NBALLS, dtype=jnp.int32)).reshape(POINTS, D)
    residual = (grouped.astype(jnp.float32) + jnp.dot(attended_rows, output_weight, preferred_element_type=jnp.float32)).astype(jnp.bfloat16)
    ffn_normed = row_norm(residual.astype(jnp.float32), feedforward_norm_gain).astype(jnp.bfloat16)
    gate_proj = jnp.dot(ffn_normed, gate_weight, preferred_element_type=jnp.float32)
    up_proj = jnp.dot(ffn_normed, up_weight, preferred_element_type=jnp.float32)
    hidden = (jax.nn.silu(gate_proj) * up_proj).astype(jnp.bfloat16)
    ball_out = (residual.astype(jnp.float32) + jnp.dot(hidden, down_weight, preferred_element_type=jnp.float32)).astype(jnp.bfloat16)
    return jnp.take(ball_out, point_row_index.astype(jnp.int32), axis=0)
```

```python
import functools
import math

import jax
import jax.numpy as jnp
from jax import lax
from jax.experimental import pallas as pl
from jax.experimental.pallas import tpu as pltpu
from jax.sharding import PartitionSpec as P

BALL = 256
POOL = 8
OWNERS = 4
REACH = 4
LANES = 128
TILE = 256
LOW = 64
LOG2E = math.log2(math.e)
F32 = jnp.float32
BF16 = jnp.bfloat16
VMEM_BYTES = 56 * 1024 * 1024


def params(**kwargs):
    return pltpu.CompilerParams(vmem_limit_bytes=VMEM_BYTES, **kwargs)


def dot(a, b):
    return jnp.dot(a, b, preferred_element_type=F32)


def dot_nt(a, b):
    return lax.dot_general(a, b, (((1,), (1,)), ((), ())), preferred_element_type=F32)


def whole(shape):
    return pl.BlockSpec(shape, lambda *_: (0,) * len(shape))


def column_of(row):
    return jnp.broadcast_to(row, (LANES, LANES)).T


def one_hot_by_lane_ids(ids_ref, first, rows):
    targets = (lax.broadcasted_iota(jnp.int32, (rows, LANES), 0) + first).astype(F32)
    tiles = [
        jnp.where(ids_ref[t : t + 1, :] == targets, 1.0, 0.0).astype(BF16)
        for t in range(ids_ref.shape[0])
    ]
    return jnp.concatenate(tiles, axis=1)


def send_kernel(rows_dev, index_ref, points_ref, out_ref, ids_ref, rank_ref, col, aux):
    tiles = rows_dev // LANES
    step = pl.program_id(0)

    @pl.when(step == 0)
    def _():
        for t in range(tiles):
            col[t * LANES : (t + 1) * LANES, :] = column_of(index_ref[t : t + 1, :].astype(F32))

        def rank_tile(t, carry):
            row = index_ref[pl.ds(t, 1), :].astype(F32)
            below = jnp.where(col[...] < row, 1.0, 0.0)
            rank_ref[pl.ds(t, 1), :] = jnp.sum(below, axis=0, keepdims=True)
            return carry

        lax.fori_loop(0, tiles, rank_tile, 0)
        local = lax.rem(col[...].astype(jnp.int32), rows_dev)
        lane = lax.broadcasted_iota(jnp.int32, (rows_dev, LANES), 1)
        high = lax.div(local, LOW)
        low = lax.rem(local, LOW)
        aux[...] = jnp.where(lane == 0, high, jnp.where(lane == 1, low, 0)).astype(F32).astype(BF16)

    pick = one_hot_by_lane_ids(rank_ref, step * TILE, TILE)
    out_ref[...] = dot(pick, points_ref[...]).astype(BF16)
    ids = dot(pick, aux[...])
    for u in range(TILE // LANES):
        part = ids[u * LANES : (u + 1) * LANES, :].T
        ids_ref[pl.ds(step * (TILE // LANES) + u, 1), :] = (
            part[0:1, :] * LOW + part[1:2, :]
        ).astype(jnp.int32)


def send_order(points, index_tiles):
    rows_dev, width = points.shape
    tiles = rows_dev // LANES
    return pl.pallas_call(
        functools.partial(send_kernel, rows_dev),
        grid=(rows_dev // TILE,),
        in_specs=[whole((tiles, LANES)), whole((rows_dev, width))],
        out_specs=[
            pl.BlockSpec((TILE, width), lambda i: (i, 0)),
            whole((tiles, LANES)),
            whole((tiles, LANES)),
        ],
        out_shape=[
            jax.ShapeDtypeStruct((rows_dev, width), BF16),
            jax.ShapeDtypeStruct((tiles, LANES), jnp.int32),
            jax.ShapeDtypeStruct((tiles, LANES), F32),
        ],
        scratch_shapes=[
            pltpu.VMEM((rows_dev, LANES), F32),
            pltpu.VMEM((rows_dev, LANES), BF16),
        ],
        compiler_params=params(),
        cost_estimate=pl.CostEstimate(
            flops=2 * rows_dev * rows_dev * (width + LANES), bytes_accessed=4 * rows_dev * width, transcendentals=0
        ),
        name="send_order",
    )(index_tiles, points)


def group_kernel(ids_ref, arrived_ref, gain_ref, grouped_ref, normed_ref, pooled_ref):
    pick = one_hot_by_lane_ids(ids_ref, pl.program_id(0) * BALL, BALL)
    grouped = dot(pick, arrived_ref[...])
    grouped_ref[...] = grouped.astype(BF16)
    mean_square = jnp.mean(grouped * grouped, axis=-1, keepdims=True)
    normed = (grouped * lax.rsqrt(mean_square + 1e-05) * gain_ref[...]).astype(BF16)
    normed_ref[...] = normed
    comp = BALL // POOL
    member = lax.broadcasted_iota(jnp.int32, (comp, BALL), 1) // POOL
    pool_of = lax.broadcasted_iota(jnp.int32, (comp, BALL), 0)
    mean_of = jnp.where(member == pool_of, 1.0 / POOL, 0.0).astype(BF16)
    pooled_ref[...] = dot(mean_of, normed).astype(BF16)


def group(ids, arrived, gain):
    rows_dev, width = arrived.shape
    tiles = rows_dev // LANES
    comp = BALL // POOL
    return pl.pallas_call(
        group_kernel,
        grid=(rows_dev // BALL,),
        in_specs=[whole((tiles, LANES)), whole((rows_dev, width)), whole((1, width))],
        out_specs=[
            pl.BlockSpec((BALL, width), lambda i: (i, 0)),
            pl.BlockSpec((BALL, width), lambda i: (i, 0)),
            pl.BlockSpec((comp, width), lambda i: (i, 0)),
        ],
        out_shape=[
            jax.ShapeDtypeStruct((rows_dev, width), BF16),
            jax.ShapeDtypeStruct((rows_dev, width), BF16),
            jax.ShapeDtypeStruct((rows_dev // POOL, width), BF16),
        ],
        compiler_params=params(),
        cost_estimate=pl.CostEstimate(
            flops=2 * rows_dev * rows_dev * width, bytes_accessed=6 * rows_dev * width, transcendentals=0
        ),
        name="group_balls",
    )(ids, arrived, gain)


def head_normed(columns, head_size, factors=None):
    heads = columns.shape[0] // head_size
    parts = []
    for h in range(heads):
        part = columns[h * head_size : (h + 1) * head_size, :]
        root = lax.rsqrt(jnp.mean(part * part, axis=0, keepdims=True) + 1e-06)
        if factors is not None:
            root = root * factors[h]
        parts.append((part * root).astype(BF16))
    return parts


def head_sums(query, key_rows, value, h, head_size):
    per_group = LANES // head_size
    group_at, at = h // per_group, h % per_group
    empty = jnp.zeros_like(query)
    spread = jnp.concatenate([query if j == at else empty for j in range(per_group)], axis=0)
    score = dot(key_rows[:, group_at * LANES : (group_at + 1) * LANES], spread)
    weight = jnp.exp2(score).astype(BF16)
    ones = jnp.ones((16, value.shape[1]), BF16)
    both = dot(jnp.concatenate([value, ones], axis=0), weight)
    return both[:head_size, :], both[head_size : head_size + 1, :]


def local_kernel(heads, scale_ref, normed_ref, wq_ref, wk_ref, wv_ref, query_ref, num_ref, den_ref):
    normed = normed_ref[...]
    head_size = wq_ref.shape[0] // heads
    factors = [scale_ref[h] for h in range(heads)]
    queries = head_normed(dot_nt(wq_ref[...], normed), head_size, factors)
    for h in range(heads):
        query_ref[h * head_size : (h + 1) * head_size, :] = queries[h]
    key_rows = jnp.concatenate(head_normed(dot_nt(wk_ref[...], normed), head_size), axis=0).T
    values = dot_nt(wv_ref[...], normed).astype(BF16)
    for h in range(heads):
        rows = slice(h * head_size, (h + 1) * head_size)
        num, den = head_sums(queries[h], key_rows, values[rows, :], h, head_size)
        num_ref[rows, :] = num
        den_ref[h : h + 1, :] = den


def local_attention(normed, wq, wk, wv, scale):
    rows_dev, width = normed.shape
    heads = scale.shape[0]
    square = whole((width, width))
    columns = lambda rows: pl.BlockSpec((rows, BALL), lambda i: (0, i))
    return pl.pallas_call(
        functools.partial(local_kernel, heads),
        grid=(rows_dev // BALL,),
        in_specs=[
            pl.BlockSpec(memory_space=pltpu.SMEM),
            pl.BlockSpec((BALL, width), lambda i: (i, 0)),
            square,
            square,
            square,
        ],
        out_specs=[columns(width), columns(width), columns(heads)],
        out_shape=[
            jax.ShapeDtypeStruct((width, rows_dev), BF16),
            jax.ShapeDtypeStruct((width, rows_dev), F32),
            jax.ShapeDtypeStruct((heads, rows_dev), F32),
        ],
        compiler_params=params(),
        cost_estimate=pl.CostEstimate(
            flops=20 * rows_dev * width * width, bytes_accessed=8 * rows_dev * width, transcendentals=heads * rows_dev * BALL
        ),
        name="local_attention",
    )(scale, normed, wq, wk, wv)


def finish_kernel(
    heads,
    chosen_ref,
    candidates_ref,
    query_ref,
    num_ref,
    den_ref,
    grouped_ref,
    wpk_ref,
    wpv_ref,
    wo_ref,
    gain_ref,
    wg_ref,
    wu_ref,
    wd_ref,
    out_ref,
    attended,
):
    ball = pl.program_id(0)
    width = wpk_ref.shape[0]
    head_size = width // heads
    coarse = jnp.concatenate(
        [candidates_ref[chosen_ref[ball * OWNERS + o]] for o in range(OWNERS)], axis=0
    )
    key_rows = jnp.concatenate(head_normed(dot_nt(wpk_ref[...], coarse), head_size), axis=0).T
    values = dot_nt(wpv_ref[...], coarse).astype(BF16)
    for h in range(heads):
        rows = slice(h * head_size, (h + 1) * head_size)
        num, den = head_sums(query_ref[rows, :], key_rows, values[rows, :], h, head_size)
        num = num + num_ref[rows, :]
        den = den + den_ref[h : h + 1, :]
        attended[rows, :] = (num / den).astype(BF16)
    projected = dot(attended[...].T, wo_ref[...])
    residual = (grouped_ref[...].astype(F32) + projected).astype(BF16)
    rows32 = residual.astype(F32)
    mean_square = jnp.mean(rows32 * rows32, axis=-1, keepdims=True)
    ffn = (rows32 * lax.rsqrt(mean_square + 1e-05) * gain_ref[...]).astype(BF16)
    gate = dot(ffn, wg_ref[...])
    up = dot(ffn, wu_ref[...])
    hidden = (gate / (1.0 + jnp.exp(-gate)) * up).astype(BF16)
    out_ref[...] = (rows32 + dot(hidden, wd_ref[...])).astype(BF16)


def finish(chosen, candidates, query, num, den, grouped, wpk, wpv, wo, gain, wg, wu, wd):
    rows_dev, width = grouped.shape
    heads = den.shape[0]
    hidden = wg.shape[1]
    columns = lambda rows: pl.BlockSpec((rows, BALL), lambda i, *_: (0, i))
    return pl.pallas_call(
        functools.partial(finish_kernel, heads),
        grid_spec=pltpu.PrefetchScalarGridSpec(
            num_scalar_prefetch=1,
            grid=(rows_dev // BALL,),
            in_specs=[
                whole(candidates.shape),
                columns(width),
                columns(width),
                columns(heads),
                pl.BlockSpec((BALL, width), lambda i, *_: (i, 0)),
                whole(wpk.shape),
                whole(wpv.shape),
                whole(wo.shape),
                whole(gain.shape),
                whole(wg.shape),
                whole(wu.shape),
                whole(wd.shape),
            ],
            out_specs=pl.BlockSpec((BALL, width), lambda i, *_: (i, 0)),
            scratch_shapes=[pltpu.VMEM((width, BALL), BF16)],
        ),
        out_shape=jax.ShapeDtypeStruct((rows_dev, width), BF16),
        compiler_params=params(),
        cost_estimate=pl.CostEstimate(
            flops=2 * rows_dev * width * (3 * hidden + 6 * width),
            bytes_accessed=12 * rows_dev * width,
            transcendentals=heads * rows_dev * BALL // 2,
        ),
        name="finish_balls",
    )(chosen, candidates, query, num, den, grouped, wpk, wpv, wo, gain, wg, wu, wd)


def rows_kernel(ids_ref, source_ref, out_ref):
    first = pl.program_id(0) * (TILE // LANES)
    count = source_ref.shape[0]
    lane = lax.broadcasted_iota(jnp.int32, (LANES, LANES), 1).astype(F32)
    for u in range(TILE // LANES):
        wanted = column_of(ids_ref[pl.ds(first + u, 1), :])
        pick = jnp.concatenate(
            [
                jnp.where(wanted - float(c) == lane, 1.0, 0.0).astype(BF16)
                for c in range(0, count, LANES)
            ],
            axis=1,
        )
        out_ref[u * LANES : (u + 1) * LANES, :] = dot(pick, source_ref[...]).astype(BF16)


def take_rows(ids, source):
    rows_dev, width = source.shape
    return pl.pallas_call(
        rows_kernel,
        grid=(rows_dev // TILE,),
        in_specs=[whole(ids.shape), whole(source.shape)],
        out_specs=pl.BlockSpec((TILE, width), lambda i: (i, 0)),
        out_shape=jax.ShapeDtypeStruct((rows_dev, width), BF16),
        compiler_params=params(),
        cost_estimate=pl.CostEstimate(
            flops=2 * rows_dev * rows_dev * width, bytes_accessed=4 * rows_dev * width, transcendentals=0
        ),
        name="take_rows",
    )(ids, source)


def from_behind(block, axis, distance):
    devices = range(lax.axis_size(axis))
    route = [((i - distance) % len(devices), i) for i in devices]
    return lax.ppermute(block, axis, route)


def fetch_blocks(payload):
    return jnp.stack(
        [payload if k == 0 else from_behind(payload, "pts", k) for k in range(REACH, -REACH - 1, -1)]
    )


def on_device(
    points,
    point_row_index,
    neighbour_ball_list,
    attention_norm_gain,
    query_weight,
    key_weight,
    value_weight,
    pooled_key_weight,
    pooled_value_weight,
    head_score_scale,
    output_weight,
    feedforward_norm_gain,
    gate_weight,
    up_weight,
    down_weight,
):
    rows_dev, width = points.shape
    heads = head_score_scale.shape[0]
    peers = lax.axis_size("pts")
    me = lax.axis_index("pts")
    send_each = rows_dev // peers
    blocks_dev = rows_dev // BALL
    comp = BALL // POOL
    tiles = (rows_dev // LANES, LANES)

    def swap(array):
        return lax.all_to_all(array, "pts", split_axis=0, concat_axis=0, tiled=True)

    outgoing, outgoing_ids, rank = send_order(points, point_row_index.reshape(tiles))
    ids = swap(outgoing_ids.reshape(peers, send_each)).reshape(tiles).astype(F32)
    arrived = swap(outgoing.reshape(peers, send_each, width)).reshape(rows_dev, width)
    grouped, normed, pooled = group(ids, arrived, attention_norm_gain[None])
    candidates = fetch_blocks(pooled).reshape((2 * REACH + 1) * blocks_dev, comp, width)
    owner = neighbour_ball_list // blocks_dev
    offset = jnp.mod(owner - me + REACH, peers)
    chosen = (offset * blocks_dev + neighbour_ball_list % blocks_dev).reshape(-1)
    scale = head_score_scale * (LOG2E * heads / width)
    query, num, den = local_attention(normed, query_weight.T, key_weight.T, value_weight.T, scale)
    ball_out = finish(
        chosen,
        candidates,
        query,
        num,
        den,
        grouped,
        pooled_key_weight.T,
        pooled_value_weight.T,
        output_weight,
        feedforward_norm_gain[None],
        gate_weight,
        up_weight,
        down_weight,
    )
    returning = take_rows(ids, ball_out).reshape(peers, send_each, width)
    came_back = swap(returning).reshape(rows_dev, width)
    return take_rows(rank, came_back)


def solution(mesh):
    rows = P(("rep", "pts"), None)
    return jax.shard_map(
        on_device,
        mesh=mesh,
        in_specs=(rows, P(("rep", "pts")), rows) + (P(),) * 12,
        out_specs=rows,
        check_vma=False,
    )
```

```python
import functools
import math

import jax
import jax.numpy as jnp
from jax import lax
from jax.experimental import pallas as pl
from jax.experimental.pallas import tpu as pltpu
from jax.sharding import PartitionSpec as P

BALL = 256
POOL = 8
OWNERS = 4
REACH = 4
LANES = 128
TILE = 512
DEPTH = 512
BALLS_STEP = 2
LOW = 64
LOG2E = math.log2(math.e)
F32 = jnp.float32
BF16 = jnp.bfloat16
VMEM_BYTES = 40 * 1024 * 1024


def params(**kwargs):
    return pltpu.CompilerParams(vmem_limit_bytes=VMEM_BYTES, **kwargs)


def dot(a, b):
    return jnp.dot(a, b, preferred_element_type=F32)


def dot_nt(a, b):
    return lax.dot_general(a, b, (((1,), (1,)), ((), ())), preferred_element_type=F32)


def whole(shape):
    return pl.BlockSpec(shape, lambda *_: (0,) * len(shape))


def row_blocks(rows, width):
    return pl.BlockSpec((rows, width), lambda i, *_: (i, 0))


def column_of(row):
    return jnp.broadcast_to(row, (LANES, LANES)).T


def picked_rows(pick_tile, rows, source_ref):
    count = source_ref.shape[0]
    total = None
    for start in range(0, count, DEPTH):
        pick = jnp.concatenate(
            [pick_tile(t) for t in range(start // LANES, (start + DEPTH) // LANES)], axis=1
        )
        part = dot(pick, source_ref[start : start + DEPTH, :])
        total = part if total is None else total + part
    return total


def by_lane_ids(ids_ref, first, rows):
    targets = (lax.broadcasted_iota(jnp.int32, (rows, LANES), 0) + first).astype(F32)
    return lambda t: jnp.where(ids_ref[t : t + 1, :] == targets, 1.0, 0.0).astype(BF16)


def by_row_ids(ids_ref, first, rows):
    wanted = jnp.concatenate(
        [column_of(ids_ref[pl.ds(first + u, 1), :]) for u in range(rows // LANES)], axis=0
    )
    lane = lax.broadcasted_iota(jnp.int32, (rows, LANES), 1).astype(F32)
    return lambda t: jnp.where(wanted - float(t * LANES) == lane, 1.0, 0.0).astype(BF16)


def send_kernel(send_each, me_ref, index_ref, points_ref, out_ref, rank_ref, col, aux):
    rows_dev, width = points_ref.shape
    tiles = rows_dev // LANES
    chunks = width // LANES
    per_tile = LANES // send_each
    step = pl.program_id(0)

    @pl.when(step == 0)
    def _():
        for t in range(tiles):
            col[t * LANES : (t + 1) * LANES, :] = column_of(index_ref[t : t + 1, :].astype(F32))

        def rank_tile(t, carry):
            row = index_ref[pl.ds(t, 1), :].astype(F32)
            below = jnp.where(col[...] < row, 1.0, 0.0)
            rank_ref[pl.ds(t, 1), :] = jnp.sum(below, axis=0, keepdims=True)
            return carry

        lax.fori_loop(0, tiles, rank_tile, 0)
        local = lax.rem(col[...].astype(jnp.int32), rows_dev)
        lane = lax.broadcasted_iota(jnp.int32, (rows_dev, LANES), 1)
        high = lax.div(local, LOW)
        low = lax.rem(local, LOW)
        aux[...] = jnp.where(lane == 0, high, jnp.where(lane == 1, low, 0)).astype(F32).astype(BF16)

    tile = by_lane_ids(rank_ref, step * TILE, TILE)
    rows = picked_rows(tile, TILE, points_ref).astype(BF16)
    ids = picked_rows(tile, TILE, aux)
    for u in range(TILE // LANES):
        both = ids[u * LANES : (u + 1) * LANES, :].T[0:16, :]
        for v in range(per_tile):
            peer = u * per_tile + v
            mine = both
            if per_tile > 1:
                lane = lax.broadcasted_iota(jnp.int32, both.shape, 1)
                mine = jnp.where(lane // send_each == v, both, 0.0)
                mine = pltpu.roll(mine, (me_ref[0] - v + per_tile) % per_tile * send_each, 1)
            out_ref[peer, chunks * send_each :, :] = mine.astype(BF16)
            first = peer * send_each
            for c in range(chunks):
                out_ref[peer, c * send_each : (c + 1) * send_each, :] = rows[
                    first : first + send_each, c * LANES : (c + 1) * LANES
                ]


def send_order(points, index_tiles, me, peers):
    rows_dev, width = points.shape
    tiles = rows_dev // LANES
    send_each = rows_dev // peers
    payload = width // LANES * send_each + 16
    return pl.pallas_call(
        functools.partial(send_kernel, send_each),
        grid_spec=pltpu.PrefetchScalarGridSpec(
            num_scalar_prefetch=1,
            grid=(rows_dev // TILE,),
            in_specs=[whole((tiles, LANES)), whole((rows_dev, width))],
            out_specs=[
                pl.BlockSpec((TILE // send_each, payload, LANES), lambda i, *_: (i, 0, 0)),
                whole((tiles, LANES)),
            ],
            scratch_shapes=[
                pltpu.VMEM((rows_dev, LANES), F32),
                pltpu.VMEM((rows_dev, LANES), BF16),
            ],
        ),
        out_shape=[
            jax.ShapeDtypeStruct((peers, payload, LANES), BF16),
            jax.ShapeDtypeStruct((tiles, LANES), F32),
        ],
        compiler_params=params(),
        cost_estimate=pl.CostEstimate(
            flops=2 * rows_dev * rows_dev * (width + LANES), bytes_accessed=4 * rows_dev * width, transcendentals=0
        ),
        name="send_order",
    )(me.reshape(1), index_tiles, points)


def group_kernel(arrived_ref, gain_ref, grouped_ref, normed_ref, pooled_ref, ids_ref, source):
    peers = arrived_ref.shape[0]
    rows_dev, width = source.shape
    chunks = width // LANES
    send_each = rows_dev // peers
    per_tile = LANES // send_each

    @pl.when(pl.program_id(0) == 0)
    def _():
        for t in range(rows_dev // LANES):
            row = jnp.zeros((1, LANES), F32)
            for p in range(t * per_tile, (t + 1) * per_tile):
                both = arrived_ref[p, chunks * send_each :, :].astype(F32)
                row = row + both[0:1, :] * LOW + both[1:2, :]
            ids_ref[t : t + 1, :] = row
        for p in range(peers):
            for c in range(chunks):
                source[p * send_each : (p + 1) * send_each, c * LANES : (c + 1) * LANES] = arrived_ref[
                    p, c * send_each : (c + 1) * send_each, :
                ]

    tile = by_lane_ids(ids_ref, pl.program_id(0) * TILE, TILE)
    grouped = picked_rows(tile, TILE, source)
    grouped_ref[...] = grouped.astype(BF16)
    mean_square = jnp.mean(grouped * grouped, axis=-1, keepdims=True)
    normed = (grouped * lax.rsqrt(mean_square + 1e-05) * gain_ref[...]).astype(BF16)
    normed_ref[...] = normed
    mean_of = block_matrix(TILE // POOL, 1, TILE, POOL, 1.0 / POOL)
    pooled_ref[...] = dot(mean_of, normed).astype(BF16)


def group(arrived, gain, rows_dev):
    width = gain.shape[1]
    tiles = rows_dev // LANES
    return pl.pallas_call(
        group_kernel,
        grid=(rows_dev // TILE,),
        in_specs=[whole(arrived.shape), whole((1, width))],
        out_specs=[
            row_blocks(TILE, width),
            row_blocks(TILE, width),
            row_blocks(TILE // POOL, width),
            whole((tiles, LANES)),
        ],
        out_shape=[
            jax.ShapeDtypeStruct((rows_dev, width), BF16),
            jax.ShapeDtypeStruct((rows_dev, width), BF16),
            jax.ShapeDtypeStruct((rows_dev // POOL, width), BF16),
            jax.ShapeDtypeStruct((tiles, LANES), F32),
        ],
        scratch_shapes=[pltpu.VMEM((rows_dev, width), BF16)],
        compiler_params=params(),
        cost_estimate=pl.CostEstimate(
            flops=2 * rows_dev * rows_dev * width, bytes_accessed=6 * rows_dev * width, transcendentals=0
        ),
        name="group_balls",
    )(arrived, gain)


def block_matrix(rows, row_step, cols, col_step, value):
    row = lax.broadcasted_iota(jnp.int32, (rows, cols), 0) // row_step
    col = lax.broadcasted_iota(jnp.int32, (rows, cols), 1) // col_step
    return jnp.where(row == col, value, 0.0).astype(BF16)


def clear_spread(head_size, keys_ref, values_ref):
    keys_ref[...] = jnp.zeros_like(keys_ref)
    ones = block_matrix(values_ref.shape[1], values_ref.shape[1] * head_size // LANES, LANES, head_size, 1.0)
    for g in range(values_ref.shape[0]):
        values_ref[g, :, LANES:] = ones


def spread_keys(head_size, columns, ref):
    count = columns.shape[1]
    per_group = LANES // head_size
    for h in range(columns.shape[0] // head_size):
        g, j = h // per_group, h % per_group
        part = columns[h * head_size : (h + 1) * head_size, :]
        root = lax.rsqrt(jnp.mean(part * part, axis=0, keepdims=True) + 1e-06)
        ref[g, j * head_size : (j + 1) * head_size, j * count : (j + 1) * count] = (part * root).astype(BF16)


def spread_values(head_size, values, ref):
    count, width = values.shape
    head = lax.broadcasted_iota(jnp.int32, (count, LANES), 1) // head_size
    for g in range(width // LANES):
        lanes = values[:, g * LANES : (g + 1) * LANES]
        for j in range(LANES // head_size):
            ref[g, j * count : (j + 1) * count, :LANES] = jnp.where(head == j, lanes, jnp.zeros((), BF16))


def local_kernel(head_size, scale_ref, normed_ref, wq_ref, wk_ref, wv_ref, query_ref, num_ref, den_ref, mean_of, keys, values, weights):
    width = normed_ref.shape[1]
    half = mean_of.shape[0]

    @pl.when(pl.program_id(0) == 0)
    def _():
        mean_of[...] = block_matrix(half, head_size, half, head_size, 1.0 / head_size)
        clear_spread(head_size, keys, values)

    normed = normed_ref[...]
    query = dot(normed, wq_ref[...])
    square = query * query
    high = square.astype(BF16)
    low = (square - high.astype(F32)).astype(BF16)
    mean_square = jnp.concatenate(
        [
            dot(high[:, c : c + half], mean_of[...]) + dot(low[:, c : c + half], mean_of[...])
            for c in range(0, width, half)
        ],
        axis=1,
    )
    query = (query * lax.rsqrt(mean_square + 1e-06) * scale_ref[...]).astype(BF16)
    query_ref[...] = query
    spread_keys(head_size, dot_nt(wk_ref[...], normed), keys)
    spread_values(head_size, dot(normed, wv_ref[...]).astype(BF16), values)
    groups = width // LANES
    for g in range(groups):
        weights[g] = jnp.exp2(dot(query[:, g * LANES : (g + 1) * LANES], keys[g])).astype(BF16)
    for g in range(groups):
        both = dot(weights[g], values[g])
        num_ref[:, g * LANES : (g + 1) * LANES] = both[:, :LANES]
        den_ref[:, g * LANES : (g + 1) * LANES] = both[:, LANES:]


def local_attention(normed, wq, wk, wv, scale, head_size):
    rows_dev, width = normed.shape
    square = whole((width, width))
    groups = width // LANES
    spread = LANES // head_size * BALL
    return pl.pallas_call(
        functools.partial(local_kernel, head_size),
        grid=(rows_dev // BALL,),
        in_specs=[whole((1, width)), row_blocks(BALL, width), square, square, square],
        out_specs=[row_blocks(BALL, width)] * 3,
        out_shape=[
            jax.ShapeDtypeStruct((rows_dev, width), BF16),
            jax.ShapeDtypeStruct((rows_dev, width), F32),
            jax.ShapeDtypeStruct((rows_dev, width), F32),
        ],
        scratch_shapes=[
            pltpu.VMEM((2 * LANES, 2 * LANES), BF16),
            pltpu.VMEM((groups, LANES, spread), BF16),
            pltpu.VMEM((groups, spread, 2 * LANES), BF16),
            pltpu.VMEM((groups, BALL, spread), BF16),
        ],
        compiler_params=params(),
        cost_estimate=pl.CostEstimate(
            flops=20 * rows_dev * width * width, bytes_accessed=12 * rows_dev * width, transcendentals=0
        ),
        name="local_attention",
    )(scale, normed, wq, wk, wv)


def finish_kernel(
    head_size,
    chosen_ref,
    candidates_ref,
    query_ref,
    num_ref,
    den_ref,
    grouped_ref,
    wpk_ref,
    wpv_ref,
    wo_ref,
    gain_ref,
    wg_ref,
    wu_ref,
    wd_ref,
    out_ref,
    keys,
    values,
    weights,
    attended,
):
    step = pl.program_id(0)
    groups = wo_ref.shape[0] // LANES
    far = OWNERS * BALL // POOL

    @pl.when(step == 0)
    def _():
        for b in range(BALLS_STEP):
            clear_spread(head_size, keys.at[b], values.at[b])

    first = step * BALLS_STEP * OWNERS
    coarse = jnp.concatenate(
        [candidates_ref[chosen_ref[first + o]] for o in range(BALLS_STEP * OWNERS)], axis=0
    )
    key_columns = dot_nt(wpk_ref[...], coarse)
    value_rows = dot(coarse, wpv_ref[...]).astype(BF16)
    for b in range(BALLS_STEP):
        spread_keys(head_size, key_columns[:, b * far : (b + 1) * far], keys.at[b])
        spread_values(head_size, value_rows[b * far : (b + 1) * far, :], values.at[b])
    for b in range(BALLS_STEP):
        rows = slice(b * BALL, (b + 1) * BALL)
        for g in range(groups):
            score = dot(query_ref[rows, g * LANES : (g + 1) * LANES], keys[b, g])
            weights[b, g] = jnp.exp2(score).astype(BF16)
    for b in range(BALLS_STEP):
        rows = slice(b * BALL, (b + 1) * BALL)
        for g in range(groups):
            lanes = slice(g * LANES, (g + 1) * LANES)
            both = dot(weights[b, g], values[b, g])
            num = both[:, :LANES] + num_ref[rows, lanes]
            den = both[:, LANES:] + den_ref[rows, lanes]
            attended[rows, lanes] = (num / den).astype(BF16)
    projected = dot(attended[...], wo_ref[...])
    residual = (grouped_ref[...].astype(F32) + projected).astype(BF16)
    rows32 = residual.astype(F32)
    mean_square = jnp.mean(rows32 * rows32, axis=-1, keepdims=True)
    ffn = (rows32 * lax.rsqrt(mean_square + 1e-05) * gain_ref[...]).astype(BF16)
    gate = dot(ffn, wg_ref[...])
    up = dot(ffn, wu_ref[...])
    hidden = (0.5 * gate * (1.0 + jnp.tanh(0.5 * gate)) * up).astype(BF16)
    out_ref[...] = (rows32 + dot(hidden, wd_ref[...])).astype(BF16)


def finish(chosen, candidates, query, num, den, grouped, wpk, wpv, wo, gain, wg, wu, wd, head_size):
    rows_dev, width = grouped.shape
    hidden = wg.shape[1]
    groups = width // LANES
    step_rows = BALLS_STEP * BALL
    spread = LANES // head_size * OWNERS * BALL // POOL
    rows = row_blocks(step_rows, width)
    fixed = [wpk, wpv, wo, gain, wg, wu, wd]
    return pl.pallas_call(
        functools.partial(finish_kernel, head_size),
        grid_spec=pltpu.PrefetchScalarGridSpec(
            num_scalar_prefetch=1,
            grid=(rows_dev // step_rows,),
            in_specs=[whole(candidates.shape), rows, rows, rows, rows] + [whole(a.shape) for a in fixed],
            out_specs=rows,
            scratch_shapes=[
                pltpu.VMEM((BALLS_STEP, groups, LANES, spread), BF16),
                pltpu.VMEM((BALLS_STEP, groups, spread, 2 * LANES), BF16),
                pltpu.VMEM((BALLS_STEP, groups, BALL, spread), BF16),
                pltpu.VMEM((step_rows, width), BF16),
            ],
        ),
        out_shape=jax.ShapeDtypeStruct((rows_dev, width), BF16),
        compiler_params=params(),
        cost_estimate=pl.CostEstimate(
            flops=2 * rows_dev * width * (3 * hidden + 6 * width),
            bytes_accessed=12 * rows_dev * width,
            transcendentals=0,
        ),
        name="finish_balls",
    )(chosen, candidates, query, num, den, grouped, *fixed)


def rows_kernel(ids_ref, source_ref, out_ref):
    tile = by_row_ids(ids_ref, pl.program_id(0) * (TILE // LANES), TILE)
    out_ref[...] = picked_rows(tile, TILE, source_ref).astype(BF16)


def take_rows(ids, source):
    rows_dev, width = source.shape
    return pl.pallas_call(
        rows_kernel,
        grid=(rows_dev // TILE,),
        in_specs=[whole(ids.shape), whole(source.shape)],
        out_specs=row_blocks(TILE, width),
        out_shape=jax.ShapeDtypeStruct((rows_dev, width), BF16),
        compiler_params=params(),
        cost_estimate=pl.CostEstimate(
            flops=2 * rows_dev * rows_dev * width, bytes_accessed=4 * rows_dev * width, transcendentals=0
        ),
        name="take_rows",
    )(ids, source)


def from_behind(block, axis, distance):
    devices = range(lax.axis_size(axis))
    route = [((i - distance) % len(devices), i) for i in devices]
    return lax.ppermute(block, axis, route)


def fetch_blocks(payload):
    return jnp.stack(
        [payload if k == 0 else from_behind(payload, "pts", k) for k in range(REACH, -REACH - 1, -1)]
    )


def on_device(
    points,
    point_row_index,
    neighbour_ball_list,
    attention_norm_gain,
    query_weight,
    key_weight,
    value_weight,
    pooled_key_weight,
    pooled_value_weight,
    head_score_scale,
    output_weight,
    feedforward_norm_gain,
    gate_weight,
    up_weight,
    down_weight,
):
    rows_dev, width = points.shape
    head_size = width // head_score_scale.shape[0]
    peers = lax.axis_size("pts")
    me = lax.axis_index("pts")
    send_each = rows_dev // peers
    blocks_dev = rows_dev // BALL
    comp = BALL // POOL

    def swap(array):
        return lax.all_to_all(array, "pts", split_axis=0, concat_axis=0, tiled=True)

    outgoing, rank = send_order(points, point_row_index.reshape(rows_dev // LANES, LANES), me, peers)
    grouped, normed, pooled, ids = group(swap(outgoing), attention_norm_gain[None], rows_dev)
    candidates = fetch_blocks(pooled).reshape((2 * REACH + 1) * blocks_dev, comp, width)
    owner = neighbour_ball_list // blocks_dev
    offset = jnp.mod(owner - me + REACH, peers)
    chosen = (offset * blocks_dev + neighbour_ball_list % blocks_dev).reshape(-1)
    scale = jnp.repeat(head_score_scale * (LOG2E / head_size), head_size)[None]
    query, num, den = local_attention(normed, query_weight, key_weight.T, value_weight, scale, head_size)
    ball_out = finish(
        chosen,
        candidates,
        query,
        num,
        den,
        grouped,
        pooled_key_weight.T,
        pooled_value_weight,
        output_weight,
        feedforward_norm_gain[None],
        gate_weight,
        up_weight,
        down_weight,
        head_size,
    )
    returning = take_rows(ids, ball_out).reshape(peers, send_each, width)
    came_back = swap(returning).reshape(rows_dev, width)
    return take_rows(rank, came_back)


def solution(mesh):
    rows = P(("rep", "pts"), None)
    return jax.shard_map(
        on_device,
        mesh=mesh,
        in_specs=(rows, P(("rep", "pts")), rows) + (P(),) * 12,
        out_specs=rows,
        check_vma=False,
    )
```

```python
import functools
import math

import jax
import jax.numpy as jnp
from jax import lax
from jax.experimental import pallas as pl
from jax.experimental.pallas import tpu as pltpu
from jax.sharding import PartitionSpec as P

BALL = 256
POOL = 8
OWNERS = 4
GROUP = 4
LANES = 128
TILE = 512
DEPTH = 512
BALLS_STEP = 2
LOW = 64
LOG2E = math.log2(math.e)
F32 = jnp.float32
BF16 = jnp.bfloat16


def params(mebibytes=40):
    return pltpu.CompilerParams(vmem_limit_bytes=mebibytes * 1024 * 1024)


def dot(a, b):
    return jnp.dot(a, b, preferred_element_type=F32)


def dot_nt(a, b):
    return lax.dot_general(a, b, (((1,), (1,)), ((), ())), preferred_element_type=F32)


def whole(shape):
    return pl.BlockSpec(shape, lambda *_: (0,) * len(shape))


def row_blocks(rows, width):
    return pl.BlockSpec((rows, width), lambda i, *_: (i, 0))


def column_of(row):
    return jnp.broadcast_to(row, (LANES, LANES)).T


def picked_rows(pick_tile, rows, source_ref):
    count = source_ref.shape[0]
    total = None
    for start in range(0, count, DEPTH):
        pick = jnp.concatenate(
            [pick_tile(t) for t in range(start // LANES, (start + DEPTH) // LANES)], axis=1
        )
        part = dot(pick, source_ref[start : start + DEPTH, :])
        total = part if total is None else total + part
    return total


def by_lane_ids(ids_ref, first, rows):
    targets = (lax.broadcasted_iota(jnp.int32, (rows, LANES), 0) + first).astype(F32)
    return lambda t: jnp.where(ids_ref[t : t + 1, :] == targets, 1.0, 0.0).astype(BF16)


def by_row_ids(ids_ref, first, rows):
    wanted = jnp.concatenate(
        [column_of(ids_ref[pl.ds(first + u, 1), :]) for u in range(rows // LANES)], axis=0
    )
    lane = lax.broadcasted_iota(jnp.int32, (rows, LANES), 1).astype(F32)
    return lambda t: jnp.where(wanted - float(t * LANES) == lane, 1.0, 0.0).astype(BF16)


def send_kernel(send_each, me_ref, index_ref, points_ref, out_ref, slot_ref, held, aux, arrivals):
    rows_dev, width = held.shape
    tiles = rows_dev // LANES
    chunks = width // LANES
    per_tile = LANES // send_each
    peers = rows_dev // send_each
    step = pl.program_id(0)
    pieces = [
        pltpu.make_async_copy(points_ref.at[pl.ds(k, DEPTH)], held.at[pl.ds(k, DEPTH)], arrivals.at[k // DEPTH])
        for k in range(0, rows_dev, DEPTH)
    ]

    @pl.when(step == 0)
    def _():
        for piece in pieces:
            piece.start()
        index = index_ref[...].astype(F32)
        dest = jnp.floor(index * (1.0 / rows_dev))
        local = index - dest * rows_dev
        high = jnp.floor(local * (1.0 / LOW))
        low = local - high * LOW
        row = lax.broadcasted_iota(jnp.int32, (LANES, LANES), 0)
        for t in range(tiles):
            pair = jnp.where(row == 0, high[t : t + 1, :], jnp.where(row == 1, low[t : t + 1, :], 0.0))
            aux[t * LANES : (t + 1) * LANES, :] = pair.T.astype(BF16)
        peer = lax.broadcasted_iota(jnp.int32, (peers, LANES), 0).astype(F32)
        member = [jnp.where(dest[t : t + 1, :] == peer, 1.0, 0.0) for t in range(tiles)]
        lane = lax.broadcasted_iota(jnp.int32, (LANES, LANES), 1)
        up_to = jnp.where(row <= lane, 1.0, 0.0).astype(BF16)
        counts = dot(jnp.concatenate(member, axis=0).astype(BF16), up_to)
        before = peer[:, 0:1] * send_each - 1.0
        for t in range(tiles):
            count = counts[t * peers : (t + 1) * peers, :]
            slot_ref[t : t + 1, :] = jnp.sum(member[t] * (count + before), axis=0, keepdims=True)
            before = before + count[:, LANES - 1 :]
        for piece in pieces:
            piece.wait()

    tile = by_lane_ids(slot_ref, step * TILE, TILE)
    rows = picked_rows(tile, TILE, held).astype(BF16)
    ids = picked_rows(tile, TILE, aux)
    for u in range(TILE // LANES):
        both = ids[u * LANES : (u + 1) * LANES, :].T[0:16, :]
        for v in range(per_tile):
            peer = u * per_tile + v
            mine = both
            if per_tile > 1:
                lane = lax.broadcasted_iota(jnp.int32, both.shape, 1)
                mine = jnp.where(lane // send_each == v, both, 0.0)
                mine = pltpu.roll(mine, (me_ref[0] - v + per_tile) % per_tile * send_each, 1)
            out_ref[peer, chunks * send_each :, :] = mine.astype(BF16)
            first = peer * send_each
            for c in range(chunks):
                out_ref[peer, c * send_each : (c + 1) * send_each, :] = rows[
                    first : first + send_each, c * LANES : (c + 1) * LANES
                ]


def send_order(points, index_tiles, me, peers):
    rows_dev, width = points.shape
    tiles = rows_dev // LANES
    send_each = rows_dev // peers
    payload = width // LANES * send_each + 16
    return pl.pallas_call(
        functools.partial(send_kernel, send_each),
        grid_spec=pltpu.PrefetchScalarGridSpec(
            num_scalar_prefetch=1,
            grid=(rows_dev // TILE,),
            in_specs=[whole((tiles, LANES)), pl.BlockSpec(memory_space=pl.ANY)],
            out_specs=[
                pl.BlockSpec((TILE // send_each, payload, LANES), lambda i, *_: (i, 0, 0)),
                whole((tiles, LANES)),
            ],
            scratch_shapes=[
                pltpu.VMEM((rows_dev, width), BF16),
                pltpu.VMEM((rows_dev, LANES), BF16),
                pltpu.SemaphoreType.DMA((rows_dev // DEPTH,)),
            ],
        ),
        out_shape=[
            jax.ShapeDtypeStruct((peers, payload, LANES), BF16),
            jax.ShapeDtypeStruct((tiles, LANES), F32),
        ],
        compiler_params=params(60),
        cost_estimate=pl.CostEstimate(
            flops=2 * rows_dev * rows_dev * (width + LANES), bytes_accessed=4 * rows_dev * width, transcendentals=0
        ),
        name="send_order",
    )(me.reshape(1), index_tiles, points)


def normed_rows(rows32, gain):
    mean_square = jnp.mean(rows32 * rows32, axis=-1, keepdims=True)
    return (rows32 * lax.rsqrt(mean_square + 1e-05) * gain).astype(BF16)


def pool_kernel(arrived_ref, gain_ref, source_ref, ids_ref, pooled_ref, ids, total):
    peers = arrived_ref.shape[0]
    rows, width = source_ref.shape
    chunks = width // LANES
    send_each = rows // peers
    per_tile = LANES // send_each
    step = pl.program_id(0)

    @pl.when(step == 0)
    def _():
        total[...] = jnp.zeros_like(total)

    for t in range(rows // LANES):
        row = jnp.zeros((1, LANES), F32)
        for p in range(t * per_tile, (t + 1) * per_tile):
            both = arrived_ref[p, chunks * send_each :, :].astype(F32)
            row = row + both[0:1, :] * LOW + both[1:2, :]
        ids[t : t + 1, :] = row
        ids_ref[pl.ds(step * (rows // LANES) + t, 1), :] = row
    for p in range(peers):
        for c in range(chunks):
            source_ref[p * send_each : (p + 1) * send_each, c * LANES : (c + 1) * LANES] = arrived_ref[
                p, c * send_each : (c + 1) * send_each, :
            ]
    normed = normed_rows(source_ref[...].astype(F32), gain_ref[...])
    pools = total.shape[0]
    pool = lax.broadcasted_iota(jnp.int32, (pools, LANES), 0).astype(F32)
    pick = jnp.concatenate(
        [
            jnp.where(jnp.floor(ids[t : t + 1, :] * (1.0 / POOL)) == pool, 1.0 / POOL, 0.0).astype(BF16)
            for t in range(rows // LANES)
        ],
        axis=1,
    )
    total[...] += dot(pick, normed)

    @pl.when(step == pl.num_programs(0) - 1)
    def _():
        pooled_ref[...] = total[...].astype(BF16)


def pool(arrived, gain, rows_dev):
    width = gain.shape[1]
    tiles = rows_dev // LANES
    peers, payload, _ = arrived.shape
    steps = rows_dev // TILE
    pooled = (rows_dev // POOL, width)
    return pl.pallas_call(
        pool_kernel,
        grid=(steps,),
        in_specs=[
            pl.BlockSpec((peers // steps, payload, LANES), lambda i: (i, 0, 0)),
            whole((1, width)),
        ],
        out_specs=[row_blocks(TILE, width), whole((tiles, LANES)), whole(pooled)],
        out_shape=[
            jax.ShapeDtypeStruct((rows_dev, width), BF16),
            jax.ShapeDtypeStruct((tiles, LANES), F32),
            jax.ShapeDtypeStruct(pooled, BF16),
        ],
        scratch_shapes=[pltpu.VMEM((TILE // LANES, LANES), F32), pltpu.VMEM(pooled, F32)],
        compiler_params=params(),
        cost_estimate=pl.CostEstimate(
            flops=rows_dev * rows_dev * width // 4, bytes_accessed=4 * rows_dev * width, transcendentals=0
        ),
        name="pool_arrived",
    )(arrived, gain)


def group_kernel(ids_ref, source_ref, gain_ref, grouped_ref, normed_ref):
    tile = by_lane_ids(ids_ref, pl.program_id(0) * TILE, TILE)
    grouped = picked_rows(tile, TILE, source_ref)
    grouped_ref[...] = grouped.astype(BF16)
    normed_ref[...] = normed_rows(grouped, gain_ref[...])


def group(ids, source, gain):
    rows_dev, width = source.shape
    rows = row_blocks(TILE, width)
    return pl.pallas_call(
        group_kernel,
        grid=(rows_dev // TILE,),
        in_specs=[whole(ids.shape), whole(source.shape), whole((1, width))],
        out_specs=[rows, rows],
        out_shape=[jax.ShapeDtypeStruct((rows_dev, width), BF16)] * 2,
        compiler_params=params(),
        cost_estimate=pl.CostEstimate(
            flops=2 * rows_dev * rows_dev * width, bytes_accessed=6 * rows_dev * width, transcendentals=0
        ),
        name="group_balls",
    )(ids, source, gain)


def block_matrix(rows, row_step, cols, col_step, value):
    row = lax.broadcasted_iota(jnp.int32, (rows, cols), 0) // row_step
    col = lax.broadcasted_iota(jnp.int32, (rows, cols), 1) // col_step
    return jnp.where(row == col, value, 0.0).astype(BF16)


def clear_spread(head_size, keys_ref, values_ref):
    keys_ref[...] = jnp.zeros_like(keys_ref)
    ones = block_matrix(values_ref.shape[1], values_ref.shape[1] * head_size // LANES, LANES, head_size, 1.0)
    for g in range(values_ref.shape[0]):
        values_ref[g, :, LANES:] = ones


def spread_keys(head_size, columns, ref):
    count = columns.shape[1]
    per_group = LANES // head_size
    for h in range(columns.shape[0] // head_size):
        g, j = h // per_group, h % per_group
        part = columns[h * head_size : (h + 1) * head_size, :]
        root = lax.rsqrt(jnp.mean(part * part, axis=0, keepdims=True) + 1e-06)
        ref[g, j * head_size : (j + 1) * head_size, j * count : (j + 1) * count] = (part * root).astype(BF16)


def spread_values(head_size, values, ref):
    count, width = values.shape
    head = lax.broadcasted_iota(jnp.int32, (count, LANES), 1) // head_size
    for g in range(width // LANES):
        lanes = values[:, g * LANES : (g + 1) * LANES]
        for j in range(LANES // head_size):
            ref[g, j * count : (j + 1) * count, :LANES] = jnp.where(head == j, lanes, jnp.zeros((), BF16))


def local_kernel(head_size, scale_ref, normed_ref, wq_ref, wk_ref, wv_ref, *rest):
    query_ref, num_ref, den_ref, mean_of, keys, values, weights = rest[-7:]
    width = normed_ref.shape[1]
    half = mean_of.shape[0]

    @pl.when(pl.program_id(0) == 0)
    def _():
        mean_of[...] = block_matrix(half, head_size, half, head_size, 1.0 / head_size)
        clear_spread(head_size, keys, values)

    normed = normed_ref[...]
    query = dot(normed, wq_ref[...])
    square = query * query
    high = square.astype(BF16)
    low = (square - high.astype(F32)).astype(BF16)
    mean_square = jnp.concatenate(
        [
            dot(high[:, c : c + half], mean_of[...]) + dot(low[:, c : c + half], mean_of[...])
            for c in range(0, width, half)
        ],
        axis=1,
    )
    query = (query * lax.rsqrt(mean_square + 1e-06) * scale_ref[...]).astype(BF16)
    query_ref[...] = query
    spread_keys(head_size, dot_nt(wk_ref[...], normed), keys)
    spread_values(head_size, dot(normed, wv_ref[...]).astype(BF16), values)
    groups = width // LANES
    for g in range(groups):
        weights[g] = jnp.exp2(dot(query[:, g * LANES : (g + 1) * LANES], keys[g])).astype(BF16)
    for g in range(groups):
        both = dot(weights[g], values[g])
        num_ref[:, g * LANES : (g + 1) * LANES] = both[:, :LANES]
        den_ref[:, g * LANES : (g + 1) * LANES] = both[:, LANES:]


def local_attention(part, parts, normed, wq, wk, wv, scale, head_size, earlier=()):
    rows_dev, width = normed.shape
    square = whole((width, width))
    groups = width // LANES
    spread = LANES // head_size * BALL
    steps = rows_dev // BALL // parts
    rows = pl.BlockSpec((BALL, width), lambda i: (part * steps + i, 0))
    return pl.pallas_call(
        functools.partial(local_kernel, head_size),
        grid=(steps,),
        in_specs=[whole((1, width)), rows, square, square, square]
        + [pl.BlockSpec(memory_space=pl.ANY)] * len(earlier),
        out_specs=[rows] * 3,
        out_shape=[
            jax.ShapeDtypeStruct((rows_dev, width), BF16),
            jax.ShapeDtypeStruct((rows_dev, width), F32),
            jax.ShapeDtypeStruct((rows_dev, width), F32),
        ],
        scratch_shapes=[
            pltpu.VMEM((2 * LANES, 2 * LANES), BF16),
            pltpu.VMEM((groups, LANES, spread), BF16),
            pltpu.VMEM((groups, spread, 2 * LANES), BF16),
            pltpu.VMEM((groups, BALL, spread), BF16),
        ],
        input_output_aliases={5 + k: k for k in range(len(earlier))},
        compiler_params=params(),
        cost_estimate=pl.CostEstimate(
            flops=20 * rows_dev * width * width // parts, bytes_accessed=12 * rows_dev * width // parts, transcendentals=0
        ),
        name="local_attention",
    )(scale, normed, wq, wk, wv, *earlier)


def finish_kernel(
    head_size,
    chosen_ref,
    candidates_ref,
    query_ref,
    num_ref,
    den_ref,
    grouped_ref,
    wpk_ref,
    wpv_ref,
    wo_ref,
    gain_ref,
    wg_ref,
    wu_ref,
    wd_ref,
    out_ref,
    keys,
    values,
    weights,
    attended,
):
    step = pl.program_id(0)
    groups = wo_ref.shape[0] // LANES
    far = OWNERS * BALL // POOL

    @pl.when(step == 0)
    def _():
        for b in range(BALLS_STEP):
            clear_spread(head_size, keys.at[b], values.at[b])

    first = step * BALLS_STEP * OWNERS
    coarse = jnp.concatenate(
        [candidates_ref[chosen_ref[first + o]] for o in range(BALLS_STEP * OWNERS)], axis=0
    )
    key_columns = dot_nt(wpk_ref[...], coarse)
    value_rows = dot(coarse, wpv_ref[...]).astype(BF16)
    for b in range(BALLS_STEP):
        spread_keys(head_size, key_columns[:, b * far : (b + 1) * far], keys.at[b])
        spread_values(head_size, value_rows[b * far : (b + 1) * far, :], values.at[b])
    for b in range(BALLS_STEP):
        rows = slice(b * BALL, (b + 1) * BALL)
        for g in range(groups):
            score = dot(query_ref[rows, g * LANES : (g + 1) * LANES], keys[b, g])
            weights[b, g] = jnp.exp2(score).astype(BF16)
    for b in range(BALLS_STEP):
        rows = slice(b * BALL, (b + 1) * BALL)
        for g in range(groups):
            lanes = slice(g * LANES, (g + 1) * LANES)
            both = dot(weights[b, g], values[b, g])
            num = both[:, :LANES] + num_ref[rows, lanes]
            den = both[:, LANES:] + den_ref[rows, lanes]
            attended[rows, lanes] = (num / den).astype(BF16)
    projected = dot(attended[...], wo_ref[...])
    residual = (grouped_ref[...].astype(F32) + projected).astype(BF16)
    rows32 = residual.astype(F32)
    ffn = normed_rows(rows32, gain_ref[...])
    gate = dot(ffn, wg_ref[...])
    up = dot(ffn, wu_ref[...])
    hidden = (0.5 * gate * (1.0 + jnp.tanh(0.5 * gate)) * up).astype(BF16)
    out_ref[...] = (rows32 + dot(hidden, wd_ref[...])).astype(BF16)


def finish(chosen, candidates, query, num, den, grouped, wpk, wpv, wo, gain, wg, wu, wd, head_size):
    rows_dev, width = grouped.shape
    hidden = wg.shape[1]
    groups = width // LANES
    step_rows = BALLS_STEP * BALL
    spread = LANES // head_size * OWNERS * BALL // POOL
    rows = row_blocks(step_rows, width)
    fixed = [wpk, wpv, wo, gain, wg, wu, wd]
    return pl.pallas_call(
        functools.partial(finish_kernel, head_size),
        grid_spec=pltpu.PrefetchScalarGridSpec(
            num_scalar_prefetch=1,
            grid=(rows_dev // step_rows,),
            in_specs=[whole(candidates.shape), rows, rows, rows, rows] + [whole(a.shape) for a in fixed],
            out_specs=rows,
            scratch_shapes=[
                pltpu.VMEM((BALLS_STEP, groups, LANES, spread), BF16),
                pltpu.VMEM((BALLS_STEP, groups, spread, 2 * LANES), BF16),
                pltpu.VMEM((BALLS_STEP, groups, BALL, spread), BF16),
                pltpu.VMEM((step_rows, width), BF16),
            ],
        ),
        out_shape=jax.ShapeDtypeStruct((rows_dev, width), BF16),
        compiler_params=params(),
        cost_estimate=pl.CostEstimate(
            flops=2 * rows_dev * width * (3 * hidden + 6 * width),
            bytes_accessed=12 * rows_dev * width,
            transcendentals=0,
        ),
        name="finish_balls",
    )(chosen, candidates, query, num, den, grouped, *fixed)


def rows_kernel(ids_ref, source_ref, out_ref):
    tile = by_row_ids(ids_ref, pl.program_id(0) * (TILE // LANES), TILE)
    out_ref[...] = picked_rows(tile, TILE, source_ref).astype(BF16)


def take_rows(ids, source):
    rows_dev, width = source.shape
    return pl.pallas_call(
        rows_kernel,
        grid=(rows_dev // TILE,),
        in_specs=[whole(ids.shape), whole(source.shape)],
        out_specs=row_blocks(TILE, width),
        out_shape=jax.ShapeDtypeStruct((rows_dev, width), BF16),
        compiler_params=params(),
        cost_estimate=pl.CostEstimate(
            flops=2 * rows_dev * rows_dev * width, bytes_accessed=4 * rows_dev * width, transcendentals=0
        ),
        name="take_rows",
    )(ids, source)


def route(block, target):
    devices = range(lax.axis_size("pts"))
    return lax.ppermute(block, "pts", [(i, target(i) % len(devices)) for i in devices])


def to_mate(block, mate):
    return route(block, lambda i: i ^ mate)


def first_stage(pooled):
    below = route(pooled, lambda i: i + GROUP)
    above = route(pooled, lambda i: i - GROUP)
    return below, above, [to_mate(pooled, mate) for mate in range(1, GROUP)]


def second_stage(below, above, place):
    return [
        to_mate(jnp.where(place > (place ^ mate), below, above), mate) for mate in range(1, GROUP)
    ]


def block_slots(owner, me, peers):
    mate = (owner % GROUP) ^ (me % GROUP)
    ahead = jnp.mod(owner // GROUP - me // GROUP, peers // GROUP)
    outside = jnp.where(mate == 0, jnp.where(ahead == 1, GROUP + 1, GROUP), GROUP + 1 + mate)
    return jnp.where(ahead == 0, mate, outside)


def on_device(
    points,
    point_row_index,
    neighbour_ball_list,
    attention_norm_gain,
    query_weight,
    key_weight,
    value_weight,
    pooled_key_weight,
    pooled_value_weight,
    head_score_scale,
    output_weight,
    feedforward_norm_gain,
    gate_weight,
    up_weight,
    down_weight,
):
    rows_dev, width = points.shape
    head_size = width // head_score_scale.shape[0]
    peers = lax.axis_size("pts")
    me = lax.axis_index("pts")
    send_each = rows_dev // peers
    blocks_dev = rows_dev // BALL
    comp = BALL // POOL

    def swap(array):
        return lax.all_to_all(array, "pts", split_axis=0, concat_axis=0, tiled=True)

    outgoing, slot = send_order(points, point_row_index.reshape(rows_dev // LANES, LANES), me, peers)
    source, ids, pooled = pool(swap(outgoing), attention_norm_gain[None], rows_dev)
    below, above, mates = first_stage(pooled)
    grouped, normed = group(ids, source, attention_norm_gain[None])
    scale = jnp.repeat(head_score_scale * (LOG2E / head_size), head_size)[None]
    attend = functools.partial(
        local_attention,
        normed=normed,
        wq=query_weight,
        wk=key_weight.T,
        wv=value_weight,
        scale=scale,
        head_size=head_size,
    )
    part = attend(0, 2)
    below, above, part = lax.optimization_barrier((below, above, part))
    more = second_stage(below, above, me % GROUP)
    query, num, den = attend(1, 2, earlier=part)
    candidates = jnp.stack([pooled, *mates, below, above, *more])
    candidates = candidates.reshape(candidates.shape[0] * blocks_dev, comp, width)
    slots = block_slots(neighbour_ball_list // blocks_dev, me, peers)
    chosen = (slots * blocks_dev + neighbour_ball_list % blocks_dev).reshape(-1)
    ball_out = finish(
        chosen,
        candidates,
        query,
        num,
        den,
        grouped,
        pooled_key_weight.T,
        pooled_value_weight,
        output_weight,
        feedforward_norm_gain[None],
        gate_weight,
        up_weight,
        down_weight,
        head_size,
    )
    returning = take_rows(ids, ball_out).reshape(peers, send_each, width)
    came_back = swap(returning).reshape(rows_dev, width)
    return take_rows(slot, came_back)


def solution(mesh):
    rows = P(("rep", "pts"), None)
    return jax.shard_map(
        on_device,
        mesh=mesh,
        in_specs=(rows, P(("rep", "pts")), rows) + (P(),) * 12,
        out_specs=rows,
        check_vma=False,
    )
```

```python
import functools
import math

import jax
import jax.numpy as jnp
from jax import lax
from jax.experimental import pallas as pl
from jax.experimental.pallas import tpu as pltpu
from jax.sharding import PartitionSpec as P

BALL = 256
POOL = 8
OWNERS = 4
GROUP = 4
LANES = 128
TILE = 512
DEPTH = 512
BALLS_STEP = 2
LOW = 64
LOG2E = math.log2(math.e)
F32 = jnp.float32
BF16 = jnp.bfloat16


def params(mebibytes=28):
    return pltpu.CompilerParams(vmem_limit_bytes=mebibytes * 1024 * 1024)


def dot(a, b):
    return jnp.dot(a, b, preferred_element_type=F32)


def dot_nt(a, b):
    return lax.dot_general(a, b, (((1,), (1,)), ((), ())), preferred_element_type=F32)


def whole(shape):
    return pl.BlockSpec(shape, lambda *_: (0,) * len(shape), pipeline_mode=pl.Buffered(1))


def kept(shape):
    return pl.BlockSpec(shape, lambda *_: (0,) * len(shape))


def row_blocks(rows, width):
    return pl.BlockSpec((rows, width), lambda i, *_: (i, 0))


def column_of(row):
    return jnp.broadcast_to(row, (LANES, LANES)).T


def picked_rows(pick_tile, rows, source_ref):
    count = source_ref.shape[0]
    total = None
    for start in range(0, count, DEPTH):
        pick = jnp.concatenate(
            [pick_tile(t) for t in range(start // LANES, (start + DEPTH) // LANES)], axis=1
        )
        part = dot(pick, source_ref[start : start + DEPTH, :])
        total = part if total is None else total + part
    return total


def by_lane_ids(ids_ref, first, rows):
    targets = (lax.broadcasted_iota(jnp.int32, (rows, LANES), 0) + first).astype(F32)
    return lambda t: jnp.where(ids_ref[t : t + 1, :] == targets, 1.0, 0.0).astype(BF16)


def by_row_ids(ids_ref, first, rows):
    wanted = jnp.concatenate(
        [column_of(ids_ref[pl.ds(first + u, 1), :]) for u in range(rows // LANES)], axis=0
    )
    lane = lax.broadcasted_iota(jnp.int32, (rows, LANES), 1).astype(F32)
    return lambda t: jnp.where(wanted - float(t * LANES) == lane, 1.0, 0.0).astype(BF16)


def send_kernel(send_each, me_ref, index_ref, points_ref, out_ref, slot_ref, held, aux, arrivals):
    rows_dev, width = held.shape
    tiles = rows_dev // LANES
    chunks = width // LANES
    per_tile = LANES // send_each
    peers = rows_dev // send_each
    step = pl.program_id(0)
    pieces = [
        pltpu.make_async_copy(points_ref.at[pl.ds(k, DEPTH)], held.at[pl.ds(k, DEPTH)], arrivals.at[k // DEPTH])
        for k in range(0, rows_dev, DEPTH)
    ]

    @pl.when(step == 0)
    def _():
        for piece in pieces:
            piece.start()
        index = index_ref[...].astype(F32)
        dest = jnp.floor(index * (1.0 / rows_dev))
        local = index - dest * rows_dev
        high = jnp.floor(local * (1.0 / LOW))
        low = local - high * LOW
        row = lax.broadcasted_iota(jnp.int32, (LANES, LANES), 0)
        for t in range(tiles):
            pair = jnp.where(row == 0, high[t : t + 1, :], jnp.where(row == 1, low[t : t + 1, :], 0.0))
            aux[t * LANES : (t + 1) * LANES, :] = pair.T.astype(BF16)
        peer = lax.broadcasted_iota(jnp.int32, (peers, LANES), 0).astype(F32)
        member = [jnp.where(dest[t : t + 1, :] == peer, 1.0, 0.0) for t in range(tiles)]
        lane = lax.broadcasted_iota(jnp.int32, (LANES, LANES), 1)
        up_to = jnp.where(row <= lane, 1.0, 0.0).astype(BF16)
        counts = dot(jnp.concatenate(member, axis=0).astype(BF16), up_to)
        before = peer[:, 0:1] * send_each - 1.0
        for t in range(tiles):
            count = counts[t * peers : (t + 1) * peers, :]
            slot_ref[t : t + 1, :] = jnp.sum(member[t] * (count + before), axis=0, keepdims=True)
            before = before + count[:, LANES - 1 :]
        for piece in pieces:
            piece.wait()

    tile = by_lane_ids(slot_ref, step * TILE, TILE)
    rows = picked_rows(tile, TILE, held).astype(BF16)
    ids = picked_rows(tile, TILE, aux)
    for u in range(TILE // LANES):
        both = ids[u * LANES : (u + 1) * LANES, :].T[0:16, :]
        for v in range(per_tile):
            peer = u * per_tile + v
            mine = both
            if per_tile > 1:
                lane = lax.broadcasted_iota(jnp.int32, both.shape, 1)
                mine = jnp.where(lane // send_each == v, both, 0.0)
                mine = pltpu.roll(mine, (me_ref[0] - v + per_tile) % per_tile * send_each, 1)
            out_ref[peer, chunks * send_each :, :] = mine.astype(BF16)
            first = peer * send_each
            for c in range(chunks):
                out_ref[peer, c * send_each : (c + 1) * send_each, :] = rows[
                    first : first + send_each, c * LANES : (c + 1) * LANES
                ]


def send_order(points, index_tiles, me, peers):
    rows_dev, width = points.shape
    tiles = rows_dev // LANES
    send_each = rows_dev // peers
    payload = width // LANES * send_each + 16
    return pl.pallas_call(
        functools.partial(send_kernel, send_each),
        grid_spec=pltpu.PrefetchScalarGridSpec(
            num_scalar_prefetch=1,
            grid=(rows_dev // TILE,),
            in_specs=[whole((tiles, LANES)), pl.BlockSpec(memory_space=pl.ANY)],
            out_specs=[
                pl.BlockSpec((TILE // send_each, payload, LANES), lambda i, *_: (i, 0, 0)),
                kept((tiles, LANES)),
            ],
            scratch_shapes=[
                pltpu.VMEM((rows_dev, width), BF16),
                pltpu.VMEM((rows_dev, LANES), BF16),
                pltpu.SemaphoreType.DMA((rows_dev // DEPTH,)),
            ],
        ),
        out_shape=[
            jax.ShapeDtypeStruct((peers, payload, LANES), BF16),
            jax.ShapeDtypeStruct((tiles, LANES), F32),
        ],
        compiler_params=params(60),
        cost_estimate=pl.CostEstimate(
            flops=2 * rows_dev * rows_dev * (width + LANES), bytes_accessed=4 * rows_dev * width, transcendentals=0
        ),
        name="send_order",
    )(me.reshape(1), index_tiles, points)


def normed_rows(rows32, gain):
    mean_square = jnp.mean(rows32 * rows32, axis=-1, keepdims=True)
    return (rows32 * lax.rsqrt(mean_square + 1e-05) * gain).astype(BF16)


def pool_kernel(arrived_ref, gain_ref, source_ref, ids_ref, pooled_ref, ids, total):
    peers = arrived_ref.shape[0]
    rows, width = source_ref.shape
    chunks = width // LANES
    send_each = rows // peers
    per_tile = LANES // send_each
    step = pl.program_id(0)

    @pl.when(step == 0)
    def _():
        total[...] = jnp.zeros_like(total)

    for t in range(rows // LANES):
        row = jnp.zeros((1, LANES), F32)
        for p in range(t * per_tile, (t + 1) * per_tile):
            both = arrived_ref[p, chunks * send_each :, :].astype(F32)
            row = row + both[0:1, :] * LOW + both[1:2, :]
        ids[t : t + 1, :] = row
        ids_ref[pl.ds(step * (rows // LANES) + t, 1), :] = row
    for p in range(peers):
        for c in range(chunks):
            source_ref[p * send_each : (p + 1) * send_each, c * LANES : (c + 1) * LANES] = arrived_ref[
                p, c * send_each : (c + 1) * send_each, :
            ]
    normed = normed_rows(source_ref[...].astype(F32), gain_ref[...])
    pools = total.shape[0]
    pool = lax.broadcasted_iota(jnp.int32, (pools, LANES), 0).astype(F32)
    pick = jnp.concatenate(
        [
            jnp.where(jnp.floor(ids[t : t + 1, :] * (1.0 / POOL)) == pool, 1.0 / POOL, 0.0).astype(BF16)
            for t in range(rows // LANES)
        ],
        axis=1,
    )
    total[...] += dot(pick, normed)

    @pl.when(step == pl.num_programs(0) - 1)
    def _():
        pooled_ref[...] = total[...].astype(BF16)


def pool(arrived, gain, rows_dev):
    width = gain.shape[1]
    tiles = rows_dev // LANES
    peers, payload, _ = arrived.shape
    steps = rows_dev // TILE
    pooled = (rows_dev // POOL, width)
    return pl.pallas_call(
        pool_kernel,
        grid=(steps,),
        in_specs=[
            pl.BlockSpec((peers // steps, payload, LANES), lambda i: (i, 0, 0)),
            whole((1, width)),
        ],
        out_specs=[row_blocks(TILE, width), kept((tiles, LANES)), kept(pooled)],
        out_shape=[
            jax.ShapeDtypeStruct((rows_dev, width), BF16),
            jax.ShapeDtypeStruct((tiles, LANES), F32),
            jax.ShapeDtypeStruct(pooled, BF16),
        ],
        scratch_shapes=[pltpu.VMEM((TILE // LANES, LANES), F32), pltpu.VMEM(pooled, F32)],
        compiler_params=params(),
        cost_estimate=pl.CostEstimate(
            flops=rows_dev * rows_dev * width // 4, bytes_accessed=4 * rows_dev * width, transcendentals=0
        ),
        name="pool_arrived",
    )(arrived, gain)


def group_kernel(ids_ref, source_ref, gain_ref, grouped_ref, normed_ref):
    tile = by_lane_ids(ids_ref, pl.program_id(0) * TILE, TILE)
    grouped = picked_rows(tile, TILE, source_ref)
    grouped_ref[...] = grouped.astype(BF16)
    normed_ref[...] = normed_rows(grouped, gain_ref[...])


def group(ids, source, gain):
    rows_dev, width = source.shape
    rows = row_blocks(TILE, width)
    return pl.pallas_call(
        group_kernel,
        grid=(rows_dev // TILE,),
        in_specs=[whole(ids.shape), whole(source.shape), whole((1, width))],
        out_specs=[rows, rows],
        out_shape=[jax.ShapeDtypeStruct((rows_dev, width), BF16)] * 2,
        compiler_params=params(),
        cost_estimate=pl.CostEstimate(
            flops=2 * rows_dev * rows_dev * width, bytes_accessed=6 * rows_dev * width, transcendentals=0
        ),
        name="group_balls",
    )(ids, source, gain)


def block_matrix(rows, row_step, cols, col_step, value):
    row = lax.broadcasted_iota(jnp.int32, (rows, cols), 0) // row_step
    col = lax.broadcasted_iota(jnp.int32, (rows, cols), 1) // col_step
    return jnp.where(row == col, value, 0.0).astype(BF16)


def clear_spread(head_size, keys_ref, values_ref):
    keys_ref[...] = jnp.zeros_like(keys_ref)
    ones = block_matrix(values_ref.shape[1], values_ref.shape[1] * head_size // LANES, LANES, head_size, 1.0)
    for g in range(values_ref.shape[0]):
        values_ref[g, :, LANES:] = ones


def spread_keys(head_size, columns, ref):
    count = columns.shape[1]
    per_group = LANES // head_size
    for h in range(columns.shape[0] // head_size):
        g, j = h // per_group, h % per_group
        part = columns[h * head_size : (h + 1) * head_size, :]
        root = lax.rsqrt(jnp.mean(part * part, axis=0, keepdims=True) + 1e-06)
        ref[g, j * head_size : (j + 1) * head_size, j * count : (j + 1) * count] = (part * root).astype(BF16)


def spread_values(head_size, values, ref):
    count, width = values.shape
    head = lax.broadcasted_iota(jnp.int32, (count, LANES), 1) // head_size
    for g in range(width // LANES):
        lanes = values[:, g * LANES : (g + 1) * LANES]
        for j in range(LANES // head_size):
            ref[g, j * count : (j + 1) * count, :LANES] = jnp.where(head == j, lanes, jnp.zeros((), BF16))


def local_kernel(head_size, scale_ref, normed_ref, wq_ref, wk_ref, wv_ref, *rest):
    query_ref, num_ref, den_ref, mean_of, keys, values, weights = rest[-7:]
    width = normed_ref.shape[1]
    half = mean_of.shape[0]

    @pl.when(pl.program_id(0) == 0)
    def _():
        mean_of[...] = block_matrix(half, head_size, half, head_size, 1.0 / head_size)
        clear_spread(head_size, keys, values)

    normed = normed_ref[...]
    query = dot(normed, wq_ref[...])
    square = query * query
    high = square.astype(BF16)
    low = (square - high.astype(F32)).astype(BF16)
    mean_square = jnp.concatenate(
        [
            dot(high[:, c : c + half], mean_of[...]) + dot(low[:, c : c + half], mean_of[...])
            for c in range(0, width, half)
        ],
        axis=1,
    )
    query = (query * lax.rsqrt(mean_square + 1e-06) * scale_ref[...]).astype(BF16)
    query_ref[...] = query
    spread_keys(head_size, dot_nt(wk_ref[...], normed), keys)
    spread_values(head_size, dot(normed, wv_ref[...]).astype(BF16), values)
    groups = width // LANES
    for g in range(groups):
        weights[g] = jnp.exp2(dot(query[:, g * LANES : (g + 1) * LANES], keys[g])).astype(BF16)
    for g in range(groups):
        both = dot(weights[g], values[g])
        num_ref[:, g * LANES : (g + 1) * LANES] = both[:, :LANES].astype(BF16)
        den_ref[:, g * LANES : (g + 1) * LANES] = both[:, LANES:].astype(BF16)


def local_attention(part, parts, normed, wq, wk, wv, scale, head_size, earlier=()):
    rows_dev, width = normed.shape
    square = whole((width, width))
    groups = width // LANES
    spread = LANES // head_size * BALL
    steps = rows_dev // BALL // parts
    rows = pl.BlockSpec((BALL, width), lambda i: (part * steps + i, 0))
    return pl.pallas_call(
        functools.partial(local_kernel, head_size),
        grid=(steps,),
        in_specs=[whole((1, width)), rows, square, square, square]
        + [pl.BlockSpec(memory_space=pl.ANY)] * len(earlier),
        out_specs=[rows] * 3,
        out_shape=[
            jax.ShapeDtypeStruct((rows_dev, width), BF16),
            jax.ShapeDtypeStruct((rows_dev, width), BF16),
            jax.ShapeDtypeStruct((rows_dev, width), BF16),
        ],
        scratch_shapes=[
            pltpu.VMEM((2 * LANES, 2 * LANES), BF16),
            pltpu.VMEM((groups, LANES, spread), BF16),
            pltpu.VMEM((groups, spread, 2 * LANES), BF16),
            pltpu.VMEM((groups, BALL, spread), BF16),
        ],
        input_output_aliases={5 + k: k for k in range(len(earlier))},
        compiler_params=params(),
        cost_estimate=pl.CostEstimate(
            flops=20 * rows_dev * width * width // parts, bytes_accessed=12 * rows_dev * width // parts, transcendentals=0
        ),
        name="local_attention",
    )(scale, normed, wq, wk, wv, *earlier)


def finish_kernel(
    head_size,
    chosen_ref,
    candidates_ref,
    query_ref,
    num_ref,
    den_ref,
    grouped_ref,
    wpk_ref,
    wpv_ref,
    wo_ref,
    gain_ref,
    wg_ref,
    wu_ref,
    wd_ref,
    out_ref,
    keys,
    values,
    weights,
    attended,
):
    step = pl.program_id(0)
    groups = wo_ref.shape[0] // LANES
    far = OWNERS * BALL // POOL

    @pl.when(step == 0)
    def _():
        for b in range(BALLS_STEP):
            clear_spread(head_size, keys.at[b], values.at[b])

    first = step * BALLS_STEP * OWNERS
    coarse = jnp.concatenate(
        [candidates_ref[chosen_ref[first + o]] for o in range(BALLS_STEP * OWNERS)], axis=0
    )
    key_columns = dot_nt(wpk_ref[...], coarse)
    value_rows = dot(coarse, wpv_ref[...]).astype(BF16)
    for b in range(BALLS_STEP):
        spread_keys(head_size, key_columns[:, b * far : (b + 1) * far], keys.at[b])
        spread_values(head_size, value_rows[b * far : (b + 1) * far, :], values.at[b])
    for b in range(BALLS_STEP):
        rows = slice(b * BALL, (b + 1) * BALL)
        for g in range(groups):
            score = dot(query_ref[rows, g * LANES : (g + 1) * LANES], keys[b, g])
            weights[b, g] = jnp.exp2(score).astype(BF16)
    for b in range(BALLS_STEP):
        rows = slice(b * BALL, (b + 1) * BALL)
        for g in range(groups):
            lanes = slice(g * LANES, (g + 1) * LANES)
            both = dot(weights[b, g], values[b, g])
            num = both[:, :LANES] + num_ref[rows, lanes].astype(F32)
            den = both[:, LANES:] + den_ref[rows, lanes].astype(F32)
            attended[rows, lanes] = (num / den).astype(BF16)
    projected = dot(attended[...], wo_ref[...])
    residual = (grouped_ref[...].astype(F32) + projected).astype(BF16)
    rows32 = residual.astype(F32)
    ffn = normed_rows(rows32, gain_ref[...])
    gate = dot(ffn, wg_ref[...])
    up = dot(ffn, wu_ref[...])
    hidden = (0.5 * gate * (1.0 + jnp.tanh(0.5 * gate)) * up).astype(BF16)
    out_ref[...] = (rows32 + dot(hidden, wd_ref[...])).astype(BF16)


def finish(chosen, candidates, query, num, den, grouped, wpk, wpv, wo, gain, wg, wu, wd, head_size):
    rows_dev, width = grouped.shape
    hidden = wg.shape[1]
    groups = width // LANES
    step_rows = BALLS_STEP * BALL
    spread = LANES // head_size * OWNERS * BALL // POOL
    rows = row_blocks(step_rows, width)
    fixed = [wpk, wpv, wo, gain, wg, wu, wd]
    return pl.pallas_call(
        functools.partial(finish_kernel, head_size),
        grid_spec=pltpu.PrefetchScalarGridSpec(
            num_scalar_prefetch=1,
            grid=(rows_dev // step_rows,),
            in_specs=[whole(candidates.shape), rows, rows, rows, rows] + [whole(a.shape) for a in fixed],
            out_specs=rows,
            scratch_shapes=[
                pltpu.VMEM((BALLS_STEP, groups, LANES, spread), BF16),
                pltpu.VMEM((BALLS_STEP, groups, spread, 2 * LANES), BF16),
                pltpu.VMEM((BALLS_STEP, groups, BALL, spread), BF16),
                pltpu.VMEM((step_rows, width), BF16),
            ],
        ),
        out_shape=jax.ShapeDtypeStruct((rows_dev, width), BF16),
        compiler_params=params(),
        cost_estimate=pl.CostEstimate(
            flops=2 * rows_dev * width * (3 * hidden + 6 * width),
            bytes_accessed=12 * rows_dev * width,
            transcendentals=0,
        ),
        name="finish_balls",
    )(chosen, candidates, query, num, den, grouped, *fixed)


def rows_kernel(ids_ref, source_ref, out_ref):
    tile = by_row_ids(ids_ref, pl.program_id(0) * (TILE // LANES), TILE)
    out_ref[...] = picked_rows(tile, TILE, source_ref).astype(BF16)


def take_rows(ids, source):
    rows_dev, width = source.shape
    return pl.pallas_call(
        rows_kernel,
        grid=(rows_dev // TILE,),
        in_specs=[whole(ids.shape), whole(source.shape)],
        out_specs=row_blocks(TILE, width),
        out_shape=jax.ShapeDtypeStruct((rows_dev, width), BF16),
        compiler_params=params(),
        cost_estimate=pl.CostEstimate(
            flops=2 * rows_dev * rows_dev * width, bytes_accessed=4 * rows_dev * width, transcendentals=0
        ),
        name="take_rows",
    )(ids, source)


def route(block, target):
    devices = range(lax.axis_size("pts"))
    return lax.ppermute(block, "pts", [(i, target(i) % len(devices)) for i in devices])


def to_mate(block, mate):
    return route(block, lambda i: i ^ mate)


def wanted(below, above, place, mate):
    return jnp.where(place > (place ^ mate), below, above)


SLOT_INSIDE = (0, 5, 1, 6)
SLOT_BELOW = (2, 7, 4, 8)


def block_slots(owner, me, peers):
    mate = (owner % GROUP) ^ (me % GROUP)
    ahead = jnp.mod(owner // GROUP - me // GROUP, peers // GROUP)
    pick = lambda table: sum(jnp.where(mate == m, table[m], 0) for m in range(GROUP))
    outside = pick(SLOT_BELOW) + jnp.where((mate == 0) & (ahead == 1), 1, 0)
    return jnp.where(ahead == 0, pick(SLOT_INSIDE), outside)


def on_device(
    points,
    point_row_index,
    neighbour_ball_list,
    attention_norm_gain,
    query_weight,
    key_weight,
    value_weight,
    pooled_key_weight,
    pooled_value_weight,
    head_score_scale,
    output_weight,
    feedforward_norm_gain,
    gate_weight,
    up_weight,
    down_weight,
):
    rows_dev, width = points.shape
    head_size = width // head_score_scale.shape[0]
    peers = lax.axis_size("pts")
    me = lax.axis_index("pts")
    send_each = rows_dev // peers
    blocks_dev = rows_dev // BALL
    comp = BALL // POOL

    def swap(array):
        return lax.all_to_all(array, "pts", split_axis=0, concat_axis=0, tiled=True)

    outgoing, slot = send_order(points, point_row_index.reshape(rows_dev // LANES, LANES), me, peers)
    source, ids, pooled = pool(swap(outgoing), attention_norm_gain[None], rows_dev)
    below = route(pooled, lambda i: i + GROUP)
    above = route(pooled, lambda i: i - GROUP)
    beside = to_mate(pooled, 2)
    grouped, normed = group(ids, source, attention_norm_gain[None])
    scale = jnp.repeat(head_score_scale * (LOG2E / head_size), head_size)[None]
    attend = functools.partial(
        local_attention,
        normed=normed,
        wq=query_weight,
        wk=key_weight.T,
        wv=value_weight,
        scale=scale,
        head_size=head_size,
    )
    part = attend(0, 2)
    below, above, beside, part = lax.optimization_barrier((below, above, beside, part))
    place = me % GROUP
    second = to_mate(wanted(below, above, place, 2), 2)
    near = to_mate(jnp.stack([pooled, beside, wanted(below, above, place, 1)]), 1)
    query, num, den = attend(1, 2, earlier=part)
    second, query = lax.optimization_barrier((second, query))
    last = to_mate(second, 1)
    candidates = jnp.concatenate([jnp.stack([pooled, beside, below, above, second]), near, last[None]])
    candidates = candidates.reshape(candidates.shape[0] * blocks_dev, comp, width)
    slots = block_slots(neighbour_ball_list // blocks_dev, me, peers)
    chosen = (slots * blocks_dev + neighbour_ball_list % blocks_dev).reshape(-1)
    ball_out = finish(
        chosen,
        candidates,
        query,
        num,
        den,
        grouped,
        pooled_key_weight.T,
        pooled_value_weight,
        output_weight,
        feedforward_norm_gain[None],
        gate_weight,
        up_weight,
        down_weight,
        head_size,
    )
    returning = take_rows(ids, ball_out).reshape(peers, send_each, width)
    came_back = swap(returning).reshape(rows_dev, width)
    return take_rows(slot, came_back)


def solution(mesh):
    rows = P(("rep", "pts"), None)
    return jax.shard_map(
        on_device,
        mesh=mesh,
        in_specs=(rows, P(("rep", "pts")), rows) + (P(),) * 12,
        out_specs=rows,
        check_vma=False,
    )
```

```python
import functools
import math

import jax
import jax.numpy as jnp
from jax import lax
from jax.experimental import pallas as pl
from jax.experimental.pallas import tpu as pltpu
from jax.sharding import PartitionSpec as P

BALL = 256
POOL = 8
OWNERS = 4
GROUP = 4
LANES = 128
TILE = 512
DEPTH = 512
BALLS_STEP = 2
LOW = 64
SEND_PITCH = 8
SEND_STEPS = 2
TAKE_STEPS = 2
LOG2E = math.log2(math.e)
F32 = jnp.float32
BF16 = jnp.bfloat16


def params(mebibytes=28):
    return pltpu.CompilerParams(vmem_limit_bytes=mebibytes * 1024 * 1024)


def dot(a, b):
    return jnp.dot(a, b, preferred_element_type=F32)


def dot_nt(a, b):
    return lax.dot_general(a, b, (((1,), (1,)), ((), ())), preferred_element_type=F32)


def whole(shape):
    return pl.BlockSpec(shape, lambda *_: (0,) * len(shape), pipeline_mode=pl.Buffered(1))


def kept(shape):
    return pl.BlockSpec(shape, lambda *_: (0,) * len(shape))


def row_blocks(rows, width):
    return pl.BlockSpec((rows, width), lambda i, *_: (i, 0))


def picked_rows(pick_tile, rows, source_ref):
    count = source_ref.shape[0]
    total = None
    for start in range(0, count, DEPTH):
        pick = jnp.concatenate(
            [pick_tile(t) for t in range(start // LANES, (start + DEPTH) // LANES)], axis=1
        )
        part = dot(pick, source_ref[start : start + DEPTH, :])
        total = part if total is None else total + part
    return total


def by_lane_ids(ids_ref, first, rows):
    targets = (lax.broadcasted_iota(jnp.int32, (rows, LANES), 0) + first).astype(F32)
    return lambda t: jnp.where(ids_ref[t : t + 1, :] == targets, 1.0, 0.0).astype(BF16)


def chunk_rows(ref, first, rows, chunk, pitch):
    return ref.at[pl.ds(first * pitch + chunk, rows, stride=pitch), :]


def gather_rows(places_ref, first_tile, tiles, source, target, pitch):
    def move(t, carry):
        places = [places_ref[first_tile + t, l] for l in range(LANES)]
        rows = [source[pl.ds(pl.multiple_of(p, pitch), pitch), :] for p in places]
        for l in range(LANES):
            target[pl.ds(pl.multiple_of((t * LANES + l) * pitch, pitch), pitch), :] = rows[l]
        return carry

    lax.fori_loop(0, tiles, move, 0)


def scatter_rows(places_ref, tiles, source, target, pitch):
    def move(t, carry):
        places = [places_ref[t, l] for l in range(LANES)]
        rows = [
            source[pl.ds(pl.multiple_of((t * LANES + l) * pitch, pitch), pitch), :] for l in range(LANES)
        ]
        for l in range(LANES):
            target[pl.ds(pl.multiple_of(places[l], pitch), pitch), :] = rows[l]
        return carry

    lax.fori_loop(0, tiles, move, 0)


def send_kernel(send_each, me_ref, index_ref, points_ref, out_ref, slot_ref, held, rows, sent, places, places_smem, arrivals, moved):
    rows_dev, width = held.shape
    tiles = rows_dev // LANES
    chunks = width // LANES
    per_tile = LANES // send_each
    peers = rows_dev // send_each
    step_peers = out_ref.shape[0]
    step = pl.program_id(0)

    @pl.when(step == 0)
    def _():
        pieces = [
            pltpu.make_async_copy(points_ref.at[pl.ds(k, DEPTH)], held.at[pl.ds(k, DEPTH)], arrivals.at[k // DEPTH])
            for k in range(0, rows_dev, DEPTH)
        ]
        for piece in pieces:
            piece.start()
        index = index_ref[...].astype(F32)
        dest = jnp.floor(index * (1.0 / rows_dev))
        local = index - dest * rows_dev
        high = jnp.floor(local * (1.0 / LOW))
        low = local - high * LOW
        row = lax.broadcasted_iota(jnp.int32, (LANES, LANES), 0)
        lane = lax.broadcasted_iota(jnp.int32, (LANES, LANES), 1)
        peer = lax.broadcasted_iota(jnp.int32, (peers, LANES), 0).astype(F32)
        member = [jnp.where(dest[t : t + 1, :] == peer, 1.0, 0.0) for t in range(tiles)]
        up_to = jnp.where(row <= lane, 1.0, 0.0).astype(BF16)
        counts = dot(jnp.concatenate(member, axis=0).astype(BF16), up_to)
        before = peer[:, 0:1] * send_each - 1.0
        for t in range(tiles):
            count = counts[t * peers : (t + 1) * peers, :]
            slot = jnp.sum(member[t] * (count + before), axis=0, keepdims=True)
            places[t : t + 1, :] = (slot * SEND_PITCH).astype(jnp.int32)
            slot_ref[t : t + 1, :] = (slot * chunks).astype(jnp.int32)
            before = before + count[:, LANES - 1 :]
        move = pltpu.make_async_copy(places, places_smem, moved.at[0])
        move.start()
        for t in range(tiles):
            pair = jnp.where(row == 0, high[t : t + 1, :], jnp.where(row == 1, low[t : t + 1, :], 0.0))
            chunk_rows(rows, t * LANES, LANES, chunks, SEND_PITCH)[...] = pair.T
        for k, piece in enumerate(pieces):
            piece.wait()
            for c in range(chunks):
                part = held[k * DEPTH : (k + 1) * DEPTH, c * LANES : (c + 1) * LANES]
                chunk_rows(rows, k * DEPTH, DEPTH, c, SEND_PITCH)[...] = part.astype(F32)
        move.wait()
        scatter_rows(places_smem, tiles, rows, sent, SEND_PITCH)

    base = step * (step_peers * send_each)
    for peer in range(step_peers):
        for c in range(chunks):
            part = chunk_rows(sent, base + peer * send_each, send_each, c, SEND_PITCH)[...]
            out_ref[peer, c * send_each : (c + 1) * send_each, :] = part.astype(BF16)
    for t in range(step_peers // per_tile):
        both = chunk_rows(sent, base + t * LANES, LANES, chunks, SEND_PITCH)[...].T[0:16, :]
        for v in range(per_tile):
            mine = both
            if per_tile > 1:
                lane = lax.broadcasted_iota(jnp.int32, both.shape, 1)
                mine = jnp.where(lane // send_each == v, both, 0.0)
                mine = pltpu.roll(mine, (me_ref[0] - v + per_tile) % per_tile * send_each, 1)
            out_ref[t * per_tile + v, chunks * send_each :, :] = mine.astype(BF16)


def send_order(points, index_tiles, me, peers):
    rows_dev, width = points.shape
    tiles = rows_dev // LANES
    send_each = rows_dev // peers
    payload = width // LANES * send_each + 16
    return pl.pallas_call(
        functools.partial(send_kernel, send_each),
        grid_spec=pltpu.PrefetchScalarGridSpec(
            num_scalar_prefetch=1,
            grid=(SEND_STEPS,),
            in_specs=[whole((tiles, LANES)), pl.BlockSpec(memory_space=pl.ANY)],
            out_specs=[
                pl.BlockSpec((peers // SEND_STEPS, payload, LANES), lambda i, *_: (i, 0, 0)),
                kept((tiles, LANES)),
            ],
            scratch_shapes=[
                pltpu.VMEM((rows_dev, width), BF16),
                pltpu.VMEM((rows_dev * SEND_PITCH, LANES), F32),
                pltpu.VMEM((rows_dev * SEND_PITCH, LANES), F32),
                pltpu.VMEM((tiles, LANES), jnp.int32),
                pltpu.SMEM((tiles, LANES), jnp.int32),
                pltpu.SemaphoreType.DMA((rows_dev // DEPTH,)),
                pltpu.SemaphoreType.DMA((1,)),
            ],
        ),
        out_shape=[
            jax.ShapeDtypeStruct((peers, payload, LANES), BF16),
            jax.ShapeDtypeStruct((tiles, LANES), jnp.int32),
        ],
        compiler_params=params(60),
        cost_estimate=pl.CostEstimate(
            flops=2 * rows_dev * rows_dev * width, bytes_accessed=4 * rows_dev * width, transcendentals=0
        ),
        name="send_order",
    )(me.reshape(1), index_tiles, points)


def normed_rows(rows32, gain):
    mean_square = jnp.mean(rows32 * rows32, axis=-1, keepdims=True)
    return (rows32 * lax.rsqrt(mean_square + 1e-05) * gain).astype(BF16)


def pool_kernel(arrived_ref, gain_ref, source_ref, ids_ref, places_ref, pooled_ref, ids, total):
    peers = arrived_ref.shape[0]
    rows, width = source_ref.shape
    chunks = width // LANES
    send_each = rows // peers
    per_tile = LANES // send_each
    step = pl.program_id(0)

    @pl.when(step == 0)
    def _():
        total[...] = jnp.zeros_like(total)

    for t in range(rows // LANES):
        row = jnp.zeros((1, LANES), F32)
        for p in range(t * per_tile, (t + 1) * per_tile):
            both = arrived_ref[p, chunks * send_each :, :].astype(F32)
            row = row + both[0:1, :] * LOW + both[1:2, :]
        ids[t : t + 1, :] = row
        ids_ref[pl.ds(step * (rows // LANES) + t, 1), :] = row
        places_ref[pl.ds(step * (rows // LANES) + t, 1), :] = (row * chunks).astype(jnp.int32)
    for p in range(peers):
        for c in range(chunks):
            source_ref[p * send_each : (p + 1) * send_each, c * LANES : (c + 1) * LANES] = arrived_ref[
                p, c * send_each : (c + 1) * send_each, :
            ]
    normed = normed_rows(source_ref[...].astype(F32), gain_ref[...])
    pools = total.shape[0]
    pool = lax.broadcasted_iota(jnp.int32, (pools, LANES), 0).astype(F32)
    pick = jnp.concatenate(
        [
            jnp.where(jnp.floor(ids[t : t + 1, :] * (1.0 / POOL)) == pool, 1.0 / POOL, 0.0).astype(BF16)
            for t in range(rows // LANES)
        ],
        axis=1,
    )
    total[...] += dot(pick, normed)

    @pl.when(step == pl.num_programs(0) - 1)
    def _():
        pooled_ref[...] = total[...].astype(BF16)


def pool(arrived, gain, rows_dev):
    width = gain.shape[1]
    tiles = rows_dev // LANES
    peers, payload, _ = arrived.shape
    steps = rows_dev // TILE
    pooled = (rows_dev // POOL, width)
    return pl.pallas_call(
        pool_kernel,
        grid=(steps,),
        in_specs=[
            pl.BlockSpec((peers // steps, payload, LANES), lambda i: (i, 0, 0)),
            whole((1, width)),
        ],
        out_specs=[row_blocks(TILE, width), kept((tiles, LANES)), kept((tiles, LANES)), kept(pooled)],
        out_shape=[
            jax.ShapeDtypeStruct((rows_dev, width), BF16),
            jax.ShapeDtypeStruct((tiles, LANES), F32),
            jax.ShapeDtypeStruct((tiles, LANES), jnp.int32),
            jax.ShapeDtypeStruct(pooled, BF16),
        ],
        scratch_shapes=[pltpu.VMEM((TILE // LANES, LANES), F32), pltpu.VMEM(pooled, F32)],
        compiler_params=params(),
        cost_estimate=pl.CostEstimate(
            flops=rows_dev * rows_dev * width // 4, bytes_accessed=4 * rows_dev * width, transcendentals=0
        ),
        name="pool_arrived",
    )(arrived, gain)


def group_kernel(ids_ref, source_ref, gain_ref, grouped_ref, normed_ref):
    tile = by_lane_ids(ids_ref, pl.program_id(0) * TILE, TILE)
    grouped = picked_rows(tile, TILE, source_ref)
    grouped_ref[...] = grouped.astype(BF16)
    normed_ref[...] = normed_rows(grouped, gain_ref[...])


def group(ids, source, gain):
    rows_dev, width = source.shape
    rows = row_blocks(TILE, width)
    return pl.pallas_call(
        group_kernel,
        grid=(rows_dev // TILE,),
        in_specs=[whole(ids.shape), whole(source.shape), whole((1, width))],
        out_specs=[rows, rows],
        out_shape=[jax.ShapeDtypeStruct((rows_dev, width), BF16)] * 2,
        compiler_params=params(),
        cost_estimate=pl.CostEstimate(
            flops=2 * rows_dev * rows_dev * width, bytes_accessed=6 * rows_dev * width, transcendentals=0
        ),
        name="group_balls",
    )(ids, source, gain)


def block_matrix(rows, row_step, cols, col_step, value):
    row = lax.broadcasted_iota(jnp.int32, (rows, cols), 0) // row_step
    col = lax.broadcasted_iota(jnp.int32, (rows, cols), 1) // col_step
    return jnp.where(row == col, value, 0.0).astype(BF16)


def clear_spread(head_size, keys_ref, values_ref):
    keys_ref[...] = jnp.zeros_like(keys_ref)
    ones = block_matrix(values_ref.shape[1], values_ref.shape[1] * head_size // LANES, LANES, head_size, 1.0)
    for g in range(values_ref.shape[0]):
        values_ref[g, :, LANES:] = ones


def spread_keys(head_size, columns, ref):
    count = columns.shape[1]
    per_group = LANES // head_size
    for h in range(columns.shape[0] // head_size):
        g, j = h // per_group, h % per_group
        part = columns[h * head_size : (h + 1) * head_size, :]
        root = lax.rsqrt(jnp.mean(part * part, axis=0, keepdims=True) + 1e-06)
        ref[g, j * head_size : (j + 1) * head_size, j * count : (j + 1) * count] = (part * root).astype(BF16)


def spread_values(head_size, values, ref):
    count, width = values.shape
    head = lax.broadcasted_iota(jnp.int32, (count, LANES), 1) // head_size
    for g in range(width // LANES):
        lanes = values[:, g * LANES : (g + 1) * LANES]
        for j in range(LANES // head_size):
            ref[g, j * count : (j + 1) * count, :LANES] = jnp.where(head == j, lanes, jnp.zeros((), BF16))


def local_kernel(head_size, scale_ref, normed_ref, wq_ref, wk_ref, wv_ref, *rest):
    query_ref, num_ref, den_ref, mean_of, keys, values, weights = rest[-7:]
    width = normed_ref.shape[1]
    half = mean_of.shape[0]

    @pl.when(pl.program_id(0) == 0)
    def _():
        mean_of[...] = block_matrix(half, head_size, half, head_size, 1.0 / head_size)
        clear_spread(head_size, keys, values)

    normed = normed_ref[...]
    query = dot(normed, wq_ref[...])
    square = query * query
    high = square.astype(BF16)
    low = (square - high.astype(F32)).astype(BF16)
    mean_square = jnp.concatenate(
        [
            dot(high[:, c : c + half], mean_of[...]) + dot(low[:, c : c + half], mean_of[...])
            for c in range(0, width, half)
        ],
        axis=1,
    )
    query = (query * lax.rsqrt(mean_square + 1e-06) * scale_ref[...]).astype(BF16)
    query_ref[...] = query
    spread_keys(head_size, dot_nt(wk_ref[...], normed), keys)
    spread_values(head_size, dot(normed, wv_ref[...]).astype(BF16), values)
    groups = width // LANES
    for g in range(groups):
        weights[g] = jnp.exp2(dot(query[:, g * LANES : (g + 1) * LANES], keys[g])).astype(BF16)
    for g in range(groups):
        both = dot(weights[g], values[g])
        num_ref[:, g * LANES : (g + 1) * LANES] = both[:, :LANES].astype(BF16)
        den_ref[:, g * LANES : (g + 1) * LANES] = both[:, LANES:].astype(BF16)


def local_attention(part, parts, normed, wq, wk, wv, scale, head_size, earlier=()):
    rows_dev, width = normed.shape
    square = whole((width, width))
    groups = width // LANES
    spread = LANES // head_size * BALL
    steps = rows_dev // BALL // parts
    rows = pl.BlockSpec((BALL, width), lambda i: (part * steps + i, 0))
    return pl.pallas_call(
        functools.partial(local_kernel, head_size),
        grid=(steps,),
        in_specs=[whole((1, width)), rows, square, square, square]
        + [pl.BlockSpec(memory_space=pl.ANY)] * len(earlier),
        out_specs=[rows] * 3,
        out_shape=[
            jax.ShapeDtypeStruct((rows_dev, width), BF16),
            jax.ShapeDtypeStruct((rows_dev, width), BF16),
            jax.ShapeDtypeStruct((rows_dev, width), BF16),
        ],
        scratch_shapes=[
            pltpu.VMEM((2 * LANES, 2 * LANES), BF16),
            pltpu.VMEM((groups, LANES, spread), BF16),
            pltpu.VMEM((groups, spread, 2 * LANES), BF16),
            pltpu.VMEM((groups, BALL, spread), BF16),
        ],
        input_output_aliases={5 + k: k for k in range(len(earlier))},
        compiler_params=params(),
        cost_estimate=pl.CostEstimate(
            flops=20 * rows_dev * width * width // parts, bytes_accessed=12 * rows_dev * width // parts, transcendentals=0
        ),
        name="local_attention",
    )(scale, normed, wq, wk, wv, *earlier)


def finish_kernel(
    head_size,
    chosen_ref,
    places_ref,
    candidates_ref,
    query_ref,
    num_ref,
    den_ref,
    grouped_ref,
    wpk_ref,
    wpv_ref,
    wo_ref,
    gain_ref,
    wg_ref,
    wu_ref,
    wd_ref,
    out_ref,
    keys,
    values,
    weights,
    attended,
    rows,
    taken,
):
    step = pl.program_id(0)
    steps = pl.num_programs(0) - TAKE_STEPS
    step_rows, width = attended.shape
    chunks = width // LANES

    @pl.when(step < steps)
    def _():
        result = balls_step(
            head_size, step, chosen_ref, candidates_ref, query_ref, num_ref, den_ref, grouped_ref, wpk_ref,
            wpv_ref, wo_ref, gain_ref, wg_ref, wu_ref, wd_ref, keys, values, weights, attended,
        )
        for c in range(chunks):
            part = result[:, c * LANES : (c + 1) * LANES].astype(BF16).astype(F32)
            chunk_rows(rows, step * step_rows, step_rows, c, chunks)[...] = part

    @pl.when(step >= steps)
    def _():
        take_block(places_ref, step - steps, rows, taken, out_ref)


def take_block(places_ref, block, rows, taken, out_ref):
    count, width = out_ref.shape
    chunks = width // LANES
    gather_rows(places_ref, block * (count // LANES), count // LANES, rows, taken, chunks)
    for c in range(chunks):
        out_ref[:, c * LANES : (c + 1) * LANES] = chunk_rows(taken, 0, count, c, chunks)[...].astype(BF16)


def balls_step(
    head_size,
    step,
    chosen_ref,
    candidates_ref,
    query_ref,
    num_ref,
    den_ref,
    grouped_ref,
    wpk_ref,
    wpv_ref,
    wo_ref,
    gain_ref,
    wg_ref,
    wu_ref,
    wd_ref,
    keys,
    values,
    weights,
    attended,
):
    groups = wo_ref.shape[0] // LANES
    far = OWNERS * BALL // POOL

    @pl.when(step == 0)
    def _():
        for b in range(BALLS_STEP):
            clear_spread(head_size, keys.at[b], values.at[b])

    first = step * BALLS_STEP * OWNERS
    coarse = jnp.concatenate(
        [candidates_ref[chosen_ref[first + o]] for o in range(BALLS_STEP * OWNERS)], axis=0
    )
    key_columns = dot_nt(wpk_ref[...], coarse)
    value_rows = dot(coarse, wpv_ref[...]).astype(BF16)
    for b in range(BALLS_STEP):
        spread_keys(head_size, key_columns[:, b * far : (b + 1) * far], keys.at[b])
        spread_values(head_size, value_rows[b * far : (b + 1) * far, :], values.at[b])
    for b in range(BALLS_STEP):
        rows = slice(b * BALL, (b + 1) * BALL)
        for g in range(groups):
            score = dot(query_ref[rows, g * LANES : (g + 1) * LANES], keys[b, g])
            weights[b, g] = jnp.exp2(score).astype(BF16)
    for b in range(BALLS_STEP):
        rows = slice(b * BALL, (b + 1) * BALL)
        for g in range(groups):
            lanes = slice(g * LANES, (g + 1) * LANES)
            both = dot(weights[b, g], values[b, g])
            num = both[:, :LANES] + num_ref[rows, lanes].astype(F32)
            den = both[:, LANES:] + den_ref[rows, lanes].astype(F32)
            attended[rows, lanes] = (num / den).astype(BF16)
    projected = dot(attended[...], wo_ref[...])
    residual = (grouped_ref[...].astype(F32) + projected).astype(BF16)
    rows32 = residual.astype(F32)
    ffn = normed_rows(rows32, gain_ref[...])
    gate = dot(ffn, wg_ref[...])
    up = dot(ffn, wu_ref[...])
    hidden = (0.5 * gate * (1.0 + jnp.tanh(0.5 * gate)) * up).astype(BF16)
    return rows32 + dot(hidden, wd_ref[...])


def finish(chosen, places, candidates, query, num, den, grouped, wpk, wpv, wo, gain, wg, wu, wd, head_size):
    rows_dev, width = grouped.shape
    hidden = wg.shape[1]
    groups = width // LANES
    step_rows = BALLS_STEP * BALL
    spread = LANES // head_size * OWNERS * BALL // POOL
    steps = rows_dev // step_rows
    rows = pl.BlockSpec((step_rows, width), lambda i, *_: (jnp.minimum(i, steps - 1), 0))
    take_rows = rows_dev // TAKE_STEPS
    fixed = [wpk, wpv, wo, gain, wg, wu, wd]
    return pl.pallas_call(
        functools.partial(finish_kernel, head_size),
        grid_spec=pltpu.PrefetchScalarGridSpec(
            num_scalar_prefetch=2,
            grid=(steps + TAKE_STEPS,),
            in_specs=[whole(candidates.shape), rows, rows, rows, rows] + [whole(a.shape) for a in fixed],
            out_specs=pl.BlockSpec((take_rows, width), lambda i, *_: (jnp.maximum(i - steps, 0), 0)),
            scratch_shapes=[
                pltpu.VMEM((BALLS_STEP, groups, LANES, spread), BF16),
                pltpu.VMEM((BALLS_STEP, groups, spread, 2 * LANES), BF16),
                pltpu.VMEM((BALLS_STEP, groups, BALL, spread), BF16),
                pltpu.VMEM((step_rows, width), BF16),
                pltpu.VMEM((rows_dev * (width // LANES), LANES), F32),
                pltpu.VMEM((take_rows * (width // LANES), LANES), F32),
            ],
        ),
        out_shape=jax.ShapeDtypeStruct((rows_dev, width), BF16),
        compiler_params=params(),
        cost_estimate=pl.CostEstimate(
            flops=2 * rows_dev * width * (3 * hidden + 6 * width),
            bytes_accessed=12 * rows_dev * width,
            transcendentals=0,
        ),
        name="finish_balls",
    )(chosen, places, candidates, query, num, den, grouped, *fixed)


def take_kernel(places_ref, source_ref, out_ref, rows, taken):
    count, width = source_ref.shape
    chunks = width // LANES

    @pl.when(pl.program_id(0) == 0)
    def _():
        for first in range(0, count, DEPTH):
            for c in range(chunks):
                part = source_ref[first : first + DEPTH, c * LANES : (c + 1) * LANES]
                chunk_rows(rows, first, DEPTH, c, chunks)[...] = part.astype(F32)

    take_block(places_ref, pl.program_id(0), rows, taken, out_ref)


def take_rows(places, source):
    rows_dev, width = source.shape
    chunks = width // LANES
    return pl.pallas_call(
        take_kernel,
        grid_spec=pltpu.PrefetchScalarGridSpec(
            num_scalar_prefetch=1,
            grid=(rows_dev // TILE,),
            in_specs=[whole(source.shape)],
            out_specs=row_blocks(TILE, width),
            scratch_shapes=[
                pltpu.VMEM((rows_dev * chunks, LANES), F32),
                pltpu.VMEM((TILE * chunks, LANES), F32),
            ],
        ),
        out_shape=jax.ShapeDtypeStruct((rows_dev, width), BF16),
        compiler_params=params(),
        cost_estimate=pl.CostEstimate(
            flops=2 * rows_dev * rows_dev * width, bytes_accessed=4 * rows_dev * width, transcendentals=0
        ),
        name="take_rows",
    )(places, source)


def route(block, target):
    devices = range(lax.axis_size("pts"))
    return lax.ppermute(block, "pts", [(i, target(i) % len(devices)) for i in devices])


def to_mate(block, mate):
    return route(block, lambda i: i ^ mate)


def wanted(below, above, place, mate):
    return jnp.where(place > (place ^ mate), below, above)


SLOT_INSIDE = (0, 5, 1, 6)
SLOT_BELOW = (2, 7, 4, 8)


def block_slots(owner, me, peers):
    mate = (owner % GROUP) ^ (me % GROUP)
    ahead = jnp.mod(owner // GROUP - me // GROUP, peers // GROUP)
    pick = lambda table: sum(jnp.where(mate == m, table[m], 0) for m in range(GROUP))
    outside = pick(SLOT_BELOW) + jnp.where((mate == 0) & (ahead == 1), 1, 0)
    return jnp.where(ahead == 0, pick(SLOT_INSIDE), outside)


def on_device(
    points,
    point_row_index,
    neighbour_ball_list,
    attention_norm_gain,
    query_weight,
    key_weight,
    value_weight,
    pooled_key_weight,
    pooled_value_weight,
    head_score_scale,
    output_weight,
    feedforward_norm_gain,
    gate_weight,
    up_weight,
    down_weight,
):
    rows_dev, width = points.shape
    head_size = width // head_score_scale.shape[0]
    peers = lax.axis_size("pts")
    me = lax.axis_index("pts")
    send_each = rows_dev // peers
    blocks_dev = rows_dev // BALL
    comp = BALL // POOL

    def swap(array):
        return lax.all_to_all(array, "pts", split_axis=0, concat_axis=0, tiled=True)

    outgoing, slot = send_order(points, point_row_index.reshape(rows_dev // LANES, LANES), me, peers)
    source, ids, places, pooled = pool(swap(outgoing), attention_norm_gain[None], rows_dev)
    below = route(pooled, lambda i: i + GROUP)
    above = route(pooled, lambda i: i - GROUP)
    beside = to_mate(pooled, 2)
    grouped, normed = group(ids, source, attention_norm_gain[None])
    scale = jnp.repeat(head_score_scale * (LOG2E / head_size), head_size)[None]
    attend = functools.partial(
        local_attention,
        normed=normed,
        wq=query_weight,
        wk=key_weight.T,
        wv=value_weight,
        scale=scale,
        head_size=head_size,
    )
    part = attend(0, 2)
    below, above, beside, part = lax.optimization_barrier((below, above, beside, part))
    place = me % GROUP
    second = to_mate(wanted(below, above, place, 2), 2)
    near = to_mate(jnp.stack([pooled, beside, wanted(below, above, place, 1)]), 1)
    query, num, den = attend(1, 2, earlier=part)
    second, query = lax.optimization_barrier((second, query))
    last = to_mate(second, 1)
    candidates = jnp.concatenate([jnp.stack([pooled, beside, below, above, second]), near, last[None]])
    candidates = candidates.reshape(candidates.shape[0] * blocks_dev, comp, width)
    slots = block_slots(neighbour_ball_list // blocks_dev, me, peers)
    chosen = (slots * blocks_dev + neighbour_ball_list % blocks_dev).reshape(-1)
    returning = finish(
        chosen,
        places,
        candidates,
        query,
        num,
        den,
        grouped,
        pooled_key_weight.T,
        pooled_value_weight,
        output_weight,
        feedforward_norm_gain[None],
        gate_weight,
        up_weight,
        down_weight,
        head_size,
    )
    came_back = swap(returning.reshape(peers, send_each, width)).reshape(rows_dev, width)
    return take_rows(slot, came_back)


def solution(mesh):
    rows = P(("rep", "pts"), None)
    return jax.shard_map(
        on_device,
        mesh=mesh,
        in_specs=(rows, P(("rep", "pts")), rows) + (P(),) * 12,
        out_specs=rows,
        check_vma=False,
    )
```

```python
import functools
import math

import jax
import jax.numpy as jnp
from jax import lax
from jax.experimental import pallas as pl
from jax.experimental.pallas import tpu as pltpu
from jax.sharding import PartitionSpec as P

BALL = 256
POOL = 8
OWNERS = 4
GROUP = 4
LANES = 128
TILE = 512
DEPTH = 512
BALLS_STEP = 2
LOW = 64
SEND_PITCH = 8
SEND_STEPS = 2
TAKE_STEPS = 2
LOG2E = math.log2(math.e)
F32 = jnp.float32
BF16 = jnp.bfloat16


def params(mebibytes=28):
    return pltpu.CompilerParams(vmem_limit_bytes=mebibytes * 1024 * 1024)


def dot(a, b):
    return jnp.dot(a, b, preferred_element_type=F32)


def dot_nt(a, b):
    return lax.dot_general(a, b, (((1,), (1,)), ((), ())), preferred_element_type=F32)


def whole(shape):
    return pl.BlockSpec(shape, lambda *_: (0,) * len(shape), pipeline_mode=pl.Buffered(1))


def kept(shape):
    return pl.BlockSpec(shape, lambda *_: (0,) * len(shape))


def row_blocks(rows, width):
    return pl.BlockSpec((rows, width), lambda i, *_: (i, 0))


def chunk_rows(ref, first, rows, chunk, pitch):
    return ref.at[pl.ds(first * pitch + chunk, rows, stride=pitch), :]


def gather_rows(places_ref, first_tile, tiles, source, target, pitch):
    def move(t, carry):
        places = [places_ref[first_tile + t, l] for l in range(LANES)]
        rows = [source[pl.ds(pl.multiple_of(p, pitch), pitch), :] for p in places]
        for l in range(LANES):
            target[pl.ds(pl.multiple_of((t * LANES + l) * pitch, pitch), pitch), :] = rows[l]
        return carry

    lax.fori_loop(0, tiles, move, 0)


def scatter_rows(places_ref, tiles, source, target, pitch):
    def move(t, carry):
        places = [places_ref[t, l] for l in range(LANES)]
        rows = [
            source[pl.ds(pl.multiple_of((t * LANES + l) * pitch, pitch), pitch), :] for l in range(LANES)
        ]
        for l in range(LANES):
            target[pl.ds(pl.multiple_of(places[l], pitch), pitch), :] = rows[l]
        return carry

    lax.fori_loop(0, tiles, move, 0)


def send_kernel(send_each, me_ref, index_ref, points_ref, out_ref, slot_ref, held, rows, sent, places, places_smem, arrivals, moved):
    rows_dev, width = held.shape
    tiles = rows_dev // LANES
    chunks = width // LANES
    per_tile = LANES // send_each
    peers = rows_dev // send_each
    step_peers = out_ref.shape[0]
    step = pl.program_id(0)

    @pl.when(step == 0)
    def _():
        pieces = [
            pltpu.make_async_copy(points_ref.at[pl.ds(k, DEPTH)], held.at[pl.ds(k, DEPTH)], arrivals.at[k // DEPTH])
            for k in range(0, rows_dev, DEPTH)
        ]
        for piece in pieces:
            piece.start()
        index = index_ref[...].astype(F32)
        dest = jnp.floor(index * (1.0 / rows_dev))
        local = index - dest * rows_dev
        high = jnp.floor(local * (1.0 / LOW))
        low = local - high * LOW
        row = lax.broadcasted_iota(jnp.int32, (LANES, LANES), 0)
        lane = lax.broadcasted_iota(jnp.int32, (LANES, LANES), 1)
        peer = lax.broadcasted_iota(jnp.int32, (peers, LANES), 0).astype(F32)
        member = [jnp.where(dest[t : t + 1, :] == peer, 1.0, 0.0) for t in range(tiles)]
        up_to = jnp.where(row <= lane, 1.0, 0.0).astype(BF16)
        counts = dot(jnp.concatenate(member, axis=0).astype(BF16), up_to)
        before = peer[:, 0:1] * send_each - 1.0
        for t in range(tiles):
            count = counts[t * peers : (t + 1) * peers, :]
            slot = jnp.sum(member[t] * (count + before), axis=0, keepdims=True)
            places[t : t + 1, :] = (slot * SEND_PITCH).astype(jnp.int32)
            slot_ref[t : t + 1, :] = (slot * chunks).astype(jnp.int32)
            before = before + count[:, LANES - 1 :]
        move = pltpu.make_async_copy(places, places_smem, moved.at[0])
        move.start()
        for t in range(tiles):
            pair = jnp.where(row == 0, high[t : t + 1, :], jnp.where(row == 1, low[t : t + 1, :], 0.0))
            chunk_rows(rows, t * LANES, LANES, chunks, SEND_PITCH)[...] = pair.T
        for k, piece in enumerate(pieces):
            piece.wait()
            for c in range(chunks):
                part = held[k * DEPTH : (k + 1) * DEPTH, c * LANES : (c + 1) * LANES]
                chunk_rows(rows, k * DEPTH, DEPTH, c, SEND_PITCH)[...] = part.astype(F32)
        move.wait()
        scatter_rows(places_smem, tiles, rows, sent, SEND_PITCH)

    base = step * (step_peers * send_each)
    for peer in range(step_peers):
        for c in range(chunks):
            part = chunk_rows(sent, base + peer * send_each, send_each, c, SEND_PITCH)[...]
            out_ref[peer, c * send_each : (c + 1) * send_each, :] = part.astype(BF16)
    for t in range(step_peers // per_tile):
        both = chunk_rows(sent, base + t * LANES, LANES, chunks, SEND_PITCH)[...].T[0:16, :]
        for v in range(per_tile):
            mine = both
            if per_tile > 1:
                lane = lax.broadcasted_iota(jnp.int32, both.shape, 1)
                mine = jnp.where(lane // send_each == v, both, 0.0)
                mine = pltpu.roll(mine, (me_ref[0] - v + per_tile) % per_tile * send_each, 1)
            out_ref[t * per_tile + v, chunks * send_each :, :] = mine.astype(BF16)


def send_order(points, index_tiles, me, peers):
    rows_dev, width = points.shape
    tiles = rows_dev // LANES
    send_each = rows_dev // peers
    payload = width // LANES * send_each + 16
    return pl.pallas_call(
        functools.partial(send_kernel, send_each),
        grid_spec=pltpu.PrefetchScalarGridSpec(
            num_scalar_prefetch=1,
            grid=(SEND_STEPS,),
            in_specs=[whole((tiles, LANES)), pl.BlockSpec(memory_space=pl.ANY)],
            out_specs=[
                pl.BlockSpec((peers // SEND_STEPS, payload, LANES), lambda i, *_: (i, 0, 0)),
                kept((tiles, LANES)),
            ],
            scratch_shapes=[
                pltpu.VMEM((rows_dev, width), BF16),
                pltpu.VMEM((rows_dev * SEND_PITCH, LANES), F32),
                pltpu.VMEM((rows_dev * SEND_PITCH, LANES), F32),
                pltpu.VMEM((tiles, LANES), jnp.int32),
                pltpu.SMEM((tiles, LANES), jnp.int32),
                pltpu.SemaphoreType.DMA((rows_dev // DEPTH,)),
                pltpu.SemaphoreType.DMA((1,)),
            ],
        ),
        out_shape=[
            jax.ShapeDtypeStruct((peers, payload, LANES), BF16),
            jax.ShapeDtypeStruct((tiles, LANES), jnp.int32),
        ],
        compiler_params=params(60),
        cost_estimate=pl.CostEstimate(
            flops=2 * rows_dev * rows_dev * width, bytes_accessed=4 * rows_dev * width, transcendentals=0
        ),
        name="send_order",
    )(me.reshape(1), index_tiles, points)


def normed_rows(rows32, gain):
    mean_square = jnp.mean(rows32 * rows32, axis=-1, keepdims=True)
    return (rows32 * lax.rsqrt(mean_square + 1e-05) * gain).astype(BF16)


def pool_kernel(arrived_ref, gain_ref, rows_ref, places_ref, pooled_ref, total):
    peers, payload, _ = arrived_ref.shape
    width = gain_ref.shape[1]
    chunks = width // LANES
    send_each = (payload - 16) // chunks
    per_tile = LANES // send_each
    tiles = peers // per_tile
    step = pl.program_id(0)

    @pl.when(step == 0)
    def _():
        total[...] = jnp.zeros_like(total)

    pool = lax.broadcasted_iota(jnp.int32, (total.shape[0], LANES), 0).astype(F32)
    picks = []
    normed = []
    for t in range(tiles):
        row = jnp.zeros((1, LANES), F32)
        for p in range(t * per_tile, (t + 1) * per_tile):
            both = arrived_ref[p, chunks * send_each :, :].astype(F32)
            row = row + both[0:1, :] * LOW + both[1:2, :]
        places_ref[pl.ds(step * tiles + t, 1), :] = (row * chunks).astype(jnp.int32)
        picks.append(jnp.where(jnp.floor(row * (1.0 / POOL)) == pool, 1.0 / POOL, 0.0).astype(BF16))
    for p in range(peers):
        parts = [arrived_ref[p, c * send_each : (c + 1) * send_each, :].astype(F32) for c in range(chunks)]
        for c in range(chunks):
            chunk_rows(rows_ref, p * send_each, send_each, c, chunks)[...] = parts[c]
        normed.append(normed_rows(jnp.concatenate(parts, axis=1), gain_ref[...]))
    total[...] += dot(jnp.concatenate(picks, axis=1), jnp.concatenate(normed, axis=0))

    @pl.when(step == pl.num_programs(0) - 1)
    def _():
        pooled_ref[...] = total[...].astype(BF16)


def pool(arrived, gain, rows_dev):
    width = gain.shape[1]
    chunks = width // LANES
    tiles = rows_dev // LANES
    peers, payload, _ = arrived.shape
    steps = rows_dev // TILE
    pooled = (rows_dev // POOL, width)
    return pl.pallas_call(
        pool_kernel,
        grid=(steps,),
        in_specs=[
            pl.BlockSpec((peers // steps, payload, LANES), lambda i: (i, 0, 0)),
            whole((1, width)),
        ],
        out_specs=[row_blocks(TILE * chunks, LANES), kept((tiles, LANES)), kept(pooled)],
        out_shape=[
            jax.ShapeDtypeStruct((rows_dev * chunks, LANES), F32),
            jax.ShapeDtypeStruct((tiles, LANES), jnp.int32),
            jax.ShapeDtypeStruct(pooled, BF16),
        ],
        scratch_shapes=[pltpu.VMEM(pooled, F32)],
        compiler_params=params(),
        cost_estimate=pl.CostEstimate(
            flops=rows_dev * rows_dev * width // 4, bytes_accessed=4 * rows_dev * width, transcendentals=0
        ),
        name="pool_arrived",
    )(arrived, gain)


def group_kernel(places_ref, rows_ref, gain_ref, grouped_ref, normed_ref, placed):
    count, width = grouped_ref.shape
    chunks = width // LANES
    step = pl.program_id(0)

    @pl.when(step == 0)
    def _():
        scatter_rows(places_ref, places_ref.shape[0], rows_ref, placed, chunks)

    grouped = jnp.concatenate(
        [chunk_rows(placed, step * count, count, c, chunks)[...] for c in range(chunks)], axis=1
    )
    grouped_ref[...] = grouped.astype(BF16)
    normed_ref[...] = normed_rows(grouped, gain_ref[...])


def group(places, rows, gain):
    width = gain.shape[1]
    rows_dev = rows.shape[0] * LANES // width
    blocks = row_blocks(TILE, width)
    return pl.pallas_call(
        group_kernel,
        grid_spec=pltpu.PrefetchScalarGridSpec(
            num_scalar_prefetch=1,
            grid=(rows_dev // TILE,),
            in_specs=[whole(rows.shape), whole((1, width))],
            out_specs=[blocks, blocks],
            scratch_shapes=[pltpu.VMEM(rows.shape, F32)],
        ),
        out_shape=[jax.ShapeDtypeStruct((rows_dev, width), BF16)] * 2,
        compiler_params=params(),
        cost_estimate=pl.CostEstimate(
            flops=2 * rows_dev * rows_dev * width, bytes_accessed=6 * rows_dev * width, transcendentals=0
        ),
        name="group_balls",
    )(places, rows, gain)


def block_matrix(rows, row_step, cols, col_step, value):
    row = lax.broadcasted_iota(jnp.int32, (rows, cols), 0) // row_step
    col = lax.broadcasted_iota(jnp.int32, (rows, cols), 1) // col_step
    return jnp.where(row == col, value, 0.0).astype(BF16)


def prepare(head_size, mean_of, queries, values):
    half = mean_of.shape[0]
    mean_of[...] = block_matrix(half, head_size, half, head_size, 1.0 / head_size)
    queries[...] = jnp.zeros_like(queries)
    values[...] = jnp.ones_like(values)


def normed_keys(keys, mean_of):
    half = mean_of.shape[0]
    square = (keys * keys).astype(BF16)
    mean_square = jnp.concatenate(
        [dot(square[:, c : c + half], mean_of[...]) for c in range(0, keys.shape[1], half)], axis=1
    )
    return (keys * lax.rsqrt(mean_square + 1e-06)).astype(BF16)


def spread_head(h, head_size, columns, queries):
    count = columns.shape[1]
    per_group = LANES // head_size
    g, j = h // per_group, h % per_group
    queries[g, j * head_size : (j + 1) * head_size, j * count : (j + 1) * count] = columns


def weigh(key_rows, queries, weights):
    for g in range(queries.shape[0]):
        score = dot(key_rows[:, g * LANES : (g + 1) * LANES], queries[g])
        weights[g] = jnp.exp2(score).astype(BF16)


def head_sums(g, head_size, values, weights):
    per_group = LANES // head_size
    both = dot(values[g], weights[g])
    count = both.shape[1] // per_group
    for j in range(per_group):
        cols = slice(j * count, (j + 1) * count)
        yield g * per_group + j, both[j * head_size : (j + 1) * head_size, cols], both[LANES : LANES + 1, cols]


def local_kernel(head_size, scale_ref, normed_ref, wq_ref, wk_ref, wv_ref, *rest):
    query_ref, num_ref, den_ref, mean_of, queries, values, weights = rest[-7:]
    width = normed_ref.shape[1]
    groups = width // LANES
    balls = queries.shape[0]

    @pl.when(pl.program_id(0) == 0)
    def _():
        prepare(head_size, mean_of, queries, values)

    normed = normed_ref[...]
    query = dot_nt(wq_ref[...], normed)
    key_rows = normed_keys(dot(normed, wk_ref[...]), mean_of)
    value = dot_nt(wv_ref[...], normed).astype(BF16)
    for h in range(width // head_size):
        rows = slice(h * head_size, (h + 1) * head_size)
        part = query[rows, :]
        root = lax.rsqrt(jnp.mean(part * part, axis=0, keepdims=True) + 1e-06)
        part = (part * (root * scale_ref[h])).astype(BF16)
        query_ref[rows, :] = part
        for b in range(balls):
            spread_head(h, head_size, part[:, b * BALL : (b + 1) * BALL], queries.at[b])
    for b in range(balls):
        cols = slice(b * BALL, (b + 1) * BALL)
        for g in range(groups):
            values[b, g, :LANES, :] = value[g * LANES : (g + 1) * LANES, cols]
        weigh(key_rows[cols, :], queries.at[b], weights.at[b])
    for b in range(balls):
        cols = slice(b * BALL, (b + 1) * BALL)
        for g in range(groups):
            for h, num, den in head_sums(g, head_size, values.at[b], weights.at[b]):
                num_ref[h * head_size : (h + 1) * head_size, cols] = num.astype(BF16)
                den_ref[h : h + 1, cols] = den


def local_attention(first, last, normed, wq, wk, wv, scale, head_size, earlier=()):
    rows_dev, width = normed.shape
    square = whole((width, width))
    groups = width // LANES
    heads = width // head_size
    spread = LANES // head_size * BALL
    balls = math.gcd(math.gcd(first, last), BALLS_STEP)
    steps = (last - first) // balls
    at = lambda i: first // balls + i
    columns = lambda count: pl.BlockSpec((count, balls * BALL), lambda i: (0, at(i)))
    return pl.pallas_call(
        functools.partial(local_kernel, head_size),
        grid=(steps,),
        in_specs=[
            pl.BlockSpec(memory_space=pltpu.SMEM),
            pl.BlockSpec((balls * BALL, width), lambda i: (at(i), 0)),
            square,
            square,
            square,
        ]
        + [pl.BlockSpec(memory_space=pl.ANY)] * len(earlier),
        out_specs=[columns(width), columns(width), columns(heads)],
        out_shape=[
            jax.ShapeDtypeStruct((width, rows_dev), BF16),
            jax.ShapeDtypeStruct((width, rows_dev), BF16),
            jax.ShapeDtypeStruct((heads, rows_dev), F32),
        ],
        scratch_shapes=[
            pltpu.VMEM((2 * LANES, 2 * LANES), BF16),
            pltpu.VMEM((balls, groups, LANES, spread), BF16),
            pltpu.VMEM((balls, groups, LANES + 16, BALL), BF16),
            pltpu.VMEM((balls, groups, BALL, spread), BF16),
        ],
        input_output_aliases={5 + k: k for k in range(len(earlier))},
        compiler_params=params(),
        cost_estimate=pl.CostEstimate(
            flops=20 * (last - first) * BALL * width * width,
            bytes_accessed=12 * (last - first) * BALL * width,
            transcendentals=0,
        ),
        name="local_attention",
    )(scale, normed, wq, wk, wv, *earlier)


def finish_kernel(
    head_size,
    chosen_ref,
    places_ref,
    candidates_ref,
    query_ref,
    num_ref,
    den_ref,
    grouped_ref,
    wpk_ref,
    wpv_ref,
    wo_ref,
    gain_ref,
    wg_ref,
    wu_ref,
    wd_ref,
    out_ref,
    mean_of,
    queries,
    values,
    weights,
    attended,
    rows,
    taken,
):
    step = pl.program_id(0)
    steps = pl.num_programs(0) - TAKE_STEPS
    width, step_rows = attended.shape
    chunks = width // LANES

    @pl.when(step < steps)
    def _():
        result = balls_step(
            head_size, step, chosen_ref, candidates_ref, query_ref, num_ref, den_ref, grouped_ref, wpk_ref,
            wpv_ref, wo_ref, gain_ref, wg_ref, wu_ref, wd_ref, mean_of, queries, values, weights, attended,
        )
        for c in range(chunks):
            part = result[:, c * LANES : (c + 1) * LANES].astype(BF16).astype(F32)
            chunk_rows(rows, step * step_rows, step_rows, c, chunks)[...] = part

    @pl.when(step >= steps)
    def _():
        take_block(places_ref, step - steps, rows, taken, out_ref)


def take_block(places_ref, block, rows, taken, out_ref):
    count, width = out_ref.shape
    chunks = width // LANES
    gather_rows(places_ref, block * (count // LANES), count // LANES, rows, taken, chunks)
    for c in range(chunks):
        out_ref[:, c * LANES : (c + 1) * LANES] = chunk_rows(taken, 0, count, c, chunks)[...].astype(BF16)


def balls_step(
    head_size,
    step,
    chosen_ref,
    candidates_ref,
    query_ref,
    num_ref,
    den_ref,
    grouped_ref,
    wpk_ref,
    wpv_ref,
    wo_ref,
    gain_ref,
    wg_ref,
    wu_ref,
    wd_ref,
    mean_of,
    queries,
    values,
    weights,
    attended,
):
    groups = wo_ref.shape[0] // LANES
    far = OWNERS * BALL // POOL

    @pl.when(step == 0)
    def _():
        prepare(head_size, mean_of, queries, values)

    first = step * BALLS_STEP * OWNERS
    coarse = jnp.concatenate(
        [candidates_ref[chosen_ref[first + o]] for o in range(BALLS_STEP * OWNERS)], axis=0
    )
    key_rows = normed_keys(dot(coarse, wpk_ref[...]), mean_of)
    value = dot_nt(wpv_ref[...], coarse).astype(BF16)
    for b in range(BALLS_STEP):
        cols = slice(b * BALL, (b + 1) * BALL)
        for h in range(groups * LANES // head_size):
            spread_head(h, head_size, query_ref[h * head_size : (h + 1) * head_size, cols], queries.at[b])
        for g in range(groups):
            values[b, g, :LANES, :] = value[g * LANES : (g + 1) * LANES, b * far : (b + 1) * far]
        weigh(key_rows[b * far : (b + 1) * far, :], queries.at[b], weights.at[b])
    for b in range(BALLS_STEP):
        cols = slice(b * BALL, (b + 1) * BALL)
        for g in range(groups):
            for h, num, den in head_sums(g, head_size, values.at[b], weights.at[b]):
                rows = slice(h * head_size, (h + 1) * head_size)
                num = num + num_ref[rows, cols].astype(F32)
                attended[rows, cols] = (num * (1.0 / (den + den_ref[h : h + 1, cols]))).astype(BF16)
    projected = dot(attended[...].T, wo_ref[...])
    residual = (grouped_ref[...].astype(F32) + projected).astype(BF16)
    rows32 = residual.astype(F32)
    ffn = normed_rows(rows32, gain_ref[...])
    gate = dot(ffn, wg_ref[...])
    up = dot(ffn, wu_ref[...])
    hidden = (0.5 * gate * (1.0 + jnp.tanh(0.5 * gate)) * up).astype(BF16)
    return rows32 + dot(hidden, wd_ref[...])


def finish(chosen, places, candidates, query, num, den, grouped, wpk, wpv, wo, gain, wg, wu, wd, head_size):
    rows_dev, width = grouped.shape
    hidden = wg.shape[1]
    groups = width // LANES
    step_rows = BALLS_STEP * BALL
    spread = LANES // head_size * BALL
    far = OWNERS * BALL // POOL
    steps = rows_dev // step_rows
    rows = pl.BlockSpec((step_rows, width), lambda i, *_: (jnp.minimum(i, steps - 1), 0))
    columns = lambda count: pl.BlockSpec((count, step_rows), lambda i, *_: (0, jnp.minimum(i, steps - 1)))
    take_rows = rows_dev // TAKE_STEPS
    fixed = [wpk, wpv, wo, gain, wg, wu, wd]
    return pl.pallas_call(
        functools.partial(finish_kernel, head_size),
        grid_spec=pltpu.PrefetchScalarGridSpec(
            num_scalar_prefetch=2,
            grid=(steps + TAKE_STEPS,),
            in_specs=[
                whole(candidates.shape),
                columns(width),
                columns(width),
                columns(width // head_size),
                rows,
            ]
            + [whole(a.shape) for a in fixed],
            out_specs=pl.BlockSpec((take_rows, width), lambda i, *_: (jnp.maximum(i - steps, 0), 0)),
            scratch_shapes=[
                pltpu.VMEM((2 * LANES, 2 * LANES), BF16),
                pltpu.VMEM((BALLS_STEP, groups, LANES, spread), BF16),
                pltpu.VMEM((BALLS_STEP, groups, LANES + 16, far), BF16),
                pltpu.VMEM((BALLS_STEP, groups, far, spread), BF16),
                pltpu.VMEM((width, step_rows), BF16),
                pltpu.VMEM((rows_dev * (width // LANES), LANES), F32),
                pltpu.VMEM((take_rows * (width // LANES), LANES), F32),
            ],
        ),
        out_shape=jax.ShapeDtypeStruct((rows_dev, width), BF16),
        compiler_params=params(),
        cost_estimate=pl.CostEstimate(
            flops=2 * rows_dev * width * (3 * hidden + 6 * width),
            bytes_accessed=12 * rows_dev * width,
            transcendentals=0,
        ),
        name="finish_balls",
    )(chosen, places, candidates, query, num, den, grouped, *fixed)


def take_kernel(places_ref, source_ref, out_ref, rows, taken):
    count, width = source_ref.shape
    chunks = width // LANES

    @pl.when(pl.program_id(0) == 0)
    def _():
        for first in range(0, count, DEPTH):
            for c in range(chunks):
                part = source_ref[first : first + DEPTH, c * LANES : (c + 1) * LANES]
                chunk_rows(rows, first, DEPTH, c, chunks)[...] = part.astype(F32)

    take_block(places_ref, pl.program_id(0), rows, taken, out_ref)


def take_rows(places, source):
    rows_dev, width = source.shape
    chunks = width // LANES
    return pl.pallas_call(
        take_kernel,
        grid_spec=pltpu.PrefetchScalarGridSpec(
            num_scalar_prefetch=1,
            grid=(rows_dev // TILE,),
            in_specs=[whole(source.shape)],
            out_specs=row_blocks(TILE, width),
            scratch_shapes=[
                pltpu.VMEM((rows_dev * chunks, LANES), F32),
                pltpu.VMEM((TILE * chunks, LANES), F32),
            ],
        ),
        out_shape=jax.ShapeDtypeStruct((rows_dev, width), BF16),
        compiler_params=params(),
        cost_estimate=pl.CostEstimate(
            flops=2 * rows_dev * rows_dev * width, bytes_accessed=4 * rows_dev * width, transcendentals=0
        ),
        name="take_rows",
    )(places, source)


def route(block, target):
    devices = range(lax.axis_size("pts"))
    return lax.ppermute(block, "pts", [(i, target(i) % len(devices)) for i in devices])


def to_mate(block, mate):
    return route(block, lambda i: i ^ mate)


SLOT_INSIDE = (0, 5, 1, 6)
SLOT_OUTSIDE = (2, 7, 4, 8)


def block_slots(owner, me, peers):
    mate = (owner % GROUP) ^ (me % GROUP)
    ahead = jnp.mod(owner // GROUP - me // GROUP, peers // GROUP)
    pick = lambda table: sum(jnp.where(mate == m, table[m], 0) for m in range(GROUP))
    second = (mate == 0) & ((ahead == 1) != (me % GROUP < 2))
    return jnp.where(ahead == 0, pick(SLOT_INSIDE), pick(SLOT_OUTSIDE) + jnp.where(second, 1, 0))


def on_device(
    points,
    point_row_index,
    neighbour_ball_list,
    attention_norm_gain,
    query_weight,
    key_weight,
    value_weight,
    pooled_key_weight,
    pooled_value_weight,
    head_score_scale,
    output_weight,
    feedforward_norm_gain,
    gate_weight,
    up_weight,
    down_weight,
):
    rows_dev, width = points.shape
    head_size = width // head_score_scale.shape[0]
    peers = lax.axis_size("pts")
    me = lax.axis_index("pts")
    send_each = rows_dev // peers
    blocks_dev = rows_dev // BALL
    comp = BALL // POOL

    def swap(array):
        return lax.all_to_all(array, "pts", split_axis=0, concat_axis=0, tiled=True)

    outgoing, slot = send_order(points, point_row_index.reshape(rows_dev // LANES, LANES), me, peers)
    rows, places, pooled = pool(swap(outgoing), attention_norm_gain[None], rows_dev)
    up = lambda i: i % GROUP >= 2
    first = route(pooled, lambda i: i + GROUP if up(i) else i - GROUP)
    other = route(pooled, lambda i: i - GROUP if up(i) else i + GROUP)
    beside = to_mate(pooled, 2)
    grouped, normed = group(places, rows, attention_norm_gain[None])
    first, normed = lax.optimization_barrier((first, normed))
    handed = to_mate(first, 2)
    scale = head_score_scale * (LOG2E / head_size)
    attend = functools.partial(
        local_attention,
        normed=normed,
        wq=query_weight.T,
        wk=key_weight,
        wv=value_weight.T,
        scale=scale,
        head_size=head_size,
    )
    early = blocks_dev * 3 // 4
    part = attend(0, early)
    first, other, beside, handed, part = lax.optimization_barrier((first, other, beside, handed, part))
    place = me % GROUP
    held = jnp.stack([pooled, beside, jnp.where(place // 2 == place % 2, first, other), handed])
    near = to_mate(held, 1)
    query, num, den = attend(early, blocks_dev, earlier=part)
    candidates = jnp.concatenate([jnp.stack([pooled, beside, first, other, handed]), near])
    candidates = candidates.reshape(candidates.shape[0] * blocks_dev, comp, width)
    slots = block_slots(neighbour_ball_list // blocks_dev, me, peers)
    chosen = (slots * blocks_dev + neighbour_ball_list % blocks_dev).reshape(-1)
    returning = finish(
        chosen,
        places,
        candidates,
        query,
        num,
        den,
        grouped,
        pooled_key_weight,
        pooled_value_weight.T,
        output_weight,
        feedforward_norm_gain[None],
        gate_weight,
        up_weight,
        down_weight,
        head_size,
    )
    came_back = swap(returning.reshape(peers, send_each, width)).reshape(rows_dev, width)
    return take_rows(slot, came_back)


def solution(mesh):
    rows = P(("rep", "pts"), None)
    return jax.shard_map(
        on_device,
        mesh=mesh,
        in_specs=(rows, P(("rep", "pts")), rows) + (P(),) * 12,
        out_specs=rows,
        check_vma=False,
    )
```

```python
import functools
import math

import jax
import jax.numpy as jnp
from jax import lax
from jax.experimental import pallas as pl
from jax.experimental.pallas import tpu as pltpu
from jax.sharding import PartitionSpec as P

BALL = 256
POOL = 8
OWNERS = 4
GROUP = 4
LANES = 128
TILE = 512
DEPTH = 512
BALLS_STEP = 4
LOW = 64
SEND_PITCH = 8
SEND_STEPS = 2
TAKE_STEPS = 2
LOG2E = math.log2(math.e)
F32 = jnp.float32
BF16 = jnp.bfloat16


def params(mebibytes=28):
    return pltpu.CompilerParams(vmem_limit_bytes=mebibytes * 1024 * 1024)


def dot(a, b):
    return jnp.dot(a, b, preferred_element_type=F32)


def dot_nt(a, b):
    return lax.dot_general(a, b, (((1,), (1,)), ((), ())), preferred_element_type=F32)


def whole(shape):
    return pl.BlockSpec(shape, lambda *_: (0,) * len(shape), pipeline_mode=pl.Buffered(1))


def kept(shape):
    return pl.BlockSpec(shape, lambda *_: (0,) * len(shape))


def row_blocks(rows, width):
    return pl.BlockSpec((rows, width), lambda i, *_: (i, 0))


def chunk_rows(ref, first, rows, chunk, pitch):
    return ref.at[pl.ds(first * pitch + chunk, rows, stride=pitch), :]


def gather_rows(places_ref, first_tile, tiles, source, target, pitch):
    def move(t, carry):
        places = [places_ref[first_tile + t, l] for l in range(LANES)]
        rows = [source[pl.ds(pl.multiple_of(p, pitch), pitch), :] for p in places]
        for l in range(LANES):
            target[pl.ds(pl.multiple_of((t * LANES + l) * pitch, pitch), pitch), :] = rows[l]
        return carry

    lax.fori_loop(0, tiles, move, 0)


def scatter_rows(places_ref, tiles, source, target, pitch):
    def move(t, carry):
        places = [places_ref[t, l] for l in range(LANES)]
        rows = [
            source[pl.ds(pl.multiple_of((t * LANES + l) * pitch, pitch), pitch), :] for l in range(LANES)
        ]
        for l in range(LANES):
            target[pl.ds(pl.multiple_of(places[l], pitch), pitch), :] = rows[l]
        return carry

    lax.fori_loop(0, tiles, move, 0)


def send_kernel(send_each, me_ref, index_ref, points_ref, out_ref, slot_ref, held, rows, sent, places, places_smem, arrivals, moved):
    rows_dev, width = held.shape
    tiles = rows_dev // LANES
    chunks = width // LANES
    per_tile = LANES // send_each
    peers = rows_dev // send_each
    step_peers = out_ref.shape[0]
    step = pl.program_id(0)

    @pl.when(step == 0)
    def _():
        pieces = [
            pltpu.make_async_copy(points_ref.at[pl.ds(k, DEPTH)], held.at[pl.ds(k, DEPTH)], arrivals.at[k // DEPTH])
            for k in range(0, rows_dev, DEPTH)
        ]
        for piece in pieces:
            piece.start()
        index = index_ref[...].astype(F32)
        dest = jnp.floor(index * (1.0 / rows_dev))
        local = index - dest * rows_dev
        high = jnp.floor(local * (1.0 / LOW))
        low = local - high * LOW
        row = lax.broadcasted_iota(jnp.int32, (LANES, LANES), 0)
        lane = lax.broadcasted_iota(jnp.int32, (LANES, LANES), 1)
        peer = lax.broadcasted_iota(jnp.int32, (peers, LANES), 0).astype(F32)
        member = [jnp.where(dest[t : t + 1, :] == peer, 1.0, 0.0) for t in range(tiles)]
        up_to = jnp.where(row <= lane, 1.0, 0.0).astype(BF16)
        counts = dot(jnp.concatenate(member, axis=0).astype(BF16), up_to)
        before = peer[:, 0:1] * send_each - 1.0
        for t in range(tiles):
            count = counts[t * peers : (t + 1) * peers, :]
            slot = jnp.sum(member[t] * (count + before), axis=0, keepdims=True)
            places[t : t + 1, :] = (slot * SEND_PITCH).astype(jnp.int32)
            slot_ref[t : t + 1, :] = (slot * chunks).astype(jnp.int32)
            before = before + count[:, LANES - 1 :]
        move = pltpu.make_async_copy(places, places_smem, moved.at[0])
        move.start()
        for t in range(tiles):
            pair = jnp.where(row == 0, high[t : t + 1, :], jnp.where(row == 1, low[t : t + 1, :], 0.0))
            chunk_rows(rows, t * LANES, LANES, chunks, SEND_PITCH)[...] = pair.T
        for k, piece in enumerate(pieces):
            piece.wait()
            for c in range(chunks):
                part = held[k * DEPTH : (k + 1) * DEPTH, c * LANES : (c + 1) * LANES]
                chunk_rows(rows, k * DEPTH, DEPTH, c, SEND_PITCH)[...] = part.astype(F32)
        move.wait()
        scatter_rows(places_smem, tiles, rows, sent, SEND_PITCH)

    base = step * (step_peers * send_each)
    for peer in range(step_peers):
        for c in range(chunks):
            part = chunk_rows(sent, base + peer * send_each, send_each, c, SEND_PITCH)[...]
            out_ref[peer, c * send_each : (c + 1) * send_each, :] = part.astype(BF16)
    for t in range(step_peers // per_tile):
        both = chunk_rows(sent, base + t * LANES, LANES, chunks, SEND_PITCH)[...].T[0:16, :]
        for v in range(per_tile):
            mine = both
            if per_tile > 1:
                lane = lax.broadcasted_iota(jnp.int32, both.shape, 1)
                mine = jnp.where(lane // send_each == v, both, 0.0)
                mine = pltpu.roll(mine, (me_ref[0] - v + per_tile) % per_tile * send_each, 1)
            out_ref[t * per_tile + v, chunks * send_each :, :] = mine.astype(BF16)


def send_order(points, index_tiles, me, peers):
    rows_dev, width = points.shape
    tiles = rows_dev // LANES
    send_each = rows_dev // peers
    payload = width // LANES * send_each + 16
    return pl.pallas_call(
        functools.partial(send_kernel, send_each),
        grid_spec=pltpu.PrefetchScalarGridSpec(
            num_scalar_prefetch=1,
            grid=(SEND_STEPS,),
            in_specs=[whole((tiles, LANES)), pl.BlockSpec(memory_space=pl.ANY)],
            out_specs=[
                pl.BlockSpec((peers // SEND_STEPS, payload, LANES), lambda i, *_: (i, 0, 0)),
                kept((tiles, LANES)),
            ],
            scratch_shapes=[
                pltpu.VMEM((rows_dev, width), BF16),
                pltpu.VMEM((rows_dev * SEND_PITCH, LANES), F32),
                pltpu.VMEM((rows_dev * SEND_PITCH, LANES), F32),
                pltpu.VMEM((tiles, LANES), jnp.int32),
                pltpu.SMEM((tiles, LANES), jnp.int32),
                pltpu.SemaphoreType.DMA((rows_dev // DEPTH,)),
                pltpu.SemaphoreType.DMA((1,)),
            ],
        ),
        out_shape=[
            jax.ShapeDtypeStruct((peers, payload, LANES), BF16),
            jax.ShapeDtypeStruct((tiles, LANES), jnp.int32),
        ],
        compiler_params=params(60),
        cost_estimate=pl.CostEstimate(
            flops=2 * rows_dev * rows_dev * width, bytes_accessed=4 * rows_dev * width, transcendentals=0
        ),
        name="send_order",
    )(me.reshape(1), index_tiles, points)


def normed_rows(rows32, gain):
    mean_square = jnp.mean(rows32 * rows32, axis=-1, keepdims=True)
    return (rows32 * lax.rsqrt(mean_square + 1e-05) * gain).astype(BF16)


def pool_kernel(arrived_ref, gain_ref, rows_ref, places_ref, pooled_ref, total):
    peers, payload, _ = arrived_ref.shape
    width = gain_ref.shape[1]
    chunks = width // LANES
    send_each = (payload - 16) // chunks
    per_tile = LANES // send_each
    tiles = peers // per_tile
    step = pl.program_id(0)

    @pl.when(step == 0)
    def _():
        total[...] = jnp.zeros_like(total)

    pool = lax.broadcasted_iota(jnp.int32, (total.shape[0], LANES), 0).astype(F32)
    picks = []
    normed = []
    for t in range(tiles):
        row = jnp.zeros((1, LANES), F32)
        for p in range(t * per_tile, (t + 1) * per_tile):
            both = arrived_ref[p, chunks * send_each :, :].astype(F32)
            row = row + both[0:1, :] * LOW + both[1:2, :]
        places_ref[pl.ds(step * tiles + t, 1), :] = (row * chunks).astype(jnp.int32)
        picks.append(jnp.where(jnp.floor(row * (1.0 / POOL)) == pool, 1.0 / POOL, 0.0).astype(BF16))
    for p in range(peers):
        parts = [arrived_ref[p, c * send_each : (c + 1) * send_each, :].astype(F32) for c in range(chunks)]
        for c in range(chunks):
            chunk_rows(rows_ref, p * send_each, send_each, c, chunks)[...] = parts[c]
        normed.append(normed_rows(jnp.concatenate(parts, axis=1), gain_ref[...]))
    total[...] += dot(jnp.concatenate(picks, axis=1), jnp.concatenate(normed, axis=0))

    @pl.when(step == pl.num_programs(0) - 1)
    def _():
        pooled_ref[...] = total[...].astype(BF16)


def pool(arrived, gain, rows_dev):
    width = gain.shape[1]
    chunks = width // LANES
    tiles = rows_dev // LANES
    peers, payload, _ = arrived.shape
    steps = rows_dev // TILE
    pooled = (rows_dev // POOL, width)
    return pl.pallas_call(
        pool_kernel,
        grid=(steps,),
        in_specs=[
            pl.BlockSpec((peers // steps, payload, LANES), lambda i: (i, 0, 0)),
            whole((1, width)),
        ],
        out_specs=[row_blocks(TILE * chunks, LANES), kept((tiles, LANES)), kept(pooled)],
        out_shape=[
            jax.ShapeDtypeStruct((rows_dev * chunks, LANES), F32),
            jax.ShapeDtypeStruct((tiles, LANES), jnp.int32),
            jax.ShapeDtypeStruct(pooled, BF16),
        ],
        scratch_shapes=[pltpu.VMEM(pooled, F32)],
        compiler_params=params(),
        cost_estimate=pl.CostEstimate(
            flops=rows_dev * rows_dev * width // 4, bytes_accessed=4 * rows_dev * width, transcendentals=0
        ),
        name="pool_arrived",
    )(arrived, gain)


def group_kernel(places_ref, rows_ref, gain_ref, grouped_ref, normed_ref, placed):
    count, width = grouped_ref.shape
    chunks = width // LANES
    step = pl.program_id(0)

    @pl.when(step == 0)
    def _():
        scatter_rows(places_ref, places_ref.shape[0], rows_ref, placed, chunks)

    grouped = jnp.concatenate(
        [chunk_rows(placed, step * count, count, c, chunks)[...] for c in range(chunks)], axis=1
    )
    grouped_ref[...] = grouped.astype(BF16)
    normed_ref[...] = normed_rows(grouped, gain_ref[...])


def group(places, rows, gain):
    width = gain.shape[1]
    rows_dev = rows.shape[0] * LANES // width
    blocks = row_blocks(TILE, width)
    return pl.pallas_call(
        group_kernel,
        grid_spec=pltpu.PrefetchScalarGridSpec(
            num_scalar_prefetch=1,
            grid=(rows_dev // TILE,),
            in_specs=[whole(rows.shape), whole((1, width))],
            out_specs=[blocks, blocks],
            scratch_shapes=[pltpu.VMEM(rows.shape, F32)],
        ),
        out_shape=[jax.ShapeDtypeStruct((rows_dev, width), BF16)] * 2,
        compiler_params=params(),
        cost_estimate=pl.CostEstimate(
            flops=2 * rows_dev * rows_dev * width, bytes_accessed=6 * rows_dev * width, transcendentals=0
        ),
        name="group_balls",
    )(places, rows, gain)


def block_matrix(rows, row_step, cols, col_step, value):
    row = lax.broadcasted_iota(jnp.int32, (rows, cols), 0) // row_step
    col = lax.broadcasted_iota(jnp.int32, (rows, cols), 1) // col_step
    return jnp.where(row == col, value, 0.0).astype(BF16)


def prepare(head_size, mean_of, queries, values):
    half = mean_of.shape[0]
    mean_of[...] = block_matrix(half, head_size, half, head_size, 1.0 / head_size)
    queries[...] = jnp.zeros_like(queries)
    values[...] = jnp.ones_like(values)


def normed_keys(keys, mean_of):
    half = mean_of.shape[0]
    square = (keys * keys).astype(BF16)
    mean_square = jnp.concatenate(
        [dot(square[:, c : c + half], mean_of[...]) for c in range(0, keys.shape[1], half)], axis=1
    )
    return (keys * lax.rsqrt(mean_square + 1e-06)).astype(BF16)


def spread_head(h, head_size, columns, queries):
    count = columns.shape[1]
    per_group = LANES // head_size
    g, j = h // per_group, h % per_group
    queries[g, j * head_size : (j + 1) * head_size, j * count : (j + 1) * count] = columns


def weigh(key_rows, queries, weights):
    for g in range(queries.shape[0]):
        score = dot(key_rows[:, g * LANES : (g + 1) * LANES], queries[g])
        weights[g] = jnp.exp2(score).astype(BF16)


def head_sums(g, head_size, values, weights):
    per_group = LANES // head_size
    both = dot(values[g], weights[g])
    count = both.shape[1] // per_group
    for j in range(per_group):
        cols = slice(j * count, (j + 1) * count)
        yield g * per_group + j, both[j * head_size : (j + 1) * head_size, cols], both[LANES : LANES + 1, cols]


def local_kernel(head_size, scale_ref, normed_ref, wq_ref, wk_ref, wv_ref, *rest):
    query_ref, num_ref, den_ref, mean_of, queries, values, weights = rest[-7:]
    width = normed_ref.shape[1]
    groups = width // LANES
    balls = queries.shape[0]

    @pl.when(pl.program_id(0) == 0)
    def _():
        prepare(head_size, mean_of, queries, values)

    normed = normed_ref[...]
    query = dot_nt(wq_ref[...], normed)
    key_rows = normed_keys(dot(normed, wk_ref[...]), mean_of)
    value = dot_nt(wv_ref[...], normed).astype(BF16)
    for h in range(width // head_size):
        rows = slice(h * head_size, (h + 1) * head_size)
        part = query[rows, :]
        root = lax.rsqrt(jnp.mean(part * part, axis=0, keepdims=True) + 1e-06)
        part = (part * (root * scale_ref[h])).astype(BF16)
        query_ref[rows, :] = part
        for b in range(balls):
            spread_head(h, head_size, part[:, b * BALL : (b + 1) * BALL], queries.at[b])
    for b in range(balls):
        cols = slice(b * BALL, (b + 1) * BALL)
        for g in range(groups):
            values[b, g, :LANES, :] = value[g * LANES : (g + 1) * LANES, cols]
        weigh(key_rows[cols, :], queries.at[b], weights.at[b])
    for b in range(balls):
        cols = slice(b * BALL, (b + 1) * BALL)
        for g in range(groups):
            for h, num, den in head_sums(g, head_size, values.at[b], weights.at[b]):
                num_ref[h * head_size : (h + 1) * head_size, cols] = num.astype(BF16)
                den_ref[h : h + 1, cols] = den


def local_attention(first, last, normed, wq, wk, wv, scale, head_size, earlier=()):
    rows_dev, width = normed.shape
    square = whole((width, width))
    groups = width // LANES
    heads = width // head_size
    spread = LANES // head_size * BALL
    balls = math.gcd(math.gcd(first, last), 2)
    steps = (last - first) // balls
    at = lambda i: first // balls + i
    columns = lambda count: pl.BlockSpec((count, balls * BALL), lambda i: (0, at(i)))
    return pl.pallas_call(
        functools.partial(local_kernel, head_size),
        grid=(steps,),
        in_specs=[
            pl.BlockSpec(memory_space=pltpu.SMEM),
            pl.BlockSpec((balls * BALL, width), lambda i: (at(i), 0)),
            square,
            square,
            square,
        ]
        + [pl.BlockSpec(memory_space=pl.ANY)] * len(earlier),
        out_specs=[columns(width), columns(width), columns(heads)],
        out_shape=[
            jax.ShapeDtypeStruct((width, rows_dev), BF16),
            jax.ShapeDtypeStruct((width, rows_dev), BF16),
            jax.ShapeDtypeStruct((heads, rows_dev), F32),
        ],
        scratch_shapes=[
            pltpu.VMEM((2 * LANES, 2 * LANES), BF16),
            pltpu.VMEM((balls, groups, LANES, spread), BF16),
            pltpu.VMEM((balls, groups, LANES + 16, BALL), BF16),
            pltpu.VMEM((balls, groups, BALL, spread), BF16),
        ],
        input_output_aliases={5 + k: k for k in range(len(earlier))},
        compiler_params=params(),
        cost_estimate=pl.CostEstimate(
            flops=20 * (last - first) * BALL * width * width,
            bytes_accessed=12 * (last - first) * BALL * width,
            transcendentals=0,
        ),
        name="local_attention",
    )(scale, normed, wq, wk, wv, *earlier)


def finish_kernel(
    head_size,
    chosen_ref,
    places_ref,
    candidates_ref,
    query_ref,
    num_ref,
    den_ref,
    grouped_ref,
    wpk_ref,
    wpv_ref,
    wo_ref,
    gain_ref,
    wg_ref,
    wu_ref,
    wd_ref,
    out_ref,
    mean_of,
    queries,
    values,
    weights,
    attended,
    rows,
    taken,
):
    step = pl.program_id(0)
    steps = pl.num_programs(0) - TAKE_STEPS
    width, step_rows = attended.shape
    chunks = width // LANES

    @pl.when(step < steps)
    def _():
        result = balls_step(
            head_size, step, chosen_ref, candidates_ref, query_ref, num_ref, den_ref, grouped_ref, wpk_ref,
            wpv_ref, wo_ref, gain_ref, wg_ref, wu_ref, wd_ref, mean_of, queries, values, weights, attended,
        )
        for c in range(chunks):
            part = result[:, c * LANES : (c + 1) * LANES].astype(BF16).astype(F32)
            chunk_rows(rows, step * step_rows, step_rows, c, chunks)[...] = part

    @pl.when(step >= steps)
    def _():
        take_block(places_ref, step - steps, rows, taken, out_ref)


def take_block(places_ref, block, rows, taken, out_ref):
    count, width = out_ref.shape
    chunks = width // LANES
    gather_rows(places_ref, block * (count // LANES), count // LANES, rows, taken, chunks)
    for c in range(chunks):
        out_ref[:, c * LANES : (c + 1) * LANES] = chunk_rows(taken, 0, count, c, chunks)[...].astype(BF16)


def balls_step(
    head_size,
    step,
    chosen_ref,
    candidates_ref,
    query_ref,
    num_ref,
    den_ref,
    grouped_ref,
    wpk_ref,
    wpv_ref,
    wo_ref,
    gain_ref,
    wg_ref,
    wu_ref,
    wd_ref,
    mean_of,
    queries,
    values,
    weights,
    attended,
):
    groups = wo_ref.shape[0] // LANES
    far = OWNERS * BALL // POOL

    @pl.when(step == 0)
    def _():
        prepare(head_size, mean_of, queries, values)

    first = step * BALLS_STEP * OWNERS
    coarse = jnp.concatenate(
        [candidates_ref[chosen_ref[first + o]] for o in range(BALLS_STEP * OWNERS)], axis=0
    )
    key_rows = normed_keys(dot(coarse, wpk_ref[...]), mean_of)
    value = dot_nt(wpv_ref[...], coarse).astype(BF16)
    for b in range(BALLS_STEP):
        cols = slice(b * BALL, (b + 1) * BALL)
        for h in range(groups * LANES // head_size):
            spread_head(h, head_size, query_ref[h * head_size : (h + 1) * head_size, cols], queries.at[b])
        for g in range(groups):
            values[b, g, :LANES, :] = value[g * LANES : (g + 1) * LANES, b * far : (b + 1) * far]
        weigh(key_rows[b * far : (b + 1) * far, :], queries.at[b], weights.at[b])
    for b in range(BALLS_STEP):
        cols = slice(b * BALL, (b + 1) * BALL)
        for g in range(groups):
            for h, num, den in head_sums(g, head_size, values.at[b], weights.at[b]):
                rows = slice(h * head_size, (h + 1) * head_size)
                num = num + num_ref[rows, cols].astype(F32)
                attended[rows, cols] = (num * (1.0 / (den + den_ref[h : h + 1, cols]))).astype(BF16)
    projected = dot(attended[...].T, wo_ref[...])
    residual = (grouped_ref[...].astype(F32) + projected).astype(BF16)
    rows32 = residual.astype(F32)
    ffn = normed_rows(rows32, gain_ref[...])
    gate = dot(ffn, wg_ref[...])
    up = dot(ffn, wu_ref[...])
    hidden = (0.5 * gate * (1.0 + jnp.tanh(0.5 * gate)) * up).astype(BF16)
    return rows32 + dot(hidden, wd_ref[...])


def finish(chosen, places, candidates, query, num, den, grouped, wpk, wpv, wo, gain, wg, wu, wd, head_size):
    rows_dev, width = grouped.shape
    hidden = wg.shape[1]
    groups = width // LANES
    step_rows = BALLS_STEP * BALL
    spread = LANES // head_size * BALL
    far = OWNERS * BALL // POOL
    steps = rows_dev // step_rows
    rows = pl.BlockSpec((step_rows, width), lambda i, *_: (jnp.minimum(i, steps - 1), 0))
    columns = lambda count: pl.BlockSpec((count, step_rows), lambda i, *_: (0, jnp.minimum(i, steps - 1)))
    take_rows = rows_dev // TAKE_STEPS
    fixed = [wpk, wpv, wo, gain, wg, wu, wd]
    return pl.pallas_call(
        functools.partial(finish_kernel, head_size),
        grid_spec=pltpu.PrefetchScalarGridSpec(
            num_scalar_prefetch=2,
            grid=(steps + TAKE_STEPS,),
            in_specs=[
                whole(candidates.shape),
                columns(width),
                columns(width),
                columns(width // head_size),
                rows,
            ]
            + [whole(a.shape) for a in fixed],
            out_specs=pl.BlockSpec((take_rows, width), lambda i, *_: (jnp.maximum(i - steps, 0), 0)),
            scratch_shapes=[
                pltpu.VMEM((2 * LANES, 2 * LANES), BF16),
                pltpu.VMEM((BALLS_STEP, groups, LANES, spread), BF16),
                pltpu.VMEM((BALLS_STEP, groups, LANES + 16, far), BF16),
                pltpu.VMEM((BALLS_STEP, groups, far, spread), BF16),
                pltpu.VMEM((width, step_rows), BF16),
                pltpu.VMEM((rows_dev * (width // LANES), LANES), F32),
                pltpu.VMEM((take_rows * (width // LANES), LANES), F32),
            ],
        ),
        out_shape=jax.ShapeDtypeStruct((rows_dev, width), BF16),
        compiler_params=params(),
        cost_estimate=pl.CostEstimate(
            flops=2 * rows_dev * width * (3 * hidden + 6 * width),
            bytes_accessed=12 * rows_dev * width,
            transcendentals=0,
        ),
        name="finish_balls",
    )(chosen, places, candidates, query, num, den, grouped, *fixed)


def take_kernel(places_ref, source_ref, out_ref, rows, taken):
    count, width = source_ref.shape
    chunks = width // LANES

    @pl.when(pl.program_id(0) == 0)
    def _():
        for first in range(0, count, DEPTH):
            for c in range(chunks):
                part = source_ref[first : first + DEPTH, c * LANES : (c + 1) * LANES]
                chunk_rows(rows, first, DEPTH, c, chunks)[...] = part.astype(F32)

    take_block(places_ref, pl.program_id(0), rows, taken, out_ref)


def take_rows(places, source):
    rows_dev, width = source.shape
    chunks = width // LANES
    return pl.pallas_call(
        take_kernel,
        grid_spec=pltpu.PrefetchScalarGridSpec(
            num_scalar_prefetch=1,
            grid=(rows_dev // TILE,),
            in_specs=[whole(source.shape)],
            out_specs=row_blocks(TILE, width),
            scratch_shapes=[
                pltpu.VMEM((rows_dev * chunks, LANES), F32),
                pltpu.VMEM((TILE * chunks, LANES), F32),
            ],
        ),
        out_shape=jax.ShapeDtypeStruct((rows_dev, width), BF16),
        compiler_params=params(),
        cost_estimate=pl.CostEstimate(
            flops=2 * rows_dev * rows_dev * width, bytes_accessed=4 * rows_dev * width, transcendentals=0
        ),
        name="take_rows",
    )(places, source)


def route(block, target):
    devices = range(lax.axis_size("pts"))
    return lax.ppermute(block, "pts", [(i, target(i) % len(devices)) for i in devices])


def to_mate(block, mate):
    return route(block, lambda i: i ^ mate)


SLOT_INSIDE = (0, 5, 1, 6)
SLOT_OUTSIDE = (2, 7, 4, 8)


def block_slots(owner, me, peers):
    mate = (owner % GROUP) ^ (me % GROUP)
    ahead = jnp.mod(owner // GROUP - me // GROUP, peers // GROUP)
    pick = lambda table: sum(jnp.where(mate == m, table[m], 0) for m in range(GROUP))
    second = (mate == 0) & ((ahead == 1) != (me % GROUP < 2))
    return jnp.where(ahead == 0, pick(SLOT_INSIDE), pick(SLOT_OUTSIDE) + jnp.where(second, 1, 0))


def on_device(
    points,
    point_row_index,
    neighbour_ball_list,
    attention_norm_gain,
    query_weight,
    key_weight,
    value_weight,
    pooled_key_weight,
    pooled_value_weight,
    head_score_scale,
    output_weight,
    feedforward_norm_gain,
    gate_weight,
    up_weight,
    down_weight,
):
    rows_dev, width = points.shape
    head_size = width // head_score_scale.shape[0]
    peers = lax.axis_size("pts")
    me = lax.axis_index("pts")
    send_each = rows_dev // peers
    blocks_dev = rows_dev // BALL
    comp = BALL // POOL

    def swap(array):
        return lax.all_to_all(array, "pts", split_axis=0, concat_axis=0, tiled=True)

    outgoing, slot = send_order(points, point_row_index.reshape(rows_dev // LANES, LANES), me, peers)
    rows, places, pooled = pool(swap(outgoing), attention_norm_gain[None], rows_dev)
    up = lambda i: i % GROUP >= 2
    first = route(pooled, lambda i: i + GROUP if up(i) else i - GROUP)
    other = route(pooled, lambda i: i - GROUP if up(i) else i + GROUP)
    beside = to_mate(pooled, 2)
    grouped, normed = group(places, rows, attention_norm_gain[None])
    scale = head_score_scale * (LOG2E / head_size)
    attend = functools.partial(
        local_attention,
        normed=normed,
        wq=query_weight.T,
        wk=key_weight,
        wv=value_weight.T,
        scale=scale,
        head_size=head_size,
    )
    soon, early = blocks_dev // 4, blocks_dev * 3 // 4
    part = attend(0, soon)
    first, part = lax.optimization_barrier((first, part))
    handed = to_mate(first, 2)
    part = attend(soon, early, earlier=part)
    first, other, beside, handed, part = lax.optimization_barrier((first, other, beside, handed, part))
    place = me % GROUP
    held = jnp.stack([pooled, beside, jnp.where(place // 2 == place % 2, first, other), handed])
    near = to_mate(held, 1)
    query, num, den = attend(early, blocks_dev, earlier=part)
    candidates = jnp.concatenate([jnp.stack([pooled, beside, first, other, handed]), near])
    candidates = candidates.reshape(candidates.shape[0] * blocks_dev, comp, width)
    slots = block_slots(neighbour_ball_list // blocks_dev, me, peers)
    chosen = (slots * blocks_dev + neighbour_ball_list % blocks_dev).reshape(-1)
    returning = finish(
        chosen,
        places,
        candidates,
        query,
        num,
        den,
        grouped,
        pooled_key_weight,
        pooled_value_weight.T,
        output_weight,
        feedforward_norm_gain[None],
        gate_weight,
        up_weight,
        down_weight,
        head_size,
    )
    came_back = swap(returning.reshape(peers, send_each, width)).reshape(rows_dev, width)
    return take_rows(slot, came_back)


def solution(mesh):
    rows = P(("rep", "pts"), None)
    return jax.shard_map(
        on_device,
        mesh=mesh,
        in_specs=(rows, P(("rep", "pts")), rows) + (P(),) * 12,
        out_specs=rows,
        check_vma=False,
    )
```

```python
import functools
import math

import jax
import jax.numpy as jnp
from jax import lax
from jax.experimental import pallas as pl
from jax.experimental.pallas import tpu as pltpu
from jax.sharding import PartitionSpec as P

BALL = 256
POOL = 8
OWNERS = 4
GROUP = 4
LANES = 128
TILE = 1024
DEPTH = 512
BALLS_STEP = 4
LOW = 64
SEND_PITCH = 8
SEND_STEPS = 2
TAKE_STEPS = 2
LOG2E = math.log2(math.e)
F32 = jnp.float32
BF16 = jnp.bfloat16


def params(mebibytes=28):
    return pltpu.CompilerParams(vmem_limit_bytes=mebibytes * 1024 * 1024)


def dot(a, b):
    return jnp.dot(a, b, preferred_element_type=F32)


def dot_nt(a, b):
    return lax.dot_general(a, b, (((1,), (1,)), ((), ())), preferred_element_type=F32)


def whole(shape):
    return pl.BlockSpec(shape, lambda *_: (0,) * len(shape), pipeline_mode=pl.Buffered(1))


def kept(shape):
    return pl.BlockSpec(shape, lambda *_: (0,) * len(shape))


def row_blocks(rows, width):
    return pl.BlockSpec((rows, width), lambda i, *_: (i, 0))


def chunk_rows(ref, first, rows, chunk, pitch):
    return ref.at[pl.ds(first * pitch + chunk, rows, stride=pitch), :]


def gather_rows(places_ref, first_tile, tiles, source, target, pitch):
    def move(t, carry):
        places = [places_ref[first_tile + t, l] for l in range(LANES)]
        rows = [source[pl.ds(pl.multiple_of(p, pitch), pitch), :] for p in places]
        for l in range(LANES):
            target[pl.ds(pl.multiple_of((t * LANES + l) * pitch, pitch), pitch), :] = rows[l]
        return carry

    lax.fori_loop(0, tiles, move, 0)


def scatter_rows(places_ref, tiles, source, target, pitch):
    def move(t, carry):
        places = [places_ref[t, l] for l in range(LANES)]
        rows = [
            source[pl.ds(pl.multiple_of((t * LANES + l) * pitch, pitch), pitch), :] for l in range(LANES)
        ]
        for l in range(LANES):
            target[pl.ds(pl.multiple_of(places[l], pitch), pitch), :] = rows[l]
        return carry

    lax.fori_loop(0, tiles, move, 0)


def send_kernel(send_each, me_ref, index_ref, points_ref, out_ref, slot_ref, held, rows, sent, places, places_smem, arrivals, moved):
    rows_dev, width = held.shape
    tiles = rows_dev // LANES
    chunks = width // LANES
    per_tile = LANES // send_each
    peers = rows_dev // send_each
    step_peers = out_ref.shape[0]
    step = pl.program_id(0)

    @pl.when(step == 0)
    def _():
        pieces = [
            pltpu.make_async_copy(points_ref.at[pl.ds(k, DEPTH)], held.at[pl.ds(k, DEPTH)], arrivals.at[k // DEPTH])
            for k in range(0, rows_dev, DEPTH)
        ]
        for piece in pieces:
            piece.start()
        index = index_ref[...].astype(F32)
        dest = jnp.floor(index * (1.0 / rows_dev))
        local = index - dest * rows_dev
        high = jnp.floor(local * (1.0 / LOW))
        low = local - high * LOW
        row = lax.broadcasted_iota(jnp.int32, (LANES, LANES), 0)
        lane = lax.broadcasted_iota(jnp.int32, (LANES, LANES), 1)
        peer = lax.broadcasted_iota(jnp.int32, (peers, LANES), 0).astype(F32)
        member = [jnp.where(dest[t : t + 1, :] == peer, 1.0, 0.0) for t in range(tiles)]
        up_to = jnp.where(row <= lane, 1.0, 0.0).astype(BF16)
        counts = dot(jnp.concatenate(member, axis=0).astype(BF16), up_to)
        before = peer[:, 0:1] * send_each - 1.0
        for t in range(tiles):
            count = counts[t * peers : (t + 1) * peers, :]
            slot = jnp.sum(member[t] * (count + before), axis=0, keepdims=True)
            places[t : t + 1, :] = (slot * SEND_PITCH).astype(jnp.int32)
            slot_ref[t : t + 1, :] = (slot * chunks).astype(jnp.int32)
            before = before + count[:, LANES - 1 :]
        move = pltpu.make_async_copy(places, places_smem, moved.at[0])
        move.start()
        for t in range(tiles):
            pair = jnp.where(row == 0, high[t : t + 1, :], jnp.where(row == 1, low[t : t + 1, :], 0.0))
            chunk_rows(rows, t * LANES, LANES, chunks, SEND_PITCH)[...] = pair.T
        for k, piece in enumerate(pieces):
            piece.wait()
            for c in range(chunks):
                part = held[k * DEPTH : (k + 1) * DEPTH, c * LANES : (c + 1) * LANES]
                chunk_rows(rows, k * DEPTH, DEPTH, c, SEND_PITCH)[...] = part.astype(F32)
        move.wait()
        scatter_rows(places_smem, tiles, rows, sent, SEND_PITCH)

    base = step * (step_peers * send_each)
    for peer in range(step_peers):
        for c in range(chunks):
            part = chunk_rows(sent, base + peer * send_each, send_each, c, SEND_PITCH)[...]
            out_ref[peer, c * send_each : (c + 1) * send_each, :] = part.astype(BF16)
    for t in range(step_peers // per_tile):
        both = chunk_rows(sent, base + t * LANES, LANES, chunks, SEND_PITCH)[...].T[0:16, :]
        for v in range(per_tile):
            mine = both
            if per_tile > 1:
                lane = lax.broadcasted_iota(jnp.int32, both.shape, 1)
                mine = jnp.where(lane // send_each == v, both, 0.0)
                mine = pltpu.roll(mine, (me_ref[0] - v + per_tile) % per_tile * send_each, 1)
            out_ref[t * per_tile + v, chunks * send_each :, :] = mine.astype(BF16)


def send_order(points, index_tiles, me, peers):
    rows_dev, width = points.shape
    tiles = rows_dev // LANES
    send_each = rows_dev // peers
    payload = width // LANES * send_each + 16
    return pl.pallas_call(
        functools.partial(send_kernel, send_each),
        grid_spec=pltpu.PrefetchScalarGridSpec(
            num_scalar_prefetch=1,
            grid=(SEND_STEPS,),
            in_specs=[whole((tiles, LANES)), pl.BlockSpec(memory_space=pl.ANY)],
            out_specs=[
                pl.BlockSpec((peers // SEND_STEPS, payload, LANES), lambda i, *_: (i, 0, 0)),
                kept((tiles, LANES)),
            ],
            scratch_shapes=[
                pltpu.VMEM((rows_dev, width), BF16),
                pltpu.VMEM((rows_dev * SEND_PITCH, LANES), F32),
                pltpu.VMEM((rows_dev * SEND_PITCH, LANES), F32),
                pltpu.VMEM((tiles, LANES), jnp.int32),
                pltpu.SMEM((tiles, LANES), jnp.int32),
                pltpu.SemaphoreType.DMA((rows_dev // DEPTH,)),
                pltpu.SemaphoreType.DMA((1,)),
            ],
        ),
        out_shape=[
            jax.ShapeDtypeStruct((peers, payload, LANES), BF16),
            jax.ShapeDtypeStruct((tiles, LANES), jnp.int32),
        ],
        compiler_params=params(60),
        cost_estimate=pl.CostEstimate(
            flops=2 * rows_dev * rows_dev * width, bytes_accessed=4 * rows_dev * width, transcendentals=0
        ),
        name="send_order",
    )(me.reshape(1), index_tiles, points)


def normed_rows(rows32, gain):
    mean_square = jnp.mean(rows32 * rows32, axis=-1, keepdims=True)
    return (rows32 * lax.rsqrt(mean_square + 1e-05) * gain).astype(BF16)


def pool_kernel(arrived_ref, gain_ref, rows_ref, places_ref, pooled_ref, total):
    peers, payload, _ = arrived_ref.shape
    width = gain_ref.shape[1]
    chunks = width // LANES
    send_each = (payload - 16) // chunks
    per_tile = LANES // send_each
    tiles = peers // per_tile
    step = pl.program_id(0)

    @pl.when(step == 0)
    def _():
        total[...] = jnp.zeros_like(total)

    pool = lax.broadcasted_iota(jnp.int32, (total.shape[0], LANES), 0).astype(F32)
    picks = []
    normed = []
    for t in range(tiles):
        row = jnp.zeros((1, LANES), F32)
        for p in range(t * per_tile, (t + 1) * per_tile):
            both = arrived_ref[p, chunks * send_each :, :].astype(F32)
            row = row + both[0:1, :] * LOW + both[1:2, :]
        places_ref[pl.ds(step * tiles + t, 1), :] = (row * chunks).astype(jnp.int32)
        picks.append(jnp.where(jnp.floor(row * (1.0 / POOL)) == pool, 1.0 / POOL, 0.0).astype(BF16))
    for p in range(peers):
        parts = [arrived_ref[p, c * send_each : (c + 1) * send_each, :].astype(F32) for c in range(chunks)]
        for c in range(chunks):
            chunk_rows(rows_ref, p * send_each, send_each, c, chunks)[...] = parts[c]
        normed.append(normed_rows(jnp.concatenate(parts, axis=1), gain_ref[...]))
    total[...] += dot(jnp.concatenate(picks, axis=1), jnp.concatenate(normed, axis=0))

    @pl.when(step == pl.num_programs(0) - 1)
    def _():
        pooled_ref[...] = total[...].astype(BF16)


def pool(arrived, gain, rows_dev):
    width = gain.shape[1]
    chunks = width // LANES
    tiles = rows_dev // LANES
    peers, payload, _ = arrived.shape
    steps = rows_dev // TILE
    pooled = (rows_dev // POOL, width)
    return pl.pallas_call(
        pool_kernel,
        grid=(steps,),
        in_specs=[
            pl.BlockSpec((peers // steps, payload, LANES), lambda i: (i, 0, 0)),
            whole((1, width)),
        ],
        out_specs=[row_blocks(TILE * chunks, LANES), kept((tiles, LANES)), kept(pooled)],
        out_shape=[
            jax.ShapeDtypeStruct((rows_dev * chunks, LANES), F32),
            jax.ShapeDtypeStruct((tiles, LANES), jnp.int32),
            jax.ShapeDtypeStruct(pooled, BF16),
        ],
        scratch_shapes=[pltpu.VMEM(pooled, F32)],
        compiler_params=params(),
        cost_estimate=pl.CostEstimate(
            flops=rows_dev * rows_dev * width // 4, bytes_accessed=4 * rows_dev * width, transcendentals=0
        ),
        name="pool_arrived",
    )(arrived, gain)


def group_kernel(places_ref, rows_ref, gain_ref, grouped_ref, normed_ref, placed):
    count, width = grouped_ref.shape
    chunks = width // LANES
    step = pl.program_id(0)

    @pl.when(step == 0)
    def _():
        scatter_rows(places_ref, places_ref.shape[0], rows_ref, placed, chunks)

    grouped = jnp.concatenate(
        [chunk_rows(placed, step * count, count, c, chunks)[...] for c in range(chunks)], axis=1
    )
    grouped_ref[...] = grouped.astype(BF16)
    normed_ref[...] = normed_rows(grouped, gain_ref[...])


def group(places, rows, gain):
    width = gain.shape[1]
    rows_dev = rows.shape[0] * LANES // width
    blocks = row_blocks(TILE, width)
    return pl.pallas_call(
        group_kernel,
        grid_spec=pltpu.PrefetchScalarGridSpec(
            num_scalar_prefetch=1,
            grid=(rows_dev // TILE,),
            in_specs=[whole(rows.shape), whole((1, width))],
            out_specs=[blocks, blocks],
            scratch_shapes=[pltpu.VMEM(rows.shape, F32)],
        ),
        out_shape=[jax.ShapeDtypeStruct((rows_dev, width), BF16)] * 2,
        compiler_params=params(),
        cost_estimate=pl.CostEstimate(
            flops=2 * rows_dev * rows_dev * width, bytes_accessed=6 * rows_dev * width, transcendentals=0
        ),
        name="group_balls",
    )(places, rows, gain)


def block_matrix(rows, row_step, cols, col_step, value):
    row = lax.broadcasted_iota(jnp.int32, (rows, cols), 0) // row_step
    col = lax.broadcasted_iota(jnp.int32, (rows, cols), 1) // col_step
    return jnp.where(row == col, value, 0.0).astype(BF16)


def prepare(head_size, mean_of, queries, values):
    half = mean_of.shape[0]
    mean_of[...] = block_matrix(half, head_size, half, head_size, 1.0 / head_size)
    queries[...] = jnp.zeros_like(queries)
    values[...] = jnp.ones_like(values)


def normed_keys(keys, mean_of):
    half = mean_of.shape[0]
    square = (keys * keys).astype(BF16)
    mean_square = jnp.concatenate(
        [dot(square[:, c : c + half], mean_of[...]) for c in range(0, keys.shape[1], half)], axis=1
    )
    return (keys * lax.rsqrt(mean_square + 1e-06)).astype(BF16)


def spread_head(h, head_size, columns, queries):
    count = columns.shape[1]
    per_group = LANES // head_size
    g, j = h // per_group, h % per_group
    queries[g, j * head_size : (j + 1) * head_size, j * count : (j + 1) * count] = columns


def weigh(key_rows, queries, weights):
    for g in range(queries.shape[0]):
        score = dot(key_rows[:, g * LANES : (g + 1) * LANES], queries[g])
        weights[g] = jnp.exp2(score).astype(BF16)


def head_sums(g, head_size, values, weights):
    per_group = LANES // head_size
    both = dot(values[g], weights[g])
    count = both.shape[1] // per_group
    for j in range(per_group):
        cols = slice(j * count, (j + 1) * count)
        yield g * per_group + j, both[j * head_size : (j + 1) * head_size, cols], both[LANES : LANES + 1, cols]


def local_kernel(head_size, scale_ref, normed_ref, wq_ref, wk_ref, wv_ref, *rest):
    query_ref, num_ref, den_ref, mean_of, queries, values, weights = rest[-7:]
    width = normed_ref.shape[1]
    groups = width // LANES
    balls = queries.shape[0]

    @pl.when(pl.program_id(0) == 0)
    def _():
        prepare(head_size, mean_of, queries, values)

    normed = normed_ref[...]
    query = dot_nt(wq_ref[...], normed)
    key_rows = normed_keys(dot(normed, wk_ref[...]), mean_of)
    value = dot_nt(wv_ref[...], normed).astype(BF16)
    for h in range(width // head_size):
        rows = slice(h * head_size, (h + 1) * head_size)
        part = query[rows, :]
        root = lax.rsqrt(jnp.mean(part * part, axis=0, keepdims=True) + 1e-06)
        part = (part * (root * scale_ref[h])).astype(BF16)
        query_ref[rows, :] = part
        for b in range(balls):
            spread_head(h, head_size, part[:, b * BALL : (b + 1) * BALL], queries.at[b])
    for b in range(balls):
        cols = slice(b * BALL, (b + 1) * BALL)
        for g in range(groups):
            values[b, g, :LANES, :] = value[g * LANES : (g + 1) * LANES, cols]
        weigh(key_rows[cols, :], queries.at[b], weights.at[b])
    for b in range(balls):
        cols = slice(b * BALL, (b + 1) * BALL)
        for g in range(groups):
            for h, num, den in head_sums(g, head_size, values.at[b], weights.at[b]):
                num_ref[h * head_size : (h + 1) * head_size, cols] = num.astype(BF16)
                den_ref[h : h + 1, cols] = den


def local_attention(first, last, normed, wq, wk, wv, scale, head_size, earlier=()):
    rows_dev, width = normed.shape
    square = whole((width, width))
    groups = width // LANES
    heads = width // head_size
    spread = LANES // head_size * BALL
    balls = math.gcd(math.gcd(first, last), 2)
    steps = (last - first) // balls
    at = lambda i: first // balls + i
    columns = lambda count: pl.BlockSpec((count, balls * BALL), lambda i: (0, at(i)))
    return pl.pallas_call(
        functools.partial(local_kernel, head_size),
        grid=(steps,),
        in_specs=[
            pl.BlockSpec(memory_space=pltpu.SMEM),
            pl.BlockSpec((balls * BALL, width), lambda i: (at(i), 0)),
            square,
            square,
            square,
        ]
        + [pl.BlockSpec(memory_space=pl.ANY)] * len(earlier),
        out_specs=[columns(width), columns(width), columns(heads)],
        out_shape=[
            jax.ShapeDtypeStruct((width, rows_dev), BF16),
            jax.ShapeDtypeStruct((width, rows_dev), BF16),
            jax.ShapeDtypeStruct((heads, rows_dev), F32),
        ],
        scratch_shapes=[
            pltpu.VMEM((2 * LANES, 2 * LANES), BF16),
            pltpu.VMEM((balls, groups, LANES, spread), BF16),
            pltpu.VMEM((balls, groups, LANES + 16, BALL), BF16),
            pltpu.VMEM((balls, groups, BALL, spread), BF16),
        ],
        input_output_aliases={5 + k: k for k in range(len(earlier))},
        compiler_params=params(),
        cost_estimate=pl.CostEstimate(
            flops=20 * (last - first) * BALL * width * width,
            bytes_accessed=12 * (last - first) * BALL * width,
            transcendentals=0,
        ),
        name="local_attention",
    )(scale, normed, wq, wk, wv, *earlier)


def finish_kernel(
    head_size,
    chosen_ref,
    places_ref,
    candidates_ref,
    query_ref,
    num_ref,
    den_ref,
    grouped_ref,
    wpk_ref,
    wpv_ref,
    wo_ref,
    gain_ref,
    wg_ref,
    wu_ref,
    wd_ref,
    out_ref,
    mean_of,
    queries,
    values,
    weights,
    attended,
    rows,
    taken,
):
    step = pl.program_id(0)
    steps = pl.num_programs(0) - TAKE_STEPS
    width, step_rows = attended.shape
    chunks = width // LANES

    @pl.when(step < steps)
    def _():
        result = balls_step(
            head_size, step, chosen_ref, candidates_ref, query_ref, num_ref, den_ref, grouped_ref, wpk_ref,
            wpv_ref, wo_ref, gain_ref, wg_ref, wu_ref, wd_ref, mean_of, queries, values, weights, attended,
        )
        for c in range(chunks):
            part = result[:, c * LANES : (c + 1) * LANES].astype(BF16).astype(F32)
            chunk_rows(rows, step * step_rows, step_rows, c, chunks)[...] = part

    @pl.when(step >= steps)
    def _():
        take_block(places_ref, step - steps, rows, taken, out_ref)


def take_block(places_ref, block, rows, taken, out_ref):
    count, width = out_ref.shape
    chunks = width // LANES
    gather_rows(places_ref, block * (count // LANES), count // LANES, rows, taken, chunks)
    for c in range(chunks):
        out_ref[:, c * LANES : (c + 1) * LANES] = chunk_rows(taken, 0, count, c, chunks)[...].astype(BF16)


def balls_step(
    head_size,
    step,
    chosen_ref,
    candidates_ref,
    query_ref,
    num_ref,
    den_ref,
    grouped_ref,
    wpk_ref,
    wpv_ref,
    wo_ref,
    gain_ref,
    wg_ref,
    wu_ref,
    wd_ref,
    mean_of,
    queries,
    values,
    weights,
    attended,
):
    groups = wo_ref.shape[0] // LANES
    far = OWNERS * BALL // POOL

    @pl.when(step == 0)
    def _():
        prepare(head_size, mean_of, queries, values)

    first = step * BALLS_STEP * OWNERS
    coarse = jnp.concatenate(
        [candidates_ref[chosen_ref[first + o]] for o in range(BALLS_STEP * OWNERS)], axis=0
    )
    key_rows = normed_keys(dot(coarse, wpk_ref[...]), mean_of)
    value = dot_nt(wpv_ref[...], coarse).astype(BF16)
    for b in range(BALLS_STEP):
        cols = slice(b * BALL, (b + 1) * BALL)
        for h in range(groups * LANES // head_size):
            spread_head(h, head_size, query_ref[h * head_size : (h + 1) * head_size, cols], queries.at[b % 2])
        for g in range(groups):
            values[b, g, :LANES, :] = value[g * LANES : (g + 1) * LANES, b * far : (b + 1) * far]
        weigh(key_rows[b * far : (b + 1) * far, :], queries.at[b % 2], weights.at[b])
    for b in range(BALLS_STEP):
        cols = slice(b * BALL, (b + 1) * BALL)
        for g in range(groups):
            for h, num, den in head_sums(g, head_size, values.at[b], weights.at[b]):
                rows = slice(h * head_size, (h + 1) * head_size)
                num = num + num_ref[rows, cols].astype(F32)
                attended[rows, cols] = (num * (1.0 / (den + den_ref[h : h + 1, cols]))).astype(BF16)
    projected = dot(attended[...].T, wo_ref[...])
    residual = (grouped_ref[...].astype(F32) + projected).astype(BF16)
    rows32 = residual.astype(F32)
    ffn = normed_rows(rows32, gain_ref[...])
    gate = dot(ffn, wg_ref[...])
    up = dot(ffn, wu_ref[...])
    hidden = (0.5 * gate * (1.0 + jnp.tanh(0.5 * gate)) * up).astype(BF16)
    return rows32 + dot(hidden, wd_ref[...])


def finish(chosen, places, candidates, query, num, den, grouped, wpk, wpv, wo, gain, wg, wu, wd, head_size):
    rows_dev, width = grouped.shape
    hidden = wg.shape[1]
    groups = width // LANES
    step_rows = BALLS_STEP * BALL
    spread = LANES // head_size * BALL
    far = OWNERS * BALL // POOL
    steps = rows_dev // step_rows
    rows = pl.BlockSpec((step_rows, width), lambda i, *_: (jnp.minimum(i, steps - 1), 0))
    columns = lambda count: pl.BlockSpec((count, step_rows), lambda i, *_: (0, jnp.minimum(i, steps - 1)))
    take_rows = rows_dev // TAKE_STEPS
    fixed = [wpk, wpv, wo, gain, wg, wu, wd]
    return pl.pallas_call(
        functools.partial(finish_kernel, head_size),
        grid_spec=pltpu.PrefetchScalarGridSpec(
            num_scalar_prefetch=2,
            grid=(steps + TAKE_STEPS,),
            in_specs=[
                whole(candidates.shape),
                columns(width),
                columns(width),
                columns(width // head_size),
                rows,
            ]
            + [whole(a.shape) for a in fixed],
            out_specs=pl.BlockSpec((take_rows, width), lambda i, *_: (jnp.maximum(i - steps, 0), 0)),
            scratch_shapes=[
                pltpu.VMEM((2 * LANES, 2 * LANES), BF16),
                pltpu.VMEM((2, groups, LANES, spread), BF16),
                pltpu.VMEM((BALLS_STEP, groups, LANES + 16, far), BF16),
                pltpu.VMEM((BALLS_STEP, groups, far, spread), BF16),
                pltpu.VMEM((width, step_rows), BF16),
                pltpu.VMEM((rows_dev * (width // LANES), LANES), F32),
                pltpu.VMEM((take_rows * (width // LANES), LANES), F32),
            ],
        ),
        out_shape=jax.ShapeDtypeStruct((rows_dev, width), BF16),
        compiler_params=params(),
        cost_estimate=pl.CostEstimate(
            flops=2 * rows_dev * width * (3 * hidden + 6 * width),
            bytes_accessed=12 * rows_dev * width,
            transcendentals=0,
        ),
        name="finish_balls",
    )(chosen, places, candidates, query, num, den, grouped, *fixed)


def take_kernel(places_ref, source_ref, out_ref, rows, taken):
    count, width = source_ref.shape
    chunks = width // LANES

    @pl.when(pl.program_id(0) == 0)
    def _():
        for first in range(0, count, DEPTH):
            for c in range(chunks):
                part = source_ref[first : first + DEPTH, c * LANES : (c + 1) * LANES]
                chunk_rows(rows, first, DEPTH, c, chunks)[...] = part.astype(F32)

    take_block(places_ref, pl.program_id(0), rows, taken, out_ref)


def take_rows(places, source):
    rows_dev, width = source.shape
    chunks = width // LANES
    return pl.pallas_call(
        take_kernel,
        grid_spec=pltpu.PrefetchScalarGridSpec(
            num_scalar_prefetch=1,
            grid=(rows_dev // TILE,),
            in_specs=[whole(source.shape)],
            out_specs=row_blocks(TILE, width),
            scratch_shapes=[
                pltpu.VMEM((rows_dev * chunks, LANES), F32),
                pltpu.VMEM((TILE * chunks, LANES), F32),
            ],
        ),
        out_shape=jax.ShapeDtypeStruct((rows_dev, width), BF16),
        compiler_params=params(),
        cost_estimate=pl.CostEstimate(
            flops=2 * rows_dev * rows_dev * width, bytes_accessed=4 * rows_dev * width, transcendentals=0
        ),
        name="take_rows",
    )(places, source)


def route(block, target):
    devices = range(lax.axis_size("pts"))
    return lax.ppermute(block, "pts", [(i, target(i) % len(devices)) for i in devices])


def to_mate(block, mate):
    return route(block, lambda i: i ^ mate)


SLOT_INSIDE = (0, 5, 1, 6)
SLOT_OUTSIDE = (2, 7, 4, 8)


def block_slots(owner, me, peers):
    mate = (owner % GROUP) ^ (me % GROUP)
    ahead = jnp.mod(owner // GROUP - me // GROUP, peers // GROUP)
    pick = lambda table: sum(jnp.where(mate == m, table[m], 0) for m in range(GROUP))
    second = (mate == 0) & ((ahead == 1) != (me % GROUP < 2))
    return jnp.where(ahead == 0, pick(SLOT_INSIDE), pick(SLOT_OUTSIDE) + jnp.where(second, 1, 0))


def on_device(
    points,
    point_row_index,
    neighbour_ball_list,
    attention_norm_gain,
    query_weight,
    key_weight,
    value_weight,
    pooled_key_weight,
    pooled_value_weight,
    head_score_scale,
    output_weight,
    feedforward_norm_gain,
    gate_weight,
    up_weight,
    down_weight,
):
    rows_dev, width = points.shape
    head_size = width // head_score_scale.shape[0]
    peers = lax.axis_size("pts")
    me = lax.axis_index("pts")
    send_each = rows_dev // peers
    blocks_dev = rows_dev // BALL
    comp = BALL // POOL

    def swap(array):
        return lax.all_to_all(array, "pts", split_axis=0, concat_axis=0, tiled=True)

    outgoing, slot = send_order(points, point_row_index.reshape(rows_dev // LANES, LANES), me, peers)
    rows, places, pooled = pool(swap(outgoing), attention_norm_gain[None], rows_dev)
    up = lambda i: i % GROUP >= 2
    first = route(pooled, lambda i: i + GROUP if up(i) else i - GROUP)
    other = route(pooled, lambda i: i - GROUP if up(i) else i + GROUP)
    beside = to_mate(pooled, 2)
    grouped, normed = group(places, rows, attention_norm_gain[None])
    scale = head_score_scale * (LOG2E / head_size)
    attend = functools.partial(
        local_attention,
        normed=normed,
        wq=query_weight.T,
        wk=key_weight,
        wv=value_weight.T,
        scale=scale,
        head_size=head_size,
    )
    soon, early = blocks_dev // 4, blocks_dev * 3 // 4
    part = attend(0, soon)
    first, part = lax.optimization_barrier((first, part))
    handed = to_mate(first, 2)
    part = attend(soon, early, earlier=part)
    first, other, beside, handed, part = lax.optimization_barrier((first, other, beside, handed, part))
    place = me % GROUP
    held = jnp.stack([pooled, beside, jnp.where(place // 2 == place % 2, first, other), handed])
    near = to_mate(held, 1)
    query, num, den = attend(early, blocks_dev, earlier=part)
    candidates = jnp.concatenate([jnp.stack([pooled, beside, first, other, handed]), near])
    candidates = candidates.reshape(candidates.shape[0] * blocks_dev, comp, width)
    slots = block_slots(neighbour_ball_list // blocks_dev, me, peers)
    chosen = (slots * blocks_dev + neighbour_ball_list % blocks_dev).reshape(-1)
    returning = finish(
        chosen,
        places,
        candidates,
        query,
        num,
        den,
        grouped,
        pooled_key_weight,
        pooled_value_weight.T,
        output_weight,
        feedforward_norm_gain[None],
        gate_weight,
        up_weight,
        down_weight,
        head_size,
    )
    came_back = swap(returning.reshape(peers, send_each, width)).reshape(rows_dev, width)
    return take_rows(slot, came_back)


def solution(mesh):
    rows = P(("rep", "pts"), None)
    return jax.shard_map(
        on_device,
        mesh=mesh,
        in_specs=(rows, P(("rep", "pts")), rows) + (P(),) * 12,
        out_specs=rows,
        check_vma=False,
    )
```

```python
import functools
import math

import jax
import jax.numpy as jnp
from jax import lax
from jax.experimental import pallas as pl
from jax.experimental.pallas import tpu as pltpu
from jax.sharding import PartitionSpec as P

BALL = 256
POOL = 8
OWNERS = 4
GROUP = 4
LANES = 128
BATCH = 32
TILE = 1024
DEPTH = 512
BALLS_STEP = 4
LOW = 64
SEND_PITCH = 8
SEND_STEPS = 2
TAKE_STEPS = 2
LOG2E = math.log2(math.e)
F32 = jnp.float32
BF16 = jnp.bfloat16


def params(mebibytes=28):
    return pltpu.CompilerParams(vmem_limit_bytes=mebibytes * 1024 * 1024)


def dot(a, b):
    return jnp.dot(a, b, preferred_element_type=F32)


def dot_nt(a, b):
    return lax.dot_general(a, b, (((1,), (1,)), ((), ())), preferred_element_type=F32)


def whole(shape):
    return pl.BlockSpec(shape, lambda *_: (0,) * len(shape), pipeline_mode=pl.Buffered(1))


def kept(shape):
    return pl.BlockSpec(shape, lambda *_: (0,) * len(shape))


def row_blocks(rows, width):
    return pl.BlockSpec((rows, width), lambda i, *_: (i, 0))


def chunk_rows(ref, first, rows, chunk, pitch):
    return ref.at[pl.ds(first * pitch + chunk, rows, stride=pitch), :]


def gather_rows(places_ref, first_tile, tiles, source, target, pitch):
    def move(t, carry):
        for first in range(0, LANES, BATCH):
            lanes = range(first, first + BATCH)
            places = [places_ref[first_tile + t, l] for l in lanes]
            rows = [source[pl.ds(pl.multiple_of(p, pitch), pitch), :] for p in places]
            for l, row in zip(lanes, rows):
                target[pl.ds(pl.multiple_of((t * LANES + l) * pitch, pitch), pitch), :] = row
        return carry

    lax.fori_loop(0, tiles, move, 0)


def scatter_rows(places_ref, tiles, source, target, pitch):
    def move(t, carry):
        for first in range(0, LANES, BATCH):
            lanes = range(first, first + BATCH)
            places = [places_ref[t, l] for l in lanes]
            rows = [source[pl.ds(pl.multiple_of((t * LANES + l) * pitch, pitch), pitch), :] for l in lanes]
            for place, row in zip(places, rows):
                target[pl.ds(pl.multiple_of(place, pitch), pitch), :] = row
        return carry

    lax.fori_loop(0, tiles, move, 0)


def send_kernel(send_each, me_ref, index_ref, points_ref, out_ref, slot_ref, held, rows, sent, places, places_smem, arrivals, moved):
    rows_dev, width = held.shape
    tiles = rows_dev // LANES
    chunks = width // LANES
    per_tile = LANES // send_each
    peers = rows_dev // send_each
    step_peers = out_ref.shape[0]
    step = pl.program_id(0)

    @pl.when(step == 0)
    def _():
        pieces = [
            pltpu.make_async_copy(points_ref.at[pl.ds(k, DEPTH)], held.at[pl.ds(k, DEPTH)], arrivals.at[k // DEPTH])
            for k in range(0, rows_dev, DEPTH)
        ]
        for piece in pieces:
            piece.start()
        index = index_ref[...].astype(F32)
        dest = jnp.floor(index * (1.0 / rows_dev))
        local = index - dest * rows_dev
        high = jnp.floor(local * (1.0 / LOW))
        low = local - high * LOW
        row = lax.broadcasted_iota(jnp.int32, (LANES, LANES), 0)
        lane = lax.broadcasted_iota(jnp.int32, (LANES, LANES), 1)
        peer = lax.broadcasted_iota(jnp.int32, (peers, LANES), 0).astype(F32)
        member = [jnp.where(dest[t : t + 1, :] == peer, 1.0, 0.0) for t in range(tiles)]
        up_to = jnp.where(row <= lane, 1.0, 0.0).astype(BF16)
        counts = dot(jnp.concatenate(member, axis=0).astype(BF16), up_to)
        before = peer[:, 0:1] * send_each - 1.0
        for t in range(tiles):
            count = counts[t * peers : (t + 1) * peers, :]
            slot = jnp.sum(member[t] * (count + before), axis=0, keepdims=True)
            places[t : t + 1, :] = (slot * SEND_PITCH).astype(jnp.int32)
            slot_ref[t : t + 1, :] = (slot * chunks).astype(jnp.int32)
            before = before + count[:, LANES - 1 :]
        move = pltpu.make_async_copy(places, places_smem, moved.at[0])
        move.start()
        for t in range(tiles):
            pair = jnp.where(row == 0, high[t : t + 1, :], jnp.where(row == 1, low[t : t + 1, :], 0.0))
            chunk_rows(rows, t * LANES, LANES, chunks, SEND_PITCH)[...] = pair.T
        for k, piece in enumerate(pieces):
            piece.wait()
            for c in range(chunks):
                part = held[k * DEPTH : (k + 1) * DEPTH, c * LANES : (c + 1) * LANES]
                chunk_rows(rows, k * DEPTH, DEPTH, c, SEND_PITCH)[...] = part.astype(F32)
        move.wait()
        scatter_rows(places_smem, tiles, rows, sent, SEND_PITCH)

    base = step * (step_peers * send_each)
    for peer in range(step_peers):
        for c in range(chunks):
            part = chunk_rows(sent, base + peer * send_each, send_each, c, SEND_PITCH)[...]
            out_ref[peer, c * send_each : (c + 1) * send_each, :] = part.astype(BF16)
    for t in range(step_peers // per_tile):
        both = chunk_rows(sent, base + t * LANES, LANES, chunks, SEND_PITCH)[...].T[0:16, :]
        for v in range(per_tile):
            mine = both
            if per_tile > 1:
                lane = lax.broadcasted_iota(jnp.int32, both.shape, 1)
                mine = jnp.where(lane // send_each == v, both, 0.0)
                mine = pltpu.roll(mine, (me_ref[0] - v + per_tile) % per_tile * send_each, 1)
            out_ref[t * per_tile + v, chunks * send_each :, :] = mine.astype(BF16)


def send_order(points, index_tiles, me, peers):
    rows_dev, width = points.shape
    tiles = rows_dev // LANES
    send_each = rows_dev // peers
    payload = width // LANES * send_each + 16
    return pl.pallas_call(
        functools.partial(send_kernel, send_each),
        grid_spec=pltpu.PrefetchScalarGridSpec(
            num_scalar_prefetch=1,
            grid=(SEND_STEPS,),
            in_specs=[whole((tiles, LANES)), pl.BlockSpec(memory_space=pl.ANY)],
            out_specs=[
                pl.BlockSpec((peers // SEND_STEPS, payload, LANES), lambda i, *_: (i, 0, 0)),
                kept((tiles, LANES)),
            ],
            scratch_shapes=[
                pltpu.VMEM((rows_dev, width), BF16),
                pltpu.VMEM((rows_dev * SEND_PITCH, LANES), F32),
                pltpu.VMEM((rows_dev * SEND_PITCH, LANES), F32),
                pltpu.VMEM((tiles, LANES), jnp.int32),
                pltpu.SMEM((tiles, LANES), jnp.int32),
                pltpu.SemaphoreType.DMA((rows_dev // DEPTH,)),
                pltpu.SemaphoreType.DMA((1,)),
            ],
        ),
        out_shape=[
            jax.ShapeDtypeStruct((peers, payload, LANES), BF16),
            jax.ShapeDtypeStruct((tiles, LANES), jnp.int32),
        ],
        compiler_params=params(60),
        cost_estimate=pl.CostEstimate(
            flops=2 * rows_dev * rows_dev * width, bytes_accessed=4 * rows_dev * width, transcendentals=0
        ),
        name="send_order",
    )(me.reshape(1), index_tiles, points)


def normed_rows(rows32, gain):
    mean_square = jnp.mean(rows32 * rows32, axis=-1, keepdims=True)
    return (rows32 * lax.rsqrt(mean_square + 1e-05) * gain).astype(BF16)


def pool_kernel(arrived_ref, gain_ref, rows_ref, places_ref, pooled_ref, total):
    peers, payload, _ = arrived_ref.shape
    width = gain_ref.shape[1]
    chunks = width // LANES
    send_each = (payload - 16) // chunks
    per_tile = LANES // send_each
    tiles = peers // per_tile
    step = pl.program_id(0)

    @pl.when(step == 0)
    def _():
        total[...] = jnp.zeros_like(total)

    pool = lax.broadcasted_iota(jnp.int32, (total.shape[0], LANES), 0).astype(F32)
    picks = []
    normed = []
    for t in range(tiles):
        row = jnp.zeros((1, LANES), F32)
        for p in range(t * per_tile, (t + 1) * per_tile):
            both = arrived_ref[p, chunks * send_each :, :].astype(F32)
            row = row + both[0:1, :] * LOW + both[1:2, :]
        places_ref[pl.ds(step * tiles + t, 1), :] = (row * chunks).astype(jnp.int32)
        picks.append(jnp.where(jnp.floor(row * (1.0 / POOL)) == pool, 1.0 / POOL, 0.0).astype(BF16))
    for p in range(peers):
        parts = [arrived_ref[p, c * send_each : (c + 1) * send_each, :].astype(F32) for c in range(chunks)]
        for c in range(chunks):
            chunk_rows(rows_ref, p * send_each, send_each, c, chunks)[...] = parts[c]
        normed.append(normed_rows(jnp.concatenate(parts, axis=1), gain_ref[...]))
    total[...] += dot(jnp.concatenate(picks, axis=1), jnp.concatenate(normed, axis=0))

    @pl.when(step == pl.num_programs(0) - 1)
    def _():
        pooled_ref[...] = total[...].astype(BF16)


def pool(arrived, gain, rows_dev):
    width = gain.shape[1]
    chunks = width // LANES
    tiles = rows_dev // LANES
    peers, payload, _ = arrived.shape
    steps = rows_dev // TILE
    pooled = (rows_dev // POOL, width)
    return pl.pallas_call(
        pool_kernel,
        grid=(steps,),
        in_specs=[
            pl.BlockSpec((peers // steps, payload, LANES), lambda i: (i, 0, 0)),
            whole((1, width)),
        ],
        out_specs=[row_blocks(TILE * chunks, LANES), kept((tiles, LANES)), kept(pooled)],
        out_shape=[
            jax.ShapeDtypeStruct((rows_dev * chunks, LANES), F32),
            jax.ShapeDtypeStruct((tiles, LANES), jnp.int32),
            jax.ShapeDtypeStruct(pooled, BF16),
        ],
        scratch_shapes=[pltpu.VMEM(pooled, F32)],
        compiler_params=params(),
        cost_estimate=pl.CostEstimate(
            flops=rows_dev * rows_dev * width // 4, bytes_accessed=4 * rows_dev * width, transcendentals=0
        ),
        name="pool_arrived",
    )(arrived, gain)


def group_kernel(places_ref, rows_ref, gain_ref, grouped_ref, normed_ref, placed):
    count, width = grouped_ref.shape
    chunks = width // LANES
    step = pl.program_id(0)

    @pl.when(step == 0)
    def _():
        scatter_rows(places_ref, places_ref.shape[0], rows_ref, placed, chunks)

    grouped = jnp.concatenate(
        [chunk_rows(placed, step * count, count, c, chunks)[...] for c in range(chunks)], axis=1
    )
    grouped_ref[...] = grouped.astype(BF16)
    normed_ref[...] = normed_rows(grouped, gain_ref[...])


def group(places, rows, gain):
    width = gain.shape[1]
    rows_dev = rows.shape[0] * LANES // width
    blocks = row_blocks(TILE, width)
    return pl.pallas_call(
        group_kernel,
        grid_spec=pltpu.PrefetchScalarGridSpec(
            num_scalar_prefetch=1,
            grid=(rows_dev // TILE,),
            in_specs=[whole(rows.shape), whole((1, width))],
            out_specs=[blocks, blocks],
            scratch_shapes=[pltpu.VMEM(rows.shape, F32)],
        ),
        out_shape=[jax.ShapeDtypeStruct((rows_dev, width), BF16)] * 2,
        compiler_params=params(),
        cost_estimate=pl.CostEstimate(
            flops=2 * rows_dev * rows_dev * width, bytes_accessed=6 * rows_dev * width, transcendentals=0
        ),
        name="group_balls",
    )(places, rows, gain)


def block_matrix(rows, row_step, cols, col_step, value):
    row = lax.broadcasted_iota(jnp.int32, (rows, cols), 0) // row_step
    col = lax.broadcasted_iota(jnp.int32, (rows, cols), 1) // col_step
    return jnp.where(row == col, value, 0.0).astype(BF16)


def prepare(head_size, mean_of, queries, values):
    half = mean_of.shape[0]
    mean_of[...] = block_matrix(half, head_size, half, head_size, 1.0 / head_size)
    queries[...] = jnp.zeros_like(queries)
    values[...] = jnp.ones_like(values)


def normed_keys(keys, mean_of):
    half = mean_of.shape[0]
    square = (keys * keys).astype(BF16)
    mean_square = jnp.concatenate(
        [dot(square[:, c : c + half], mean_of[...]) for c in range(0, keys.shape[1], half)], axis=1
    )
    return (keys * lax.rsqrt(mean_square + 1e-06)).astype(BF16)


def spread_head(h, head_size, columns, queries):
    count = columns.shape[1]
    per_group = LANES // head_size
    g, j = h // per_group, h % per_group
    queries[g, j * head_size : (j + 1) * head_size, j * count : (j + 1) * count] = columns


def weigh(key_rows, queries, weights):
    for g in range(queries.shape[0]):
        score = dot(key_rows[:, g * LANES : (g + 1) * LANES], queries[g])
        weights[g] = jnp.exp2(score).astype(BF16)


def head_sums(g, head_size, values, weights):
    per_group = LANES // head_size
    both = dot(values[g], weights[g])
    count = both.shape[1] // per_group
    for j in range(per_group):
        cols = slice(j * count, (j + 1) * count)
        yield g * per_group + j, both[j * head_size : (j + 1) * head_size, cols], both[LANES : LANES + 1, cols]


def local_kernel(head_size, scale_ref, normed_ref, wq_ref, wk_ref, wv_ref, *rest):
    query_ref, num_ref, den_ref, mean_of, queries, values, weights = rest[-7:]
    width = normed_ref.shape[1]
    groups = width // LANES
    balls = queries.shape[0]

    @pl.when(pl.program_id(0) == 0)
    def _():
        prepare(head_size, mean_of, queries, values)

    normed = normed_ref[...]
    query = dot_nt(wq_ref[...], normed)
    key_rows = normed_keys(dot(normed, wk_ref[...]), mean_of)
    value = dot_nt(wv_ref[...], normed).astype(BF16)
    for h in range(width // head_size):
        rows = slice(h * head_size, (h + 1) * head_size)
        part = query[rows, :]
        root = lax.rsqrt(jnp.mean(part * part, axis=0, keepdims=True) + 1e-06)
        part = (part * (root * scale_ref[h])).astype(BF16)
        query_ref[rows, :] = part
        for b in range(balls):
            spread_head(h, head_size, part[:, b * BALL : (b + 1) * BALL], queries.at[b])
    for b in range(balls):
        cols = slice(b * BALL, (b + 1) * BALL)
        for g in range(groups):
            values[b, g, :LANES, :] = value[g * LANES : (g + 1) * LANES, cols]
        weigh(key_rows[cols, :], queries.at[b], weights.at[b])
    for b in range(balls):
        cols = slice(b * BALL, (b + 1) * BALL)
        for g in range(groups):
            for h, num, den in head_sums(g, head_size, values.at[b], weights.at[b]):
                num_ref[h * head_size : (h + 1) * head_size, cols] = num.astype(BF16)
                den_ref[h : h + 1, cols] = den


def local_attention(first, last, normed, wq, wk, wv, scale, head_size, earlier=()):
    rows_dev, width = normed.shape
    square = whole((width, width))
    groups = width // LANES
    heads = width // head_size
    spread = LANES // head_size * BALL
    balls = math.gcd(math.gcd(first, last), 2)
    steps = (last - first) // balls
    at = lambda i: first // balls + i
    columns = lambda count: pl.BlockSpec((count, balls * BALL), lambda i: (0, at(i)))
    return pl.pallas_call(
        functools.partial(local_kernel, head_size),
        grid=(steps,),
        in_specs=[
            pl.BlockSpec(memory_space=pltpu.SMEM),
            pl.BlockSpec((balls * BALL, width), lambda i: (at(i), 0)),
            square,
            square,
            square,
        ]
        + [pl.BlockSpec(memory_space=pl.ANY)] * len(earlier),
        out_specs=[columns(width), columns(width), columns(heads)],
        out_shape=[
            jax.ShapeDtypeStruct((width, rows_dev), BF16),
            jax.ShapeDtypeStruct((width, rows_dev), BF16),
            jax.ShapeDtypeStruct((heads, rows_dev), F32),
        ],
        scratch_shapes=[
            pltpu.VMEM((2 * LANES, 2 * LANES), BF16),
            pltpu.VMEM((balls, groups, LANES, spread), BF16),
            pltpu.VMEM((balls, groups, LANES + 16, BALL), BF16),
            pltpu.VMEM((balls, groups, BALL, spread), BF16),
        ],
        input_output_aliases={5 + k: k for k in range(len(earlier))},
        compiler_params=params(),
        cost_estimate=pl.CostEstimate(
            flops=20 * (last - first) * BALL * width * width,
            bytes_accessed=12 * (last - first) * BALL * width,
            transcendentals=0,
        ),
        name="local_attention",
    )(scale, normed, wq, wk, wv, *earlier)


def finish_kernel(
    head_size,
    chosen_ref,
    places_ref,
    candidates_ref,
    query_ref,
    num_ref,
    den_ref,
    grouped_ref,
    wpk_ref,
    wpv_ref,
    wo_ref,
    gain_ref,
    wg_ref,
    wu_ref,
    wd_ref,
    out_ref,
    mean_of,
    queries,
    values,
    weights,
    attended,
    rows,
    taken,
):
    step = pl.program_id(0)
    steps = pl.num_programs(0) - TAKE_STEPS
    width, step_rows = attended.shape
    chunks = width // LANES

    @pl.when(step < steps)
    def _():
        result = balls_step(
            head_size, step, chosen_ref, candidates_ref, query_ref, num_ref, den_ref, grouped_ref, wpk_ref,
            wpv_ref, wo_ref, gain_ref, wg_ref, wu_ref, wd_ref, mean_of, queries, values, weights, attended,
        )
        for c in range(chunks):
            part = result[:, c * LANES : (c + 1) * LANES].astype(BF16).astype(F32)
            chunk_rows(rows, step * step_rows, step_rows, c, chunks)[...] = part

    @pl.when(step >= steps)
    def _():
        take_block(places_ref, step - steps, rows, taken, out_ref)


def take_block(places_ref, block, rows, taken, out_ref):
    count, width = out_ref.shape
    chunks = width // LANES
    gather_rows(places_ref, block * (count // LANES), count // LANES, rows, taken, chunks)
    for c in range(chunks):
        out_ref[:, c * LANES : (c + 1) * LANES] = chunk_rows(taken, 0, count, c, chunks)[...].astype(BF16)


def balls_step(
    head_size,
    step,
    chosen_ref,
    candidates_ref,
    query_ref,
    num_ref,
    den_ref,
    grouped_ref,
    wpk_ref,
    wpv_ref,
    wo_ref,
    gain_ref,
    wg_ref,
    wu_ref,
    wd_ref,
    mean_of,
    queries,
    values,
    weights,
    attended,
):
    groups = wo_ref.shape[0] // LANES
    far = OWNERS * BALL // POOL

    @pl.when(step == 0)
    def _():
        prepare(head_size, mean_of, queries, values)

    first = step * BALLS_STEP * OWNERS
    coarse = jnp.concatenate(
        [candidates_ref[chosen_ref[first + o]] for o in range(BALLS_STEP * OWNERS)], axis=0
    )
    key_rows = normed_keys(dot(coarse, wpk_ref[...]), mean_of)
    value = dot_nt(wpv_ref[...], coarse).astype(BF16)
    for b in range(BALLS_STEP):
        cols = slice(b * BALL, (b + 1) * BALL)
        for h in range(groups * LANES // head_size):
            spread_head(h, head_size, query_ref[h * head_size : (h + 1) * head_size, cols], queries.at[b % 2])
        for g in range(groups):
            values[b, g, :LANES, :] = value[g * LANES : (g + 1) * LANES, b * far : (b + 1) * far]
        weigh(key_rows[b * far : (b + 1) * far, :], queries.at[b % 2], weights.at[b])
    for b in range(BALLS_STEP):
        cols = slice(b * BALL, (b + 1) * BALL)
        for g in range(groups):
            for h, num, den in head_sums(g, head_size, values.at[b], weights.at[b]):
                rows = slice(h * head_size, (h + 1) * head_size)
                num = num + num_ref[rows, cols].astype(F32)
                attended[rows, cols] = (num * (1.0 / (den + den_ref[h : h + 1, cols]))).astype(BF16)
    projected = dot(attended[...].T, wo_ref[...])
    residual = (grouped_ref[...].astype(F32) + projected).astype(BF16)
    rows32 = residual.astype(F32)
    ffn = normed_rows(rows32, gain_ref[...])
    parts = []
    for first_col in range(0, wg_ref.shape[1], 2 * LANES):
        cols = slice(first_col, first_col + 2 * LANES)
        gate = dot(ffn, wg_ref[:, cols])
        up = dot(ffn, wu_ref[:, cols])
        parts.append((0.5 * gate * (1.0 + jnp.tanh(0.5 * gate)) * up).astype(BF16))
    hidden = jnp.concatenate(parts, axis=1)
    return rows32 + dot(hidden, wd_ref[...])


def finish(chosen, places, candidates, query, num, den, grouped, wpk, wpv, wo, gain, wg, wu, wd, head_size):
    rows_dev, width = grouped.shape
    hidden = wg.shape[1]
    groups = width // LANES
    step_rows = BALLS_STEP * BALL
    spread = LANES // head_size * BALL
    far = OWNERS * BALL // POOL
    steps = rows_dev // step_rows
    rows = pl.BlockSpec((step_rows, width), lambda i, *_: (jnp.minimum(i, steps - 1), 0))
    columns = lambda count: pl.BlockSpec((count, step_rows), lambda i, *_: (0, jnp.minimum(i, steps - 1)))
    take_rows = rows_dev // TAKE_STEPS
    fixed = [wpk, wpv, wo, gain, wg, wu, wd]
    return pl.pallas_call(
        functools.partial(finish_kernel, head_size),
        grid_spec=pltpu.PrefetchScalarGridSpec(
            num_scalar_prefetch=2,
            grid=(steps + TAKE_STEPS,),
            in_specs=[
                whole(candidates.shape),
                columns(width),
                columns(width),
                columns(width // head_size),
                rows,
            ]
            + [whole(a.shape) for a in fixed],
            out_specs=pl.BlockSpec((take_rows, width), lambda i, *_: (jnp.maximum(i - steps, 0), 0)),
            scratch_shapes=[
                pltpu.VMEM((2 * LANES, 2 * LANES), BF16),
                pltpu.VMEM((2, groups, LANES, spread), BF16),
                pltpu.VMEM((BALLS_STEP, groups, LANES + 16, far), BF16),
                pltpu.VMEM((BALLS_STEP, groups, far, spread), BF16),
                pltpu.VMEM((width, step_rows), BF16),
                pltpu.VMEM((rows_dev * (width // LANES), LANES), F32),
                pltpu.VMEM((take_rows * (width // LANES), LANES), F32),
            ],
        ),
        out_shape=jax.ShapeDtypeStruct((rows_dev, width), BF16),
        compiler_params=params(),
        cost_estimate=pl.CostEstimate(
            flops=2 * rows_dev * width * (3 * hidden + 6 * width),
            bytes_accessed=12 * rows_dev * width,
            transcendentals=0,
        ),
        name="finish_balls",
    )(chosen, places, candidates, query, num, den, grouped, *fixed)


def take_kernel(places_ref, source_ref, out_ref, rows, taken):
    count, width = source_ref.shape
    chunks = width // LANES

    @pl.when(pl.program_id(0) == 0)
    def _():
        for first in range(0, count, DEPTH):
            for c in range(chunks):
                part = source_ref[first : first + DEPTH, c * LANES : (c + 1) * LANES]
                chunk_rows(rows, first, DEPTH, c, chunks)[...] = part.astype(F32)

    take_block(places_ref, pl.program_id(0), rows, taken, out_ref)


def take_rows(places, source):
    rows_dev, width = source.shape
    chunks = width // LANES
    return pl.pallas_call(
        take_kernel,
        grid_spec=pltpu.PrefetchScalarGridSpec(
            num_scalar_prefetch=1,
            grid=(rows_dev // TILE,),
            in_specs=[whole(source.shape)],
            out_specs=row_blocks(TILE, width),
            scratch_shapes=[
                pltpu.VMEM((rows_dev * chunks, LANES), F32),
                pltpu.VMEM((TILE * chunks, LANES), F32),
            ],
        ),
        out_shape=jax.ShapeDtypeStruct((rows_dev, width), BF16),
        compiler_params=params(),
        cost_estimate=pl.CostEstimate(
            flops=2 * rows_dev * rows_dev * width, bytes_accessed=4 * rows_dev * width, transcendentals=0
        ),
        name="take_rows",
    )(places, source)


def route(block, target):
    devices = range(lax.axis_size("pts"))
    return lax.ppermute(block, "pts", [(i, target(i) % len(devices)) for i in devices])


def to_mate(block, mate):
    return route(block, lambda i: i ^ mate)


SLOT_INSIDE = (0, 5, 1, 6)
SLOT_OUTSIDE = (2, 7, 4, 8)


def block_slots(owner, me, peers):
    mate = (owner % GROUP) ^ (me % GROUP)
    ahead = jnp.mod(owner // GROUP - me // GROUP, peers // GROUP)
    pick = lambda table: sum(jnp.where(mate == m, table[m], 0) for m in range(GROUP))
    second = (mate == 0) & ((ahead == 1) != (me % GROUP < 2))
    return jnp.where(ahead == 0, pick(SLOT_INSIDE), pick(SLOT_OUTSIDE) + jnp.where(second, 1, 0))


def on_device(
    points,
    point_row_index,
    neighbour_ball_list,
    attention_norm_gain,
    query_weight,
    key_weight,
    value_weight,
    pooled_key_weight,
    pooled_value_weight,
    head_score_scale,
    output_weight,
    feedforward_norm_gain,
    gate_weight,
    up_weight,
    down_weight,
):
    rows_dev, width = points.shape
    head_size = width // head_score_scale.shape[0]
    peers = lax.axis_size("pts")
    me = lax.axis_index("pts")
    send_each = rows_dev // peers
    blocks_dev = rows_dev // BALL
    comp = BALL // POOL

    def swap(array):
        return lax.all_to_all(array, "pts", split_axis=0, concat_axis=0, tiled=True)

    outgoing, slot = send_order(points, point_row_index.reshape(rows_dev // LANES, LANES), me, peers)
    rows, places, pooled = pool(swap(outgoing), attention_norm_gain[None], rows_dev)
    up = lambda i: i % GROUP >= 2
    first = route(pooled, lambda i: i + GROUP if up(i) else i - GROUP)
    other = route(pooled, lambda i: i - GROUP if up(i) else i + GROUP)
    beside = to_mate(pooled, 2)
    grouped, normed = group(places, rows, attention_norm_gain[None])
    scale = head_score_scale * (LOG2E / head_size)
    attend = functools.partial(
        local_attention,
        normed=normed,
        wq=query_weight.T,
        wk=key_weight,
        wv=value_weight.T,
        scale=scale,
        head_size=head_size,
    )
    soon, early = blocks_dev // 4, blocks_dev * 3 // 4
    part = attend(0, soon)
    first, part = lax.optimization_barrier((first, part))
    handed = to_mate(first, 2)
    part = attend(soon, early, earlier=part)
    first, other, beside, handed, part = lax.optimization_barrier((first, other, beside, handed, part))
    place = me % GROUP
    held = jnp.stack([pooled, beside, jnp.where(place // 2 == place % 2, first, other), handed])
    near = to_mate(held, 1)
    query, num, den = attend(early, blocks_dev, earlier=part)
    candidates = jnp.concatenate([jnp.stack([pooled, beside, first, other, handed]), near])
    candidates = candidates.reshape(candidates.shape[0] * blocks_dev, comp, width)
    slots = block_slots(neighbour_ball_list // blocks_dev, me, peers)
    chosen = (slots * blocks_dev + neighbour_ball_list % blocks_dev).reshape(-1)
    returning = finish(
        chosen,
        places,
        candidates,
        query,
        num,
        den,
        grouped,
        pooled_key_weight,
        pooled_value_weight.T,
        output_weight,
        feedforward_norm_gain[None],
        gate_weight,
        up_weight,
        down_weight,
        head_size,
    )
    came_back = swap(returning.reshape(peers, send_each, width)).reshape(rows_dev, width)
    return take_rows(slot, came_back)


def solution(mesh):
    rows = P(("rep", "pts"), None)
    return jax.shard_map(
        on_device,
        mesh=mesh,
        in_specs=(rows, P(("rep", "pts")), rows) + (P(),) * 12,
        out_specs=rows,
        check_vma=False,
    )
```

```python
import functools
import math

import jax
import jax.numpy as jnp
from jax import lax
from jax.experimental import pallas as pl
from jax.experimental.pallas import tpu as pltpu
from jax.sharding import PartitionSpec as P

BALL = 256
POOL = 8
OWNERS = 4
GROUP = 4
LANES = 128
BATCH = 32
TILE = 1024
DEPTH = 256
BALLS_STEP = 4
LOW = 64
SEND_PITCH = 8
SEND_STEPS = 2
TAKE_STEPS = 2
LOG2E = math.log2(math.e)
F32 = jnp.float32
BF16 = jnp.bfloat16


def params(mebibytes=28):
    return pltpu.CompilerParams(vmem_limit_bytes=mebibytes * 1024 * 1024)


def dot(a, b):
    return jnp.dot(a, b, preferred_element_type=F32)


def dot_nt(a, b):
    return lax.dot_general(a, b, (((1,), (1,)), ((), ())), preferred_element_type=F32)


def whole(shape):
    return pl.BlockSpec(shape, lambda *_: (0,) * len(shape), pipeline_mode=pl.Buffered(1))


def kept(shape):
    return pl.BlockSpec(shape, lambda *_: (0,) * len(shape))


def row_blocks(rows, width):
    return pl.BlockSpec((rows, width), lambda i, *_: (i, 0))


def chunk_rows(ref, first, rows, chunk, pitch):
    return ref.at[pl.ds(first * pitch + chunk, rows, stride=pitch), :]


def gather_rows(places_ref, first_tile, tiles, source, target, pitch):
    def move(t, carry):
        for first in range(0, LANES, BATCH):
            lanes = range(first, first + BATCH)
            places = [places_ref[first_tile + t, l] for l in lanes]
            rows = [source[pl.ds(pl.multiple_of(p, pitch), pitch), :] for p in places]
            for l, row in zip(lanes, rows):
                target[pl.ds(pl.multiple_of((t * LANES + l) * pitch, pitch), pitch), :] = row
        return carry

    lax.fori_loop(0, tiles, move, 0)


def scatter_rows(places_ref, tiles, source, target, pitch):
    def move(t, carry):
        for first in range(0, LANES, BATCH):
            lanes = range(first, first + BATCH)
            places = [places_ref[t, l] for l in lanes]
            rows = [source[pl.ds(pl.multiple_of((t * LANES + l) * pitch, pitch), pitch), :] for l in lanes]
            for place, row in zip(places, rows):
                target[pl.ds(pl.multiple_of(place, pitch), pitch), :] = row
        return carry

    lax.fori_loop(0, tiles, move, 0)


def send_kernel(send_each, me_ref, index_ref, points_ref, out_ref, slot_ref, held, rows, sent, places, places_smem, arrivals, moved):
    rows_dev, width = held.shape
    tiles = rows_dev // LANES
    chunks = width // LANES
    per_tile = LANES // send_each
    peers = rows_dev // send_each
    step_peers = out_ref.shape[0]
    step = pl.program_id(0)

    @pl.when(step == 0)
    def _():
        pieces = [
            pltpu.make_async_copy(points_ref.at[pl.ds(k, DEPTH)], held.at[pl.ds(k, DEPTH)], arrivals.at[k // DEPTH])
            for k in range(0, rows_dev, DEPTH)
        ]
        for piece in pieces:
            piece.start()
        index = index_ref[...].astype(F32)
        dest = jnp.floor(index * (1.0 / rows_dev))
        local = index - dest * rows_dev
        high = jnp.floor(local * (1.0 / LOW))
        low = local - high * LOW
        row = lax.broadcasted_iota(jnp.int32, (LANES, LANES), 0)
        lane = lax.broadcasted_iota(jnp.int32, (LANES, LANES), 1)
        peer = lax.broadcasted_iota(jnp.int32, (peers, LANES), 0).astype(F32)
        member = [jnp.where(dest[t : t + 1, :] == peer, 1.0, 0.0) for t in range(tiles)]
        up_to = jnp.where(row <= lane, 1.0, 0.0).astype(BF16)
        counts = dot(jnp.concatenate(member, axis=0).astype(BF16), up_to)
        before = peer[:, 0:1] * send_each - 1.0
        for t in range(tiles):
            count = counts[t * peers : (t + 1) * peers, :]
            slot = jnp.sum(member[t] * (count + before), axis=0, keepdims=True)
            places[t : t + 1, :] = (slot * SEND_PITCH).astype(jnp.int32)
            slot_ref[t : t + 1, :] = (slot * chunks).astype(jnp.int32)
            before = before + count[:, LANES - 1 :]
        move = pltpu.make_async_copy(places, places_smem, moved.at[0])
        move.start()
        for t in range(tiles):
            pair = jnp.where(row == 0, high[t : t + 1, :], jnp.where(row == 1, low[t : t + 1, :], 0.0))
            chunk_rows(rows, t * LANES, LANES, chunks, SEND_PITCH)[...] = pair.T
        for k, piece in enumerate(pieces):
            piece.wait()
            for c in range(chunks):
                part = held[k * DEPTH : (k + 1) * DEPTH, c * LANES : (c + 1) * LANES]
                chunk_rows(rows, k * DEPTH, DEPTH, c, SEND_PITCH)[...] = part.astype(F32)
        move.wait()
        scatter_rows(places_smem, tiles, rows, sent, SEND_PITCH)

    base = step * (step_peers * send_each)
    for peer in range(step_peers):
        for c in range(chunks):
            part = chunk_rows(sent, base + peer * send_each, send_each, c, SEND_PITCH)[...]
            out_ref[peer, c * send_each : (c + 1) * send_each, :] = part.astype(BF16)
    for t in range(step_peers // per_tile):
        both = chunk_rows(sent, base + t * LANES, LANES, chunks, SEND_PITCH)[...].T[0:16, :]
        for v in range(per_tile):
            mine = both
            if per_tile > 1:
                lane = lax.broadcasted_iota(jnp.int32, both.shape, 1)
                mine = jnp.where(lane // send_each == v, both, 0.0)
                mine = pltpu.roll(mine, (me_ref[0] - v + per_tile) % per_tile * send_each, 1)
            out_ref[t * per_tile + v, chunks * send_each :, :] = mine.astype(BF16)


def send_order(points, index_tiles, me, peers):
    rows_dev, width = points.shape
    tiles = rows_dev // LANES
    send_each = rows_dev // peers
    payload = width // LANES * send_each + 16
    return pl.pallas_call(
        functools.partial(send_kernel, send_each),
        grid_spec=pltpu.PrefetchScalarGridSpec(
            num_scalar_prefetch=1,
            grid=(SEND_STEPS,),
            in_specs=[whole((tiles, LANES)), pl.BlockSpec(memory_space=pl.ANY)],
            out_specs=[
                pl.BlockSpec((peers // SEND_STEPS, payload, LANES), lambda i, *_: (i, 0, 0)),
                kept((tiles, LANES)),
            ],
            scratch_shapes=[
                pltpu.VMEM((rows_dev, width), BF16),
                pltpu.VMEM((rows_dev * SEND_PITCH, LANES), F32),
                pltpu.VMEM((rows_dev * SEND_PITCH, LANES), F32),
                pltpu.VMEM((tiles, LANES), jnp.int32),
                pltpu.SMEM((tiles, LANES), jnp.int32),
                pltpu.SemaphoreType.DMA((rows_dev // DEPTH,)),
                pltpu.SemaphoreType.DMA((1,)),
            ],
        ),
        out_shape=[
            jax.ShapeDtypeStruct((peers, payload, LANES), BF16),
            jax.ShapeDtypeStruct((tiles, LANES), jnp.int32),
        ],
        compiler_params=params(60),
        cost_estimate=pl.CostEstimate(
            flops=2 * rows_dev * rows_dev * width, bytes_accessed=4 * rows_dev * width, transcendentals=0
        ),
        name="send_order",
    )(me.reshape(1), index_tiles, points)


def normed_rows(rows32, gain):
    mean_square = jnp.mean(rows32 * rows32, axis=-1, keepdims=True)
    return (rows32 * lax.rsqrt(mean_square + 1e-05) * gain).astype(BF16)


def pool_kernel(arrived_ref, gain_ref, rows_ref, places_ref, pooled_ref, total):
    peers, payload, _ = arrived_ref.shape
    width = gain_ref.shape[1]
    chunks = width // LANES
    send_each = (payload - 16) // chunks
    per_tile = LANES // send_each
    tiles = peers // per_tile
    step = pl.program_id(0)

    @pl.when(step == 0)
    def _():
        total[...] = jnp.zeros_like(total)

    pool = lax.broadcasted_iota(jnp.int32, (total.shape[0], LANES), 0).astype(F32)
    picks = []
    normed = []
    for t in range(tiles):
        row = jnp.zeros((1, LANES), F32)
        for p in range(t * per_tile, (t + 1) * per_tile):
            both = arrived_ref[p, chunks * send_each :, :].astype(F32)
            row = row + both[0:1, :] * LOW + both[1:2, :]
        places_ref[pl.ds(step * tiles + t, 1), :] = (row * chunks).astype(jnp.int32)
        picks.append(jnp.where(jnp.floor(row * (1.0 / POOL)) == pool, 1.0 / POOL, 0.0).astype(BF16))
    for p in range(peers):
        parts = [arrived_ref[p, c * send_each : (c + 1) * send_each, :].astype(F32) for c in range(chunks)]
        for c in range(chunks):
            chunk_rows(rows_ref, p * send_each, send_each, c, chunks)[...] = parts[c]
        normed.append(normed_rows(jnp.concatenate(parts, axis=1), gain_ref[...]))
    total[...] += dot(jnp.concatenate(picks, axis=1), jnp.concatenate(normed, axis=0))

    @pl.when(step == pl.num_programs(0) - 1)
    def _():
        pooled_ref[...] = total[...].astype(BF16)


def pool(arrived, gain, rows_dev):
    width = gain.shape[1]
    chunks = width // LANES
    tiles = rows_dev // LANES
    peers, payload, _ = arrived.shape
    steps = rows_dev // TILE
    pooled = (rows_dev // POOL, width)
    return pl.pallas_call(
        pool_kernel,
        grid=(steps,),
        in_specs=[
            pl.BlockSpec((peers // steps, payload, LANES), lambda i: (i, 0, 0)),
            whole((1, width)),
        ],
        out_specs=[row_blocks(TILE * chunks, LANES), kept((tiles, LANES)), kept(pooled)],
        out_shape=[
            jax.ShapeDtypeStruct((rows_dev * chunks, LANES), F32),
            jax.ShapeDtypeStruct((tiles, LANES), jnp.int32),
            jax.ShapeDtypeStruct(pooled, BF16),
        ],
        scratch_shapes=[pltpu.VMEM(pooled, F32)],
        compiler_params=params(),
        cost_estimate=pl.CostEstimate(
            flops=rows_dev * rows_dev * width // 4, bytes_accessed=4 * rows_dev * width, transcendentals=0
        ),
        name="pool_arrived",
    )(arrived, gain)


def group_kernel(places_ref, rows_ref, gain_ref, grouped_ref, normed_ref, placed):
    count, width = grouped_ref.shape
    chunks = width // LANES
    step = pl.program_id(0)

    @pl.when(step == 0)
    def _():
        scatter_rows(places_ref, places_ref.shape[0], rows_ref, placed, chunks)

    grouped = jnp.concatenate(
        [chunk_rows(placed, step * count, count, c, chunks)[...] for c in range(chunks)], axis=1
    )
    grouped_ref[...] = grouped.astype(BF16)
    normed_ref[...] = normed_rows(grouped, gain_ref[...])


def group(places, rows, gain):
    width = gain.shape[1]
    rows_dev = rows.shape[0] * LANES // width
    blocks = row_blocks(TILE, width)
    return pl.pallas_call(
        group_kernel,
        grid_spec=pltpu.PrefetchScalarGridSpec(
            num_scalar_prefetch=1,
            grid=(rows_dev // TILE,),
            in_specs=[whole(rows.shape), whole((1, width))],
            out_specs=[blocks, blocks],
            scratch_shapes=[pltpu.VMEM(rows.shape, F32)],
        ),
        out_shape=[jax.ShapeDtypeStruct((rows_dev, width), BF16)] * 2,
        compiler_params=params(),
        cost_estimate=pl.CostEstimate(
            flops=2 * rows_dev * rows_dev * width, bytes_accessed=6 * rows_dev * width, transcendentals=0
        ),
        name="group_balls",
    )(places, rows, gain)


def block_matrix(rows, row_step, cols, col_step, value):
    row = lax.broadcasted_iota(jnp.int32, (rows, cols), 0) // row_step
    col = lax.broadcasted_iota(jnp.int32, (rows, cols), 1) // col_step
    return jnp.where(row == col, value, 0.0).astype(BF16)


def prepare(head_size, mean_of, queries, values):
    half = mean_of.shape[0]
    mean_of[...] = block_matrix(half, head_size, half, head_size, 1.0 / head_size)
    queries[...] = jnp.zeros_like(queries)
    values[...] = jnp.ones_like(values)


def normed_keys(keys, mean_of):
    half = mean_of.shape[0]
    square = (keys * keys).astype(BF16)
    mean_square = jnp.concatenate(
        [dot(square[:, c : c + half], mean_of[...]) for c in range(0, keys.shape[1], half)], axis=1
    )
    return (keys * lax.rsqrt(mean_square + 1e-06)).astype(BF16)


def spread_head(h, head_size, columns, queries):
    count = columns.shape[1]
    per_group = LANES // head_size
    g, j = h // per_group, h % per_group
    queries[g, j * head_size : (j + 1) * head_size, j * count : (j + 1) * count] = columns


def weigh(key_rows, queries, weights):
    for g in range(queries.shape[0]):
        score = dot(key_rows[:, g * LANES : (g + 1) * LANES], queries[g])
        weights[g] = jnp.exp2(score).astype(BF16)


def head_sums(g, head_size, values, weights):
    per_group = LANES // head_size
    both = dot(values[g], weights[g])
    count = both.shape[1] // per_group
    for j in range(per_group):
        cols = slice(j * count, (j + 1) * count)
        yield g * per_group + j, both[j * head_size : (j + 1) * head_size, cols], both[LANES : LANES + 1, cols]


def local_kernel(head_size, scale_ref, normed_ref, wq_ref, wk_ref, wv_ref, *rest):
    query_ref, num_ref, den_ref, mean_of, queries, values, weights = rest[-7:]
    width = normed_ref.shape[1]
    groups = width // LANES
    balls = queries.shape[0]

    @pl.when(pl.program_id(0) == 0)
    def _():
        prepare(head_size, mean_of, queries, values)

    normed = normed_ref[...]
    query = dot_nt(wq_ref[...], normed)
    key_rows = normed_keys(dot(normed, wk_ref[...]), mean_of)
    value = dot_nt(wv_ref[...], normed).astype(BF16)
    for h in range(width // head_size):
        rows = slice(h * head_size, (h + 1) * head_size)
        part = query[rows, :]
        root = lax.rsqrt(jnp.mean(part * part, axis=0, keepdims=True) + 1e-06)
        part = (part * (root * scale_ref[h])).astype(BF16)
        query_ref[rows, :] = part
        for b in range(balls):
            spread_head(h, head_size, part[:, b * BALL : (b + 1) * BALL], queries.at[b])
    for b in range(balls):
        cols = slice(b * BALL, (b + 1) * BALL)
        for g in range(groups):
            values[b, g, :LANES, :] = value[g * LANES : (g + 1) * LANES, cols]
        weigh(key_rows[cols, :], queries.at[b], weights.at[b])
    for b in range(balls):
        cols = slice(b * BALL, (b + 1) * BALL)
        for g in range(groups):
            for h, num, den in head_sums(g, head_size, values.at[b], weights.at[b]):
                num_ref[h * head_size : (h + 1) * head_size, cols] = num.astype(BF16)
                den_ref[h : h + 1, cols] = den


def local_attention(first, last, normed, wq, wk, wv, scale, head_size, earlier=()):
    rows_dev, width = normed.shape
    square = whole((width, width))
    groups = width // LANES
    heads = width // head_size
    spread = LANES // head_size * BALL
    balls = math.gcd(math.gcd(first, last), 2)
    steps = (last - first) // balls
    at = lambda i: first // balls + i
    columns = lambda count: pl.BlockSpec((count, balls * BALL), lambda i: (0, at(i)))
    return pl.pallas_call(
        functools.partial(local_kernel, head_size),
        grid=(steps,),
        in_specs=[
            pl.BlockSpec(memory_space=pltpu.SMEM),
            pl.BlockSpec((balls * BALL, width), lambda i: (at(i), 0)),
            square,
            square,
            square,
        ]
        + [pl.BlockSpec(memory_space=pl.ANY)] * len(earlier),
        out_specs=[columns(width), columns(width), columns(heads)],
        out_shape=[
            jax.ShapeDtypeStruct((width, rows_dev), BF16),
            jax.ShapeDtypeStruct((width, rows_dev), BF16),
            jax.ShapeDtypeStruct((heads, rows_dev), F32),
        ],
        scratch_shapes=[
            pltpu.VMEM((2 * LANES, 2 * LANES), BF16),
            pltpu.VMEM((balls, groups, LANES, spread), BF16),
            pltpu.VMEM((balls, groups, LANES + 16, BALL), BF16),
            pltpu.VMEM((balls, groups, BALL, spread), BF16),
        ],
        input_output_aliases={5 + k: k for k in range(len(earlier))},
        compiler_params=params(),
        cost_estimate=pl.CostEstimate(
            flops=20 * (last - first) * BALL * width * width,
            bytes_accessed=12 * (last - first) * BALL * width,
            transcendentals=0,
        ),
        name="local_attention",
    )(scale, normed, wq, wk, wv, *earlier)


def finish_kernel(
    head_size,
    chosen_ref,
    places_ref,
    candidates_ref,
    query_ref,
    num_ref,
    den_ref,
    grouped_ref,
    wpk_ref,
    wpv_ref,
    wo_ref,
    gain_ref,
    wg_ref,
    wu_ref,
    wd_ref,
    out_ref,
    mean_of,
    queries,
    values,
    weights,
    attended,
    rows,
    taken,
):
    step = pl.program_id(0)
    steps = pl.num_programs(0) - TAKE_STEPS
    width, step_rows = attended.shape
    chunks = width // LANES

    @pl.when(step < steps)
    def _():
        result = balls_step(
            head_size, step, chosen_ref, candidates_ref, query_ref, num_ref, den_ref, grouped_ref, wpk_ref,
            wpv_ref, wo_ref, gain_ref, wg_ref, wu_ref, wd_ref, mean_of, queries, values, weights, attended,
        )
        for c in range(chunks):
            part = result[:, c * LANES : (c + 1) * LANES].astype(BF16).astype(F32)
            chunk_rows(rows, step * step_rows, step_rows, c, chunks)[...] = part

    @pl.when(step >= steps)
    def _():
        take_block(places_ref, step - steps, rows, taken, out_ref)


def take_block(places_ref, block, rows, taken, out_ref):
    count, width = out_ref.shape
    chunks = width // LANES
    gather_rows(places_ref, block * (count // LANES), count // LANES, rows, taken, chunks)
    for c in range(chunks):
        out_ref[:, c * LANES : (c + 1) * LANES] = chunk_rows(taken, 0, count, c, chunks)[...].astype(BF16)


def balls_step(
    head_size,
    step,
    chosen_ref,
    candidates_ref,
    query_ref,
    num_ref,
    den_ref,
    grouped_ref,
    wpk_ref,
    wpv_ref,
    wo_ref,
    gain_ref,
    wg_ref,
    wu_ref,
    wd_ref,
    mean_of,
    queries,
    values,
    weights,
    attended,
):
    groups = wo_ref.shape[0] // LANES
    far = OWNERS * BALL // POOL

    @pl.when(step == 0)
    def _():
        prepare(head_size, mean_of, queries, values)

    first = step * BALLS_STEP * OWNERS
    coarse = jnp.concatenate(
        [candidates_ref[chosen_ref[first + o]] for o in range(BALLS_STEP * OWNERS)], axis=0
    )
    key_rows = normed_keys(dot(coarse, wpk_ref[...]), mean_of)
    value = dot_nt(wpv_ref[...], coarse).astype(BF16)
    for b in range(BALLS_STEP):
        cols = slice(b * BALL, (b + 1) * BALL)
        for h in range(groups * LANES // head_size):
            spread_head(h, head_size, query_ref[h * head_size : (h + 1) * head_size, cols], queries.at[b % 2])
        for g in range(groups):
            values[b, g, :LANES, :] = value[g * LANES : (g + 1) * LANES, b * far : (b + 1) * far]
        weigh(key_rows[b * far : (b + 1) * far, :], queries.at[b % 2], weights.at[b])
    for b in range(BALLS_STEP):
        cols = slice(b * BALL, (b + 1) * BALL)
        for g in range(groups):
            for h, num, den in head_sums(g, head_size, values.at[b], weights.at[b]):
                rows = slice(h * head_size, (h + 1) * head_size)
                num = num + num_ref[rows, cols].astype(F32)
                attended[rows, cols] = (num * (1.0 / (den + den_ref[h : h + 1, cols]))).astype(BF16)
    projected = dot(attended[...].T, wo_ref[...])
    residual = (grouped_ref[...].astype(F32) + projected).astype(BF16)
    rows32 = residual.astype(F32)
    ffn = normed_rows(rows32, gain_ref[...])
    parts = []
    for first_col in range(0, wg_ref.shape[1], 2 * LANES):
        cols = slice(first_col, first_col + 2 * LANES)
        gate = dot(ffn, wg_ref[:, cols])
        up = dot(ffn, wu_ref[:, cols])
        parts.append((0.5 * gate * (1.0 + jnp.tanh(0.5 * gate)) * up).astype(BF16))
    hidden = jnp.concatenate(parts, axis=1)
    return rows32 + dot(hidden, wd_ref[...])


def finish(chosen, places, candidates, query, num, den, grouped, wpk, wpv, wo, gain, wg, wu, wd, head_size):
    rows_dev, width = grouped.shape
    hidden = wg.shape[1]
    groups = width // LANES
    step_rows = BALLS_STEP * BALL
    spread = LANES // head_size * BALL
    far = OWNERS * BALL // POOL
    steps = rows_dev // step_rows
    rows = pl.BlockSpec((step_rows, width), lambda i, *_: (jnp.minimum(i, steps - 1), 0))
    columns = lambda count: pl.BlockSpec((count, step_rows), lambda i, *_: (0, jnp.minimum(i, steps - 1)))
    take_rows = rows_dev // TAKE_STEPS
    fixed = [wpk, wpv, wo, gain, wg, wu, wd]
    return pl.pallas_call(
        functools.partial(finish_kernel, head_size),
        grid_spec=pltpu.PrefetchScalarGridSpec(
            num_scalar_prefetch=2,
            grid=(steps + TAKE_STEPS,),
            in_specs=[
                whole(candidates.shape),
                columns(width),
                columns(width),
                columns(width // head_size),
                rows,
            ]
            + [whole(a.shape) for a in fixed],
            out_specs=pl.BlockSpec((take_rows, width), lambda i, *_: (jnp.maximum(i - steps, 0), 0)),
            scratch_shapes=[
                pltpu.VMEM((2 * LANES, 2 * LANES), BF16),
                pltpu.VMEM((2, groups, LANES, spread), BF16),
                pltpu.VMEM((BALLS_STEP, groups, LANES + 16, far), BF16),
                pltpu.VMEM((BALLS_STEP, groups, far, spread), BF16),
                pltpu.VMEM((width, step_rows), BF16),
                pltpu.VMEM((rows_dev * (width // LANES), LANES), F32),
                pltpu.VMEM((take_rows * (width // LANES), LANES), F32),
            ],
        ),
        out_shape=jax.ShapeDtypeStruct((rows_dev, width), BF16),
        compiler_params=params(),
        cost_estimate=pl.CostEstimate(
            flops=2 * rows_dev * width * (3 * hidden + 6 * width),
            bytes_accessed=12 * rows_dev * width,
            transcendentals=0,
        ),
        name="finish_balls",
    )(chosen, places, candidates, query, num, den, grouped, *fixed)


def take_kernel(places_ref, source_ref, out_ref, rows, taken):
    count, width = source_ref.shape
    chunks = width // LANES

    @pl.when(pl.program_id(0) == 0)
    def _():
        for first in range(0, count, DEPTH):
            for c in range(chunks):
                part = source_ref[first : first + DEPTH, c * LANES : (c + 1) * LANES]
                chunk_rows(rows, first, DEPTH, c, chunks)[...] = part.astype(F32)

    take_block(places_ref, pl.program_id(0), rows, taken, out_ref)


def take_rows(places, source):
    rows_dev, width = source.shape
    chunks = width // LANES
    return pl.pallas_call(
        take_kernel,
        grid_spec=pltpu.PrefetchScalarGridSpec(
            num_scalar_prefetch=1,
            grid=(rows_dev // TILE,),
            in_specs=[whole(source.shape)],
            out_specs=row_blocks(TILE, width),
            scratch_shapes=[
                pltpu.VMEM((rows_dev * chunks, LANES), F32),
                pltpu.VMEM((TILE * chunks, LANES), F32),
            ],
        ),
        out_shape=jax.ShapeDtypeStruct((rows_dev, width), BF16),
        compiler_params=params(),
        cost_estimate=pl.CostEstimate(
            flops=2 * rows_dev * rows_dev * width, bytes_accessed=4 * rows_dev * width, transcendentals=0
        ),
        name="take_rows",
    )(places, source)


def route(block, target):
    devices = range(lax.axis_size("pts"))
    return lax.ppermute(block, "pts", [(i, target(i) % len(devices)) for i in devices])


def to_mate(block, mate):
    return route(block, lambda i: i ^ mate)


SLOT_INSIDE = (0, 5, 1, 6)
SLOT_OUTSIDE = (2, 7, 4, 8)


def block_slots(owner, me, peers):
    mate = (owner % GROUP) ^ (me % GROUP)
    ahead = jnp.mod(owner // GROUP - me // GROUP, peers // GROUP)
    pick = lambda table: sum(jnp.where(mate == m, table[m], 0) for m in range(GROUP))
    second = (mate == 0) & ((ahead == 1) != (me % GROUP < 2))
    return jnp.where(ahead == 0, pick(SLOT_INSIDE), pick(SLOT_OUTSIDE) + jnp.where(second, 1, 0))


def on_device(
    points,
    point_row_index,
    neighbour_ball_list,
    attention_norm_gain,
    query_weight,
    key_weight,
    value_weight,
    pooled_key_weight,
    pooled_value_weight,
    head_score_scale,
    output_weight,
    feedforward_norm_gain,
    gate_weight,
    up_weight,
    down_weight,
):
    rows_dev, width = points.shape
    head_size = width // head_score_scale.shape[0]
    peers = lax.axis_size("pts")
    me = lax.axis_index("pts")
    send_each = rows_dev // peers
    blocks_dev = rows_dev // BALL
    comp = BALL // POOL

    def swap(array):
        return lax.all_to_all(array, "pts", split_axis=0, concat_axis=0, tiled=True)

    outgoing, slot = send_order(points, point_row_index.reshape(rows_dev // LANES, LANES), me, peers)
    rows, places, pooled = pool(swap(outgoing), attention_norm_gain[None], rows_dev)
    up = lambda i: i % GROUP >= 2
    first = route(pooled, lambda i: i + GROUP if up(i) else i - GROUP)
    other = route(pooled, lambda i: i - GROUP if up(i) else i + GROUP)
    beside = to_mate(pooled, 2)
    grouped, normed = group(places, rows, attention_norm_gain[None])
    scale = head_score_scale * (LOG2E / head_size)
    attend = functools.partial(
        local_attention,
        normed=normed,
        wq=query_weight.T,
        wk=key_weight,
        wv=value_weight.T,
        scale=scale,
        head_size=head_size,
    )
    soon, early = blocks_dev // 4, blocks_dev * 3 // 4
    part = attend(0, soon)
    first, part = lax.optimization_barrier((first, part))
    handed = to_mate(first, 2)
    part = attend(soon, early, earlier=part)
    first, other, beside, handed, part = lax.optimization_barrier((first, other, beside, handed, part))
    place = me % GROUP
    held = jnp.stack([pooled, beside, jnp.where(place // 2 == place % 2, first, other), handed])
    near = to_mate(held, 1)
    query, num, den = attend(early, blocks_dev, earlier=part)
    candidates = jnp.concatenate([jnp.stack([pooled, beside, first, other, handed]), near])
    candidates = candidates.reshape(candidates.shape[0] * blocks_dev, comp, width)
    slots = block_slots(neighbour_ball_list // blocks_dev, me, peers)
    chosen = (slots * blocks_dev + neighbour_ball_list % blocks_dev).reshape(-1)
    returning = finish(
        chosen,
        places,
        candidates,
        query,
        num,
        den,
        grouped,
        pooled_key_weight,
        pooled_value_weight.T,
        output_weight,
        feedforward_norm_gain[None],
        gate_weight,
        up_weight,
        down_weight,
        head_size,
    )
    came_back = swap(returning.reshape(peers, send_each, width)).reshape(rows_dev, width)
    return take_rows(slot, came_back)


def solution(mesh):
    rows = P(("rep", "pts"), None)
    return jax.shard_map(
        on_device,
        mesh=mesh,
        in_specs=(rows, P(("rep", "pts")), rows) + (P(),) * 12,
        out_specs=rows,
        check_vma=False,
    )
```
